32 devices in a mesh: dp: 2 (over core), fsdp: 16 (over z, y, x).
Axes of the slice: x: 2, y: 2, z: 4, core: 2. Of those that a mesh axis runs over, the one named last changes fastest.
Arguments:
- tokens: float32 [32768, 768], P(('dp', 'fsdp')), may hold values from -6 to 6
- lengths: int32 [32, 3], P(('dp', 'fsdp')), may hold values from 1 to 640, 1024 in all within a row
- w_input: bfloat16 [768, 768], P(('dp', 'fsdp')), may hold values from -0.21875 to 0.21875
- w_forget: bfloat16 [768, 384], P(('dp', 'fsdp')), may hold values from -0.21875 to 0.21875
- w_gate: bfloat16 [768, 768], P(('dp', 'fsdp')), may hold values from -0.21875 to 0.21875
- w_output: bfloat16 [768, 768], P(('dp', 'fsdp')), may hold values from -0.4375 to 0.4375
- w_up_gate: bfloat16 [768, 1536], P(('dp', 'fsdp')), may hold values from -0.21875 to 0.21875
- w_up: bfloat16 [768, 1536], P(('dp', 'fsdp')), may hold values from -0.21875 to 0.21875
- w_down: bfloat16 [1536, 768], P(('dp', 'fsdp')), may hold values from -0.15625 to 0.15625
- norm_gain: bfloat16 [768], P(('dp', 'fsdp')), may hold values from 0.5 to 1.5
- group_gain: bfloat16 [768], P(('dp', 'fsdp')), may hold values from 0.5 to 1.5
- ffn_gain: bfloat16 [768], P(('dp', 'fsdp')), may hold values from 0.5 to 1.5
- lower_bound: float32 [384], replicated, may hold values from 0 to 0.9
- phase: float32 [384], replicated, may hold values from -1 to 1
- cotangent: float32 [32768, 768], P(('dp', 'fsdp')), may hold values from -6 to 6
Outputs:
- activations: float32 [32768, 768], P(('dp', 'fsdp'))
- input_grad: float32 [32768, 768], P(('dp', 'fsdp'))
- grad_input: float32 [768, 768], P(('dp', 'fsdp'))
- grad_forget: float32 [768, 384], P(('dp', 'fsdp'))
- grad_gate: float32 [768, 768], P(('dp', 'fsdp'))
- grad_output: float32 [768, 768], P(('dp', 'fsdp'))
- grad_up_gate: float32 [768, 1536], P(('dp', 'fsdp'))
- grad_up: float32 [768, 1536], P(('dp', 'fsdp'))
- grad_down: float32 [1536, 768], P(('dp', 'fsdp'))
- grad_norm_gain: float32 [768], P(('dp', 'fsdp'))
- grad_group_gain: float32 [768], P(('dp', 'fsdp'))
- grad_ffn_gain: float32 [768], P(('dp', 'fsdp'))
- grad_lower: float32 [384], replicated
- grad_phase: float32 [384], replicated
The draws below stay inside these ranges and needn't reach their ends.
Inputs may be any that keep to these rules, and one draw needn't show every extreme that they name: Each row of lengths sums to 1024; in every row some entry is exactly 640.
All inputs are finite; a program needn't handle non-finite values.
Results may differ from the reference program's by a relative error of at most 0.0078.
Values may be sent and summed in bfloat16 or wider, within the bound.
No kernel may reach another device: no remote copies, remote signals or barrier semaphores. Data moves between devices by JAX's collectives and lax.ppermute only.
A program may use at most 256 MiB of HBM per device.

```python
import math
import jax
import jax.numpy as jnp
import numpy as np
from jax import lax

D = 768
C = 384
FF = 1536
GROUPS = 4
TOK_DEV = 1024
LEN_MOST = 640
TOKENS = 32768
DEVICES = 32


def with_spikes(entries, own_key, source, target, shards_of, factor):
    def block_of(axis_at):
        return (jnp.arange(entries.shape[axis_at]) // (entries.shape[axis_at] // shards_of)).reshape((-1,) + (1,) * (entries.ndim - 1 - axis_at))

    one_side = jax.random.permutation(own_key, shards_of)[block_of(target)]
    other_side = (block_of(target) + shards_of // 2) % shards_of
    return jnp.where((block_of(source) == one_side) | (block_of(source) == other_side), factor * entries, entries)


def block_levels(rng, extent, pieces, smallest, top_value):
    factor_of = 1.0
    for dim, shards_of in pieces:
        heights = jax.random.uniform(jax.random.fold_in(jax.random.fold_in(rng, 6), dim), (shards_of,), jnp.float32, smallest / len(pieces), top_value / len(pieces))
        factor_of = factor_of * jnp.repeat(jnp.exp(heights), extent[dim] // shards_of).reshape((-1,) + (1,) * (len(extent) - 1 - dim))
    return factor_of


def profile(count, total, most, slope):
    weights = [(1 << 20) // math.isqrt(rank ** slope) + 1 for rank in range(2, count + 1)]
    spare, holding = total - most - (count - 1), [1] * (count - 1)
    while spare > 0:
        candidates = [i for i in range(count - 1) if holding[i] < most]
        mass, budget = sum([weights[i] for i in candidates]), spare
        for i in candidates:
            more = min(most - holding[i], max(1, budget * weights[i] // mass), spare)
            holding[i] = holding[i] + more
            spare = spare - more
    return np.array([most] + holding)


def uneven(key, count, total, limit, slope):
    if count == 2:
        one = jax.random.randint(key, (), max(1, total - limit), min(limit, total - 1) + 1)
        return jnp.stack([one, total - one])
    tallies = jnp.asarray(profile(count, total, limit, slope), jnp.int32)
    pairs = (count - 1) // 2
    giver, sink = tallies[1:1 + 2 * pairs:2], tallies[2:2 + 2 * pairs:2]
    slack = jnp.minimum(giver - 1, limit - sink)
    shifted = jax.random.randint(jax.random.fold_in(key, 1), (pairs,), 0, 1 << 20) % (slack + 1)
    tallies = tallies.at[1:1 + 2 * pairs:2].set(giver - shifted).at[2:2 + 2 * pairs:2].set(sink + shifted)
    return tallies[jax.random.permutation(jax.random.fold_in(key, 2), count)]


def normal_values(rng, extent, deviation, most, shards=(), held_as=jnp.bfloat16):
    values = deviation * jax.random.normal(rng, extent, jnp.float32)
    if shards:
        values = values * block_levels(rng, extent, shards, -0.22, 0.18)
    return jnp.clip(values, -most, most).astype(held_as)


def heavy_noise(key, dims, spread, bound, cuts, heavy, kind=jnp.bfloat16):
    drawn = spread * jax.random.normal(key, dims, jnp.float32)
    if cuts:
        drawn = drawn * block_levels(key, dims, cuts, -0.22, 0.18)
    return jnp.clip(with_spikes(drawn, jax.random.fold_in(key, 3), *heavy), -bound, bound).astype(kind)


def setup_inputs(seed: int = 0) -> dict:
    streams_of = jax.random.split(jax.random.key(seed), 16)
    tokens = heavy_noise(streams_of[0], (TOKENS, D), 1.0, 6.0, ((0, 32),), (0, 1, 32, 2.75), jnp.float32)
    lengths = jax.vmap(lambda own: uneven(own, 3, TOK_DEV, LEN_MOST, 2))(jax.random.split(streams_of[1], DEVICES)).reshape((DEVICES, 3)).astype(jnp.int32)
    w_input = normal_values(streams_of[2], (D, D), D ** -0.5, 0.21875, ((0, 32),))
    w_forget = normal_values(streams_of[3], (D, C), D ** -0.5, 0.21875, ((0, 32),))
    w_gate = normal_values(streams_of[4], (D, D), D ** -0.5, 0.21875, ((0, 32),))
    w_output = normal_values(streams_of[5], (D, D), (D // 4) ** -0.5, 0.4375, ((0, 32),))
    w_up_gate = normal_values(streams_of[6], (D, FF), D ** -0.5, 0.21875, ((0, 32),))
    w_up = normal_values(streams_of[7], (D, FF), D ** -0.5, 0.21875, ((0, 32),))
    w_down = normal_values(streams_of[8], (FF, D), FF ** -0.5, 0.15625, ((0, 32),))
    norm_gain = jnp.clip(1.0 + 0.1 * jax.random.normal(streams_of[9], (D,), jnp.float32), 0.5, 1.5).astype(jnp.bfloat16)
    group_gain = jnp.clip(1.0 + 0.1 * jax.random.normal(streams_of[10], (D,), jnp.float32), 0.5, 1.5).astype(jnp.bfloat16)
    ffn_gain = jnp.clip(1.0 + 0.1 * jax.random.normal(streams_of[11], (D,), jnp.float32), 0.5, 1.5).astype(jnp.bfloat16)
    lower_bound = jnp.clip(jax.random.uniform(streams_of[12], (C,), jnp.float32, 0.0, 0.9), 0.0, 0.9)
    phase = jnp.clip(jax.random.uniform(streams_of[13], (C,), jnp.float32, -1.0, 1.0), -1.0, 1.0)
    cotangent = normal_values(streams_of[14], (TOKENS, D), 1.0, 6.0, ((0, 32),), jnp.float32)
    return {"tokens": tokens, "lengths": lengths, "w_input": w_input, "w_forget": w_forget, "w_gate": w_gate, "w_output": w_output, "w_up_gate": w_up_gate, "w_up": w_up, "w_down": w_down, "norm_gain": norm_gain, "group_gain": group_gain, "ffn_gain": ffn_gain, "lower_bound": lower_bound, "phase": phase, "cotangent": cotangent}


@jax.custom_vjp
def low(v):
    return lax.optimization_barrier(v.astype(jnp.bfloat16)).astype(jnp.float32)

@jax.custom_vjp
def low_back(v):
    return v

def low_keep(v):
    return (low(v), None)

def low_pass(kept, grad):
    return (grad,)

def back_keep(v):
    return (v, None)

def back_low(kept, grad):
    return (low(grad),)
low.defvjp(low_keep, low_pass)
low_back.defvjp(back_keep, back_low)

def product(left, right):
    return jnp.dot(left, right, precision=lax.Precision.HIGHEST, preferred_element_type=jnp.float32)

def rms_norm(values, gain):
    return values * lax.rsqrt(lax.optimization_barrier(jnp.mean(values * values, axis=-1, keepdims=True)) + 1e-06) * gain

def combine(first, second):
    ar1, ai1, br1, bi1 = first
    ar2, ai2, br2, bi2 = second
    return (ar2 * ar1 - ai2 * ai1, ar2 * ai1 + ai2 * ar1, ar2 * br1 - ai2 * bi1 + br2, ar2 * bi1 + ai2 * br1 + bi2)

def layer(tokens, length_row, params, lower_bound, phase):
    w_input, w_forget, w_gate, w_output, w_up_gate, w_up, w_down, norm_gain, group_gain, ffn_gain = params
    rows, width = tokens.shape
    half = width // 2
    position = jnp.arange(rows, dtype=jnp.int32)
    first = length_row[0]
    second = first + length_row[1]
    start = (position == 0) | (position == first) | (position == second)
    valid = (position < second).astype(jnp.float32)[:, None]
    normed = low(rms_norm(tokens, norm_gain))
    inner = low_back(product(normed, w_input))
    forget = low_back(product(normed, w_forget))
    gate = low_back(product(normed, w_gate))
    lam = lower_bound + (1.0 - lower_bound) * jax.nn.sigmoid(forget)
    keep = jnp.where(start[:, None], 0.0, lam)
    source = jax.nn.silu(inner)
    state = lax.associative_scan(combine, (keep * jnp.cos(phase), keep * jnp.sin(phase), (1.0 - lam) * source[:, :half], (1.0 - lam) * source[:, half:]))
    mixed = jnp.concatenate([state[2], state[3]], axis=1)
    grouped = mixed.reshape(rows, GROUPS, width // GROUPS)
    centred = grouped - lax.optimization_barrier(jnp.mean(grouped, axis=-1, keepdims=True))
    grouped = centred * lax.rsqrt(lax.optimization_barrier(jnp.mean(centred * centred, axis=-1, keepdims=True)) + 1e-05)
    gated = low(grouped.reshape(rows, width) * group_gain * jax.nn.sigmoid(gate))
    middle = tokens + low_back(product(gated, w_output))
    ffn_in = low(rms_norm(middle, ffn_gain))
    left = low_back(product(ffn_in, w_up_gate))
    right = low_back(product(ffn_in, w_up))
    hidden = low(jax.nn.silu(left) * right)
    return valid * (middle + low_back(product(hidden, w_down)))

def reference(tokens, lengths, w_input, w_forget, w_gate, w_output, w_up_gate, w_up, w_down, norm_gain, group_gain, ffn_gain, lower_bound, phase, cotangent):
    params = tuple((item.astype(jnp.float32) for item in (w_input, w_forget, w_gate, w_output, w_up_gate, w_up, w_down, norm_gain, group_gain, ffn_gain)))
    blocks = tokens.reshape(DEVICES, TOK_DEV, D)

    def forward(blocks, params, lower_bound, phase):

        def one_row(item):
            return jax.checkpoint(lambda rows, lens: layer(rows, lens, params, lower_bound, phase))(item[0], item[1])
        return lax.map(one_row, (blocks, lengths))
    result, pullback = jax.vjp(forward, blocks, params, lower_bound, phase)
    d_blocks, d_params, d_lower, d_phase = pullback(cotangent.reshape(DEVICES, TOK_DEV, D))
    return (result.reshape(TOKENS, D), d_blocks.reshape(TOKENS, D), d_params[0], d_params[1], d_params[2], d_params[3], d_params[4], d_params[5], d_params[6], d_params[7], d_params[8], d_params[9], d_lower, d_phase)
```

```python
import jax
import jax.numpy as jnp
from jax import lax
from jax.experimental import pallas as pl
from jax.experimental.pallas import tpu as pltpu
from jax.sharding import PartitionSpec as P

GROUPS = 4
LANES = 128
CHAINS = 8
TILE = 256
CHUNK = 16
VMEM_BYTES = 60 * 2**20
BF = jnp.bfloat16
F32 = jnp.float32
TN = (((0,), (0,)), ((), ()))
NT = (((1,), (1,)), ((), ()))


def mm(left, right):
    return jnp.dot(left, right, preferred_element_type=F32)


def mm_nt(left, right):
    return lax.dot_general(left, right, NT, preferred_element_type=F32)


def mm_tn(left, right):
    return lax.dot_general(left, right, TN, preferred_element_type=F32)


def sigmoid(v):
    return 0.5 * jnp.tanh(0.5 * v) + 0.5


def chunks(rows, body, size=CHUNK, unroll=2):
    def step(i, carry):
        body(pl.multiple_of(i * size, size))
        return carry

    lax.fori_loop(0, rows // size, step, 0, unroll=unroll)


def slot_times(base, rows, total):
    row = base + lax.broadcasted_iota(jnp.int32, (rows, 1), 0)
    return (row % CHAINS) * (total // CHAINS) + row // CHAINS


def strips(value):
    return [value[:, i * LANES : (i + 1) * LANES] for i in range(value.shape[1] // LANES)]


def group_means(parts, low, size):
    zero = jnp.zeros_like(parts[0])
    sums = []
    for h in (0, 3):
        sums.append(parts[h] + jnp.where(low, parts[h + 1], zero))
        sums.append(jnp.where(low, zero, parts[h + 1]) + parts[h + 2])
    return [jnp.sum(s, axis=-1, keepdims=True) * (1.0 / size) for s in sums]


def group_spread(values, low):
    out = []
    for h in (0, 2):
        out += [values[h], jnp.where(low, values[h], values[h + 1]), values[h + 1]]
    return out


def centre_and_scale(parts, low, size):
    means = group_spread(group_means(parts, low, size), low)
    parts = [p - m for p, m in zip(parts, means)]
    variances = group_means([p * p for p in parts], low, size)
    scales = group_spread([lax.rsqrt(v + 1e-05) for v in variances], low)
    return [p * s for p, s in zip(parts, scales)], scales


def piece_copies(me, pieces, target, columns, sems, first):
    rows = pieces[0].shape[0]
    out = []
    for k, piece in enumerate(pieces):
        at = pl.multiple_of((me ^ k) * rows, 16)
        out.append(pltpu.make_async_copy(piece, target.at[pl.ds(at, rows), columns], sems.at[first + k]))
    return out


def slot_copies(me, source, columns, slots, sems, first):
    rows = slots[0].shape[0]
    out = []
    for k, slot in enumerate(slots):
        at = pl.multiple_of((me ^ k) * rows, 16)
        out.append(pltpu.make_async_copy(source.at[pl.ds(at, rows), columns], slot, sems.at[first + k]))
    return out


def tile_spec(width, index):
    return pl.BlockSpec((TILE, width), lambda i: (index(i), 0))


def whole(shape):
    return pl.BlockSpec(shape, lambda i: (0,) * len(shape))


ANY = pl.BlockSpec(memory_space=pl.ANY)
SMEM = pl.BlockSpec(memory_space=pltpu.SMEM)


def struct(shape, dtype):
    return jax.ShapeDtypeStruct(shape, dtype)


def params():
    return pltpu.CompilerParams(vmem_limit_bytes=VMEM_BYTES, dimension_semantics=("arbitrary",))


def recurrent_forward(parts, cut, dims):
    total, width, half, size = dims
    tiles = total // TILE
    wide = 2 * width + half

    def kernel(len_ref, me_ref, tok, cos, sin, low_ref, *refs):
        left_pieces, right_pieces = refs[:parts], refs[parts : 2 * parts]
        normed, inner, gate, forget, state, gated, gains = refs[2 * parts : 2 * parts + 7]
        w, keep, zr, zi, prod, gate_all, carry, ends, sems = refs[2 * parts + 7 :]
        step = pl.program_id(0)
        first = len_ref[0, 0]
        second = first + len_ref[0, 1]
        me = me_ref[0]

        @pl.when(step == 0)
        def _():
            copies = piece_copies(me, left_pieces, w, pl.ds(0, cut), sems, 0)
            copies += piece_copies(me, right_pieces, w, pl.ds(cut, w.shape[1] - cut), sems, parts)
            for c in copies:
                c.start()
            for c in copies:
                c.wait()
            gains[...] = jnp.transpose(w[:, wide : wide + LANES].astype(F32))[0:8, :]
            carry[...] = jnp.concatenate([jnp.zeros((16, half), F32), jnp.ones((8, half), F32)], axis=0)

        @pl.when(step < tiles)
        def _():
            base = step * TILE
            gain = gains[0:1, :]

            def norm(at):
                x = tok[pl.ds(at, CHUNK), :]
                scale = lax.rsqrt(jnp.mean(x * x, axis=-1, keepdims=True) + 1e-06)
                normed[pl.ds(at, CHUNK), :] = (x * scale * gain).astype(BF)

            chunks(TILE, norm)
            value = normed[...]
            inner[...] = mm(value, w[:, 0:width])
            gate_tile = mm(value, w[:, width : 2 * width])
            gate[...] = gate_tile
            gate_all[pl.ds(pl.multiple_of(base, TILE), TILE), :] = gate_tile
            forget[...] = mm(value, w[:, 2 * width : wide])
            bound = low_ref[0:1, :]

            def sources(at):
                here = pl.ds(at, CHUNK)
                there = pl.ds(pl.multiple_of(base + at, CHUNK), CHUNK)
                time = slot_times(base + at, CHUNK, total)
                start = (time == 0) | (time == first) | (time == second)
                lam = bound + (1.0 - bound) * sigmoid(forget[here, :])
                keep[here, :] = jnp.where(start, 0.0, lam)
                rest = 1.0 - lam
                re = inner[here, 0:half]
                im = inner[here, half:width]
                re = rest * re * sigmoid(re)
                im = rest * im * sigmoid(im)
                c, s = cos[here, :], sin[here, :]
                zr[there, :] = c * re + s * im
                zi[there, :] = c * im - s * re

            chunks(TILE, sources)

            def scan(j, held):
                re, im, p = held
                k = keep[pl.ds(pl.multiple_of(j * 8, 8), 8), :]
                there = pl.ds(pl.multiple_of(base + j * 8, 8), 8)
                re = k * re + zr[there, :]
                im = k * im + zi[there, :]
                p = k * p
                zr[there, :] = re
                zi[there, :] = im
                prod[there, :] = p
                return re, im, p

            held = (carry[0:8, :], carry[8:16, :], carry[16:24, :])
            held = lax.fori_loop(0, TILE // 8, scan, held, unroll=4)
            carry[0:8, :], carry[8:16, :], carry[16:24, :] = held

        @pl.when(step == tiles)
        def _():
            p = carry[16:24, :]
            for h in (0, 8):
                z = carry[h : h + 8, :]
                rows = [jnp.zeros((1, half), F32)]
                for c in range(1, CHAINS):
                    rows.append(z[c - 1 : c, :] + p[c - 1 : c, :] * rows[-1])
                into = jnp.concatenate(rows, axis=0)
                ends[2 * h : 2 * h + 16, :] = jnp.concatenate([into, into], axis=0)

        @pl.when(step >= tiles)
        def _():
            base = (step - tiles) * TILE
            gain = gains[1:2, :]
            low = lax.broadcasted_iota(jnp.int32, (CHUNK, LANES), 1) < LANES // 2

            def mix(at):
                here = pl.ds(at, CHUNK)
                there = pl.ds(pl.multiple_of(base + at, CHUNK), CHUNK)
                p = prod[there, :]
                re = zr[there, :] + p * ends[0:16, :]
                im = zi[there, :] + p * ends[16:32, :]
                state[here, 0:half] = re
                state[here, half:width] = im
                c, s = cos[here, :], sin[here, :]
                mixed = strips(c * re - s * im) + strips(c * im + s * re)
                grouped, _ = centre_and_scale(mixed, low, width // GROUPS)
                for n in range(len(grouped)):
                    lanes = slice(n * LANES, (n + 1) * LANES)
                    opened = grouped[n] * gain[:, lanes] * sigmoid(gate_all[there, lanes])
                    gated[here, lanes] = opened.astype(BF)

            chunks(TILE, mix)

    early = lambda i: jnp.minimum(i, tiles - 1)
    late = lambda i: jnp.maximum(i - tiles, 0)
    both = lambda i: jnp.where(i < tiles, i, i - tiles)
    packed = wide + LANES
    return pl.pallas_call(
        kernel,
        grid=(2 * tiles,),
        in_specs=[SMEM, SMEM, tile_spec(width, early), tile_spec(half, both), tile_spec(half, both), whole((8, half))]
        + [ANY] * (2 * parts),
        out_specs=[
            tile_spec(width, early),
            tile_spec(width, early),
            tile_spec(width, early),
            tile_spec(half, early),
            tile_spec(width, late),
            tile_spec(width, late),
            whole((8, width)),
        ],
        out_shape=[
            struct((total, width), BF),
            struct((total, width), F32),
            struct((total, width), F32),
            struct((total, half), F32),
            struct((total, width), F32),
            struct((total, width), BF),
            struct((8, width), F32),
        ],
        scratch_shapes=[
            pltpu.VMEM((width, packed), BF),
            pltpu.VMEM((TILE, half), F32),
            pltpu.VMEM((total, half), F32),
            pltpu.VMEM((total, half), F32),
            pltpu.VMEM((total, half), F32),
            pltpu.VMEM((total, width), F32),
            pltpu.VMEM((24, half), F32),
            pltpu.VMEM((32, half), F32),
            pltpu.SemaphoreType.DMA((2 * parts,)),
        ],
        compiler_params=params(),
        cost_estimate=pl.CostEstimate(
            flops=2 * total * width * wide, bytes_accessed=20 * total * width, transcendentals=3 * total * width
        ),
        name="recurrent_forward",
    )


def ffn_up(parts, cut, dims, ff):
    total, width, half, size = dims
    tiles = total // TILE
    packed = width + 2 * ff

    def kernel(me_ref, gated, tok, gains, *refs):
        left_pieces, right_pieces = refs[:parts], refs[parts : 2 * parts]
        middle, ffn_in, left, right, hidden = refs[2 * parts : 2 * parts + 5]
        w, sems = refs[2 * parts + 5 :]
        step = pl.program_id(0)
        me = me_ref[0]

        @pl.when(step == 0)
        def _():
            copies = piece_copies(me, left_pieces, w, pl.ds(0, cut), sems, 0)
            copies += piece_copies(me, right_pieces, w, pl.ds(cut, packed - cut), sems, parts)
            for c in copies:
                c.start()
            for c in copies:
                c.wait()

        middle[...] = tok[...] + mm(gated[...], w[:, 0:width])
        gain = gains[2:3, :]

        def norm(at):
            x = middle[pl.ds(at, CHUNK), :]
            scale = lax.rsqrt(jnp.mean(x * x, axis=-1, keepdims=True) + 1e-06)
            ffn_in[pl.ds(at, CHUNK), :] = (x * scale * gain).astype(BF)

        chunks(TILE, norm)
        value = ffn_in[...]
        left[...] = mm(value, w[:, width : width + ff])
        right[...] = mm(value, w[:, width + ff : packed])

        def units(at):
            here = pl.ds(at, CHUNK)
            l = left[here, :]
            hidden[here, :] = (l * sigmoid(l) * right[here, :]).astype(BF)

        chunks(TILE, units)

    same = lambda i: i
    return pl.pallas_call(
        kernel,
        grid=(tiles,),
        in_specs=[SMEM, tile_spec(width, same), tile_spec(width, same), whole((8, width))] + [ANY] * (2 * parts),
        out_specs=[
            tile_spec(width, same),
            tile_spec(width, same),
            tile_spec(ff, same),
            tile_spec(ff, same),
            tile_spec(ff, same),
        ],
        out_shape=[
            struct((total, width), F32),
            struct((total, width), BF),
            struct((total, ff), F32),
            struct((total, ff), F32),
            struct((total, ff), BF),
        ],
        scratch_shapes=[pltpu.VMEM((width, packed), BF), pltpu.SemaphoreType.DMA((2 * parts,))],
        compiler_params=params(),
        cost_estimate=pl.CostEstimate(
            flops=2 * total * width * packed, bytes_accessed=24 * total * width, transcendentals=total * ff
        ),
        name="ffn_up",
    )


def ffn_down_and_back(parts, cut, dims, ff):
    total, width, half, size = dims
    tiles = total // TILE
    rows = width // parts
    deep = ff // parts

    def kernel(len_ref, me_ref, hidden, middle, cot, left, right, ffn_any, *refs):
        left_pieces, right_pieces = refs[:parts], refs[parts : 2 * parts]
        refs = refs[2 * parts :]
        act, d_left, d_right = refs[:3]
        gate_slots, up_slots = refs[3 : 3 + parts], refs[3 + parts : 3 + 2 * parts]
        down_a, down_b = refs[3 + 2 * parts : 3 + 3 * parts], refs[3 + 3 * parts : 3 + 4 * parts]
        w, ffn_in, grad, dl_all, dr_all, g_down, g_gate, g_up, sems = refs[3 + 4 * parts :]
        step = pl.program_id(0)
        me = me_ref[0]
        second = len_ref[0, 0] + len_ref[0, 1]
        own = pltpu.make_async_copy(ffn_any, ffn_in, sems.at[2 * parts])

        @pl.when(step == 0)
        def _():
            copies = piece_copies(me, left_pieces, w, pl.ds(0, cut), sems, 0)
            copies += piece_copies(me, right_pieces, w, pl.ds(cut, width - cut), sems, parts)
            for c in copies:
                c.start()
            own.start()
            for c in copies:
                c.wait()

        @pl.when(step < tiles)
        def _():
            base = step * TILE
            block = pl.ds(pl.multiple_of(base, TILE), TILE)
            act[...] = middle[...] + mm(hidden[block, :], w[...])

            def finish(at):
                here = pl.ds(at, CHUNK)
                valid = (slot_times(base + at, CHUNK, total) < second).astype(F32)
                act[here, :] = valid * act[here, :]
                grad[pl.ds(pl.multiple_of(base + at, CHUNK), CHUNK), :] = (valid * cot[here, :]).astype(BF)

            chunks(TILE, finish)
            d_hidden = mm_nt(grad[block, :], w[...])
            hold[...] = d_hidden

            def units(at):
                here = pl.ds(at, CHUNK)
                there = pl.ds(pl.multiple_of(base + at, CHUNK), CHUNK)
                for n in range(2):
                    lanes = slice(n * (ff // 2), (n + 1) * (ff // 2))
                    l = left[here, lanes]
                    dh = hold[here, lanes]
                    s = sigmoid(l)
                    dr = (dh * (l * s)).astype(BF)
                    dl = (dh * right[here, lanes] * (s * (1.0 + l * (1.0 - s)))).astype(BF)
                    d_left[here, lanes] = dl
                    dl_all[there, lanes] = dl
                    d_right[here, lanes] = dr
                    dr_all[there, lanes] = dr

            chunks(TILE, units)

        @pl.when(step == tiles)
        def _():
            own.wait()
            for m in range(0, ff, TILE):
                g_down[m : m + TILE, :] = mm_tn(hidden[:, m : m + TILE], grad[...]).astype(BF)
            copies = slot_copies(me, g_down, pl.ds(0, cut), down_a, sems, 0)
            copies += slot_copies(me, g_down, pl.ds(cut, width - cut), down_b, sems, parts)
            for c in copies:
                c.start()
            for m in range(0, width, TILE):
                g_gate[m : m + TILE, :] = mm_tn(ffn_in[:, m : m + TILE], dl_all[...]).astype(BF)
            more = slot_copies(me, g_gate, pl.ds(0, ff), gate_slots, sems, 2 * parts)
            for c in more:
                c.start()
            for m in range(0, width, TILE):
                g_up[m : m + TILE, :] = mm_tn(ffn_in[:, m : m + TILE], dr_all[...]).astype(BF)
            last = slot_copies(me, g_up, pl.ds(0, ff), up_slots, sems, 3 * parts)
            for c in last:
                c.start()
            for c in copies + more + last:
                c.wait()

    def with_hold(*refs):
        nonlocal hold
        hold = refs[-1]
        kernel(*refs[:-1])

    hold = None
    early = lambda i: jnp.minimum(i, tiles - 1)
    return pl.pallas_call(
        with_hold,
        grid=(tiles + 1,),
        in_specs=[
            SMEM,
            SMEM,
            whole((total, ff)),
            tile_spec(width, early),
            tile_spec(width, early),
            tile_spec(ff, early),
            tile_spec(ff, early),
            ANY,
        ]
        + [ANY] * (2 * parts),
        out_specs=[tile_spec(width, early), tile_spec(ff, early), tile_spec(ff, early)] + [ANY] * (4 * parts),
        out_shape=[struct((total, width), F32), struct((total, ff), BF), struct((total, ff), BF)]
        + [struct((rows, ff), BF)] * (2 * parts)
        + [struct((deep, cut), BF)] * parts
        + [struct((deep, width - cut), BF)] * parts,
        scratch_shapes=[
            pltpu.VMEM((ff, width), BF),
            pltpu.VMEM((total, width), BF),
            pltpu.VMEM((total, width), BF),
            pltpu.VMEM((total, ff), BF),
            pltpu.VMEM((total, ff), BF),
            pltpu.VMEM((ff, width), BF),
            pltpu.VMEM((width, ff), BF),
            pltpu.VMEM((width, ff), BF),
            pltpu.SemaphoreType.DMA((4 * parts + 1,)),
            pltpu.VMEM((TILE, ff), F32),
        ],
        compiler_params=params(),
        cost_estimate=pl.CostEstimate(
            flops=10 * total * width * ff, bytes_accessed=50 * total * width, transcendentals=total * ff
        ),
        name="ffn_down_and_back",
    )


def recurrent_back(parts, cut, dims, ff, share):
    total, width, half, size = dims
    tiles = total // TILE
    packed = width + 2 * ff
    wide = 2 * width + half
    rows = width // parts

    def kernel(
        len_ref, me_ref, d_left, d_right, middle, cot, cos, sin, state, gate, forget, forget0, inner, gains, low_ref,
        gated_any, normed_any, *refs
    ):
        left_pieces, right_pieces = refs[:parts], refs[parts : 2 * parts]
        refs = refs[2 * parts :]
        d_proj, d_middle, sums = refs[:3]
        slots_a, slots_b = refs[3 : 3 + parts], refs[3 + parts : 3 + 2 * parts]
        (w, gated, normed, hold, d_mid, keep, wr, wi, prod, carry, ends, acc, g_all, sems) = refs[3 + 2 * parts :]
        step = pl.program_id(0)
        me = me_ref[0]
        first = len_ref[0, 0]
        second = first + len_ref[0, 1]
        bound = low_ref[0:1, :]
        fetch = [
            pltpu.make_async_copy(gated_any, gated, sems.at[2 * parts]),
            pltpu.make_async_copy(normed_any, normed, sems.at[2 * parts + 1]),
        ]

        def starts(base, count):
            time = slot_times(base, count, total)
            return (time == 0) | (time == first) | (time == second)

        @pl.when(step == 0)
        def _():
            copies = piece_copies(me, left_pieces, w, pl.ds(0, cut), sems, 0)
            copies += piece_copies(me, right_pieces, w, pl.ds(cut, packed - cut), sems, parts)
            for c in copies + fetch:
                c.start()
            acc[...] = jnp.zeros_like(acc)
            lam = bound + (1.0 - bound) * sigmoid(forget0[...])
            k = jnp.where(starts(0, 8), 0.0, lam)
            nothing = jnp.zeros((1, half), F32)
            carry[0:16, :] = jnp.zeros((16, half), F32)
            carry[16:24, :] = jnp.ones((8, half), F32)
            carry[24:32, :] = jnp.concatenate([k[1:8, :], nothing], axis=0)
            for c in copies:
                c.wait()

        @pl.when(step < tiles)
        def _():
            base = (tiles - 1 - step) * TILE
            block = pl.ds(pl.multiple_of(base, TILE), TILE)
            hold[...] = mm_nt(d_left[...], w[:, width : width + ff]) + mm_nt(d_right[...], w[:, width + ff : packed])
            ffn_gain = gains[2:3, :]

            def norm_back(at):
                here = pl.ds(at, CHUNK)
                valid = (slot_times(base + at, CHUNK, total) < second).astype(F32)
                x = middle[here, :]
                scale = lax.rsqrt(jnp.mean(x * x, axis=-1, keepdims=True) + 1e-06)
                d = hold[here, :]
                unit = x * scale
                part = d * unit
                acc[0:8, :] += part[0:8, :] + part[8:16, :]
                d = d * ffn_gain
                back = scale * (d - unit * jnp.mean(d * unit, axis=-1, keepdims=True))
                back = back + valid * cot[here, :]
                d_middle[here, :] = back
                d_mid[pl.ds(pl.multiple_of(base + at, CHUNK), CHUNK), :] = back.astype(BF)

            chunks(TILE, norm_back)
            hold[...] = mm_nt(d_mid[block, :], w[:, 0:width])
            gain = gains[1:2, :]
            low = lax.broadcasted_iota(jnp.int32, (CHUNK, LANES), 1) < LANES // 2

            def group_back(at):
                here = pl.ds(at, CHUNK)
                there = pl.ds(pl.multiple_of(base + at, CHUNK), CHUNK)
                re, im = state[there, 0:half], state[there, half:width]
                c, s = cos[here, :], sin[here, :]
                mixed = strips(c * re - s * im) + strips(c * im + s * re)
                grouped, scales = centre_and_scale(mixed, low, width // GROUPS)
                back = []
                for n in range(len(grouped)):
                    lanes = slice(n * LANES, (n + 1) * LANES)
                    open_ = sigmoid(gate[here, lanes])
                    d = hold[here, lanes]
                    part = d * grouped[n] * open_
                    acc[8:16, lanes] += part[0:8, :] + part[8:16, :]
                    d_proj[there, width + n * LANES : width + (n + 1) * LANES] = (
                        part * gain[:, lanes] * (1.0 - open_)
                    ).astype(BF)
                    back.append(d * open_ * gain[:, lanes])
                mean = group_spread(group_means(back, low, width // GROUPS), low)
                along = group_spread(
                    group_means([b * g for b, g in zip(back, grouped)], low, width // GROUPS), low
                )
                back = [t * (b - m - g * a) for t, b, m, g, a in zip(scales, back, mean, grouped, along)]
                for n in range(3):
                    lanes = slice(n * LANES, (n + 1) * LANES)
                    cn, sn = c[:, lanes], s[:, lanes]
                    wr[there, lanes] = cn * back[n] + sn * back[n + 3]
                    wi[there, lanes] = cn * back[n + 3] - sn * back[n]
                lam = bound + (1.0 - bound) * sigmoid(forget[here, :])
                keep[here, :] = jnp.where(starts(base + at, CHUNK), 0.0, lam)

            chunks(TILE, group_back, unroll=1)

            def scan(i, held):
                re, im, p, k = held
                j = TILE // 8 - 1 - i
                there = pl.ds(pl.multiple_of(base + j * 8, 8), 8)
                re = k * re + wr[there, :]
                im = k * im + wi[there, :]
                p = k * p
                wr[there, :] = re
                wi[there, :] = im
                prod[there, :] = p
                return re, im, p, keep[pl.ds(pl.multiple_of(j * 8, 8), 8), :]

            held = (carry[0:8, :], carry[8:16, :], carry[16:24, :], carry[24:32, :])
            held = lax.fori_loop(0, TILE // 8, scan, held, unroll=4)
            carry[0:8, :], carry[8:16, :], carry[16:24, :], carry[24:32, :] = held

        @pl.when(step == tiles)
        def _():
            p = carry[16:24, :]
            for h in (0, 8):
                z = carry[h : h + 8, :]
                made = [jnp.zeros((1, half), F32)]
                for c in range(CHAINS - 2, -1, -1):
                    made.append(z[c + 1 : c + 2, :] + p[c + 1 : c + 2, :] * made[-1])
                into = jnp.concatenate(made[::-1], axis=0)
                ends[2 * h : 2 * h + 16, :] = jnp.concatenate([into, into], axis=0)
            last = state[total - 8 : total, :]
            ends[32:40, :] = jnp.concatenate([last[7:8, 0:half], last[0:7, 0:half]], axis=0)
            ends[40:48, :] = jnp.concatenate([last[7:8, half:width], last[0:7, half:width]], axis=0)

        @pl.when((step >= tiles) & (step < 2 * tiles))
        def _():
            base = (step - tiles) * TILE

            def source_back(at):
                here = pl.ds(at, CHUNK)
                there = pl.ds(pl.multiple_of(base + at, CHUNK), CHUNK)
                row = base + at
                p = prod[there, :]
                re = wr[there, :] + p * ends[0:16, :]
                im = wi[there, :] + p * ends[16:32, :]
                before = pl.ds(pl.multiple_of(jnp.maximum(row - 8, 0), 8), 8)
                now = pl.ds(pl.multiple_of(row, 8), 8)
                opening = row == 0
                old_re = jnp.concatenate(
                    [jnp.where(opening, ends[32:40, :], state[before, 0:half]), state[now, 0:half]], axis=0
                )
                old_im = jnp.concatenate(
                    [jnp.where(opening, ends[40:48, :], state[before, half:width]), state[now, half:width]], axis=0
                )
                start = starts(row, CHUNK)
                sf = sigmoid(forget[here, :])
                lam = bound + (1.0 - bound) * sf
                turn = jnp.where(start, 0.0, lam) * (im * old_re - re * old_im)
                acc[24:32, 0:half] += turn[0:8, :] + turn[8:16, :]
                d_lam = jnp.where(start, 0.0, re * old_re + im * old_im)
                c, s = cos[here, :], sin[here, :]
                d_re = c * re - s * im
                d_im = c * im + s * re
                rest = 1.0 - lam
                for at_lane, d in ((0, d_re), (half, d_im)):
                    v = inner[here, at_lane : at_lane + half]
                    sv = sigmoid(v)
                    d_lam = d_lam - d * (v * sv)
                    d_proj[there, at_lane : at_lane + half] = (
                        rest * d * (sv * (1.0 + v * (1.0 - sv)))
                    ).astype(BF)
                part = d_lam * (1.0 - sf)
                acc[16:24, 0:half] += part[0:8, :] + part[8:16, :]
                d_proj[there, 2 * width : wide] = (part * (1.0 - bound) * sf).astype(BF)

            chunks(TILE, source_back, unroll=1)

        @pl.when(step == 2 * tiles)
        def _():
            for c in fetch:
                c.wait()
            for m in range(0, width, TILE):
                g_all[m : m + TILE, 0:wide] = mm_tn(normed[:, m : m + TILE], d_proj[...]).astype(BF)
                g_all[m : m + TILE, wide:] = mm_tn(gated[:, m : m + TILE], d_mid[...]).astype(BF)
            copies = slot_copies(me, g_all, pl.ds(0, share), slots_a, sems, 0)
            copies += slot_copies(me, g_all, pl.ds(share, wide + width - share), slots_b, sems, parts)
            for c in copies:
                c.start()
            out = [jnp.sum(acc[8 * n : 8 * n + 8, :], axis=0, keepdims=True) for n in range(4)]
            sums[...] = jnp.concatenate(out + [jnp.zeros((4, width), F32)], axis=0)
            for c in copies:
                c.wait()

    early = lambda i: jnp.maximum(tiles - 1 - i, 0)
    late = lambda i: jnp.clip(i - tiles, 0, tiles - 1)
    both = lambda i: jnp.where(i < tiles, tiles - 1 - i, jnp.minimum(i - tiles, tiles - 1))
    return pl.pallas_call(
        kernel,
        grid=(2 * tiles + 1,),
        in_specs=[
            SMEM,
            SMEM,
            tile_spec(ff, early),
            tile_spec(ff, early),
            tile_spec(width, early),
            tile_spec(width, early),
            tile_spec(half, both),
            tile_spec(half, both),
            whole((total, width)),
            tile_spec(width, early),
            tile_spec(half, both),
            whole((8, half)),
            tile_spec(width, late),
            whole((8, width)),
            whole((8, half)),
            ANY,
            ANY,
        ]
        + [ANY] * (2 * parts),
        out_specs=[whole((total, wide)), tile_spec(width, early), whole((8, width))] + [ANY] * (2 * parts),
        out_shape=[struct((total, wide), BF), struct((total, width), F32), struct((8, width), F32)]
        + [struct((rows, share), BF)] * parts
        + [struct((rows, wide + width - share), BF)] * parts,
        scratch_shapes=[
            pltpu.VMEM((width, packed), BF),
            pltpu.VMEM((total, width), BF),
            pltpu.VMEM((total, width), BF),
            pltpu.VMEM((TILE, width), F32),
            pltpu.VMEM((total, width), BF),
            pltpu.VMEM((TILE, half), F32),
            pltpu.VMEM((total, half), F32),
            pltpu.VMEM((total, half), F32),
            pltpu.VMEM((total, half), F32),
            pltpu.VMEM((32, half), F32),
            pltpu.VMEM((48, half), F32),
            pltpu.VMEM((32, width), F32),
            pltpu.VMEM((width, wide + width), BF),
            pltpu.SemaphoreType.DMA((2 * parts + 2,)),
        ],
        compiler_params=params(),
        cost_estimate=pl.CostEstimate(
            flops=2 * total * width * (2 * packed + wide),
            bytes_accessed=50 * total * width,
            transcendentals=6 * total * width,
        ),
        name="recurrent_back",
    )


def input_back(parts, cut, dims):
    total, width, half, size = dims
    tiles = total // TILE
    wide = 2 * width + half

    def kernel(me_ref, d_proj, tok, d_middle, gains, *refs):
        left_pieces, right_pieces = refs[:parts], refs[parts : 2 * parts]
        out, sums, w, hold, acc, sems = refs[2 * parts :]
        step = pl.program_id(0)
        me = me_ref[0]

        @pl.when(step == 0)
        def _():
            copies = piece_copies(me, left_pieces, w, pl.ds(0, cut), sems, 0)
            copies += piece_copies(me, right_pieces, w, pl.ds(cut, w.shape[1] - cut), sems, parts)
            for c in copies:
                c.start()
            acc[...] = jnp.zeros_like(acc)
            for c in copies:
                c.wait()

        hold[...] = mm_nt(d_proj[...], w[:, 0:wide])
        gain = gains[0:1, :]

        def norm_back(at):
            here = pl.ds(at, CHUNK)
            x = tok[here, :]
            scale = lax.rsqrt(jnp.mean(x * x, axis=-1, keepdims=True) + 1e-06)
            d = hold[here, :]
            unit = x * scale
            part = d * unit
            acc[...] += part[0:8, :] + part[8:16, :]
            d = d * gain
            out[here, :] = d_middle[here, :] + scale * (d - unit * jnp.mean(d * unit, axis=-1, keepdims=True))

        chunks(TILE, norm_back)

        @pl.when(step == tiles - 1)
        def _():
            sums[...] = jnp.broadcast_to(jnp.sum(acc[...], axis=0, keepdims=True), sums.shape)

    same = lambda i: i
    return pl.pallas_call(
        kernel,
        grid=(tiles,),
        in_specs=[SMEM, tile_spec(wide, same), tile_spec(width, same), tile_spec(width, same), whole((8, width))]
        + [ANY] * (2 * parts),
        out_specs=[tile_spec(width, same), whole((8, width))],
        out_shape=[struct((total, width), F32), struct((8, width), F32)],
        scratch_shapes=[
            pltpu.VMEM((width, wide + LANES), BF),
            pltpu.VMEM((TILE, width), F32),
            pltpu.VMEM((8, width), F32),
            pltpu.SemaphoreType.DMA((2 * parts,)),
        ],
        compiler_params=params(),
        cost_estimate=pl.CostEstimate(
            flops=2 * total * width * wide, bytes_accessed=18 * total * width, transcendentals=total
        ),
        name="input_back",
    )


class Exchange:
    def __init__(self, mesh):
        self.parts = mesh.shape["dp"]
        self.count = mesh.shape["fsdp"]
        self.deep = self.count // 4
        me = lax.axis_index("fsdp")
        self.dp = lax.axis_index("dp")
        self.z = me // 4
        self.y_bit = (me // 2) % 2 == 1
        self.x_bit = me % 2 == 1

    def swap(self, value, mask):
        return lax.ppermute(value, "fsdp", [(i, i ^ mask) for i in range(self.count)])

    def swap_dp(self, value, mask):
        return lax.ppermute(value, "dp", [(i, i ^ mask) for i in range(self.parts)])

    def gather(self, shard, cut):
        held = [shard] + [self.swap(shard, 4 * k) for k in range(1, self.deep)]
        step = 1
        while step < self.deep:
            bit = (self.z // step) % 2 == 1
            held = [jnp.where(bit, held[k ^ step], held[k]) for k in range(self.deep)]
            step *= 2
        stack = jnp.stack(held)
        shares = []
        for piece, order in ((stack[:, :, :cut], "xy"), (stack[:, :, cut:], "yx")):
            if order == "xy":
                got = self.swap(piece, 1)
                piece = jnp.stack([jnp.where(self.x_bit, got, piece), jnp.where(self.x_bit, piece, got)], axis=1)
                got = self.swap(piece, 2)
                piece = jnp.stack([jnp.where(self.y_bit, got, piece), jnp.where(self.y_bit, piece, got)], axis=1)
            else:
                got = self.swap(piece, 2)
                piece = jnp.stack([jnp.where(self.y_bit, got, piece), jnp.where(self.y_bit, piece, got)], axis=1)
                got = self.swap(piece, 1)
                piece = jnp.stack([jnp.where(self.x_bit, got, piece), jnp.where(self.x_bit, piece, got)], axis=2)
            piece = piece.reshape(-1, piece.shape[-1])
            shares.append([piece] + [self.swap_dp(piece, k) for k in range(1, self.parts)])
        return shares

    def scatter(self, slots, order):
        total = slots[0].astype(F32)
        for k in range(1, self.parts):
            total = total + self.swap_dp(slots[k], k).astype(F32)
        rows, columns = total.shape
        total = total.reshape(self.deep, 2, 2, rows // self.count, columns)
        for axis in order:
            if axis == "x":
                low, high, bit, mask = total[..., 0, :, :], total[..., 1, :, :], self.x_bit, 1
            else:
                low, high, bit, mask = total[:, 0], total[:, 1], self.y_bit, 2
            got = self.swap(jnp.where(bit, low, high).astype(BF), mask)
            total = jnp.where(bit, high, low) + got.astype(F32)
        return total

    def scatter_z(self, total):
        out = lax.dynamic_index_in_dim(total, self.z, 0, keepdims=False)
        for k in range(1, self.deep):
            sent = lax.dynamic_index_in_dim(total, self.z ^ k, 0, keepdims=False).astype(BF)
            out = out + self.swap(sent, 4 * k).astype(F32)
        return out

    def total(self, value):
        for k in range(self.parts.bit_length() - 1):
            value = value + self.swap_dp(value, 1 << k)
        for k in range(self.count.bit_length() - 1):
            value = value + self.swap(value, 1 << k)
        return value


def to_chains(value):
    rows, columns = value.shape
    return value.reshape(CHAINS, rows // CHAINS, columns).transpose(1, 0, 2).reshape(rows, columns)


def from_chains(value):
    rows, columns = value.shape
    return value.reshape(rows // CHAINS, CHAINS, columns).transpose(1, 0, 2).reshape(rows, columns)


def turns(phase, rows):
    span = rows // CHAINS
    inside = jnp.arange(span, dtype=F32)[:, None, None] * phase
    outside = (jnp.arange(CHAINS, dtype=F32) * span)[None, :, None] * phase
    ci, si, co, so = jnp.cos(inside), jnp.sin(inside), jnp.cos(outside), jnp.sin(outside)
    shape = (rows, phase.shape[0])
    return (ci * co - si * so).reshape(shape), (si * co + ci * so).reshape(shape)


def build(mesh):
    def per_device(
        tokens,
        lengths,
        w_input,
        w_forget,
        w_gate,
        w_output,
        w_up_gate,
        w_up,
        w_down,
        norm_gain,
        group_gain,
        ffn_gain,
        lower_bound,
        phase,
        cotangent,
    ):
        ex = Exchange(mesh)
        parts = ex.parts
        total, width = tokens.shape
        half = lower_bound.shape[0]
        ff = w_up.shape[1]
        dims = (total, width, half, width // GROUPS)
        shard = w_input.shape[0]
        me = ex.dp.astype(jnp.int32).reshape(1)

        columns = jnp.stack([norm_gain, group_gain, ffn_gain], axis=1)
        columns = jnp.pad(columns, ((0, 0), (0, LANES - 3)))
        pack1 = jnp.concatenate([w_input, w_gate, w_forget, columns], axis=1)
        cut1 = pack1.shape[1] // 2
        pack2 = jnp.concatenate([w_output, w_up_gate, w_up], axis=1)
        cut2 = pack2.shape[1] // 2
        cut3 = width // 2
        one = ex.gather(pack1, cut1)
        two = ex.gather(pack2, cut2)
        three = ex.gather(w_down, cut3)

        tok = to_chains(tokens)
        cot = to_chains(cotangent)
        cos, sin = turns(phase, total)
        low = jnp.broadcast_to(lower_bound, (8, half))

        normed, inner, gate, forget, state, gated, gains = recurrent_forward(parts, cut1, dims)(
            lengths, me, tok, cos, sin, low, *one[0], *one[1]
        )
        middle, ffn_in, left, right, hidden = ffn_up(parts, cut2, dims, ff)(
            me, gated, tok, gains, *two[0], *two[1]
        )
        act, d_left, d_right, *slots = ffn_down_and_back(parts, cut3, dims, ff)(
            lengths, me, hidden, middle, cot, left, right, ffn_in, *three[0], *three[1]
        )
        g_gate, g_up = slots[:parts], slots[parts : 2 * parts]
        down_a, down_b = slots[2 * parts : 3 * parts], slots[3 * parts :]
        s_gate, s_up = ex.scatter(g_gate, "xy"), ex.scatter(g_up, "yx")
        s_down = [ex.scatter(down_a, "xy"), ex.scatter(down_b, "yx")]
        grad_up_gate = ex.scatter_z(s_gate)
        grad_up = ex.scatter_z(s_up)
        grad_down = ex.scatter_z(jnp.concatenate(s_down, axis=-1))

        share = 10 * LANES
        d_proj, d_middle, sums, *slots = recurrent_back(parts, cut2, dims, ff, share)(
            lengths, me, d_left, d_right, middle, cot, cos, sin, state, gate, forget, forget, inner, gains, low,
            gated, normed, *two[0], *two[1]
        )
        rest = [ex.scatter(slots[:parts], "xy"), ex.scatter(slots[parts:], "yx")]
        input_grad, more = input_back(parts, cut1, dims)(me, d_proj, tok, d_middle, gains, *one[0], *one[1])
        rest = ex.scatter_z(jnp.concatenate(rest, axis=-1))
        vector = jnp.concatenate([sums[0:4], more[0:4]], axis=0)
        vector = ex.total(vector)
        at = (ex.dp * ex.count + lax.axis_index("fsdp")) * shard
        own = lax.dynamic_slice(vector, (0, at), (8, shard))
        return (
            from_chains(act),
            from_chains(input_grad),
            rest[:, 0:width],
            rest[:, 2 * width : 2 * width + half],
            rest[:, width : 2 * width],
            rest[:, 2 * width + half :],
            grad_up_gate,
            grad_up,
            grad_down,
            own[4],
            own[1],
            own[0],
            vector[2, 0:half],
            vector[3, 0:half],
        )

    return per_device


def solution(mesh):
    rows = P(("dp", "fsdp"), None)
    vec = P(("dp", "fsdp"))
    in_specs = (rows,) * 9 + (vec,) * 3 + (P(), P(), rows)
    out_specs = (rows,) * 9 + (vec,) * 3 + (P(), P())
    return jax.shard_map(build(mesh), mesh=mesh, in_specs=in_specs, out_specs=out_specs, check_vma=False)
```

```python
import jax
import jax.numpy as jnp
from jax import lax
from jax.experimental import pallas as pl
from jax.experimental.pallas import tpu as pltpu
from jax.sharding import PartitionSpec as P

GROUPS = 4
LANES = 128
CHAINS = 8
TILE = 256
BF = jnp.bfloat16
F32 = jnp.float32
TN = (((0,), (0,)), ((), ()))
NT = (((1,), (1,)), ((), ()))


def mm(left, right):
    return jnp.dot(left, right, preferred_element_type=F32)


def mm_nt(left, right):
    return lax.dot_general(left, right, NT, preferred_element_type=F32)


def mm_tn(left, right):
    return lax.dot_general(left, right, TN, preferred_element_type=F32)


def sigmoid(v):
    return 0.5 * jnp.tanh(0.5 * v) + 0.5


STEPS = {
    "norm": (32, 4),
    "sources": (64, 2),
    "mix": (64, 2),
    "units": (32, 4),
    "finish": (32, 4),
    "norm_back": (32, 4),
    "through": (64, 2),
    "kept": (32, 4),
    "source_back": (64, 2),
}


def chunks(name, body):
    rows, unroll = STEPS[name]

    def step(i, carry):
        body(pl.multiple_of(i * rows, rows), rows)
        return carry

    lax.fori_loop(0, TILE // rows, step, 0, unroll=unroll)


def tiles_of(total, body, backwards=False):
    count = total // TILE

    def step(i, carry):
        body(pl.multiple_of(((count - 1 - i) if backwards else i) * TILE, TILE))
        return carry

    lax.fori_loop(0, count, step, 0)


def span(at, rows):
    return pl.ds(pl.multiple_of(at, rows), rows)


def repeat(value, rows):
    return jnp.concatenate([value] * (rows // 8), axis=0)


def fold(value):
    return jnp.sum(value.reshape(value.shape[0] // 8, 8, value.shape[1]), axis=0)


def cost(micros, moved):
    return pl.CostEstimate(flops=int(micros * 1.15e9), bytes_accessed=moved, transcendentals=0)


def slot_times(base, rows, total):
    row = base + lax.broadcasted_iota(jnp.int32, (rows, 1), 0)
    return (row % CHAINS) * (total // CHAINS) + row // CHAINS


def turned(tables, base, rows):
    ci, si, co, so = tables
    inside = span(base // CHAINS, rows // CHAINS)
    half = ci.shape[1]
    c, s = ci[inside, :][:, None, :], si[inside, :][:, None, :]
    oc, os = co[...][None], so[...][None]
    return (c * oc - s * os).reshape(rows, half), (s * oc + c * os).reshape(rows, half)


def strips(value):
    return [value[:, i * LANES : (i + 1) * LANES] for i in range(value.shape[1] // LANES)]


def group_means(parts, low, size):
    zero = jnp.zeros_like(parts[0])
    sums = []
    for h in (0, 3):
        sums.append(parts[h] + jnp.where(low, parts[h + 1], zero))
        sums.append(jnp.where(low, zero, parts[h + 1]) + parts[h + 2])
    return [jnp.sum(s, axis=-1, keepdims=True) * (1.0 / size) for s in sums]


def group_spread(values, low):
    out = []
    for h in (0, 2):
        out += [values[h], jnp.where(low, values[h], values[h + 1]), values[h + 1]]
    return out


def centre_and_scale(parts, low, size):
    means = group_spread(group_means(parts, low, size), low)
    parts = [p - m for p, m in zip(parts, means)]
    variances = group_means([p * p for p in parts], low, size)
    scales = group_spread([lax.rsqrt(v + 1e-05) for v in variances], low)
    return [p * s for p, s in zip(parts, scales)], scales


def piece_copies(me, pieces, target, columns, sems, first):
    rows = pieces[0].shape[0]
    out = []
    for k, piece in enumerate(pieces):
        at = pl.multiple_of((me ^ k) * rows, 16)
        out.append(pltpu.make_async_copy(piece, target.at[pl.ds(at, rows), columns], sems.at[first + k]))
    return out


HBM = pl.BlockSpec(memory_space=pltpu.HBM)
SMEM = pl.BlockSpec(memory_space=pltpu.SMEM)


def struct(shape, dtype):
    return jax.ShapeDtypeStruct(shape, dtype)


VMEM = pl.BlockSpec(memory_space=pltpu.VMEM)


def far(*arrays):
    return [pltpu.with_memory_space_constraint(v, pltpu.HBM) for v in arrays]


def kernel_call(body, name, ins, outs, scratch, room, estimate, distant=0):
    near = len(outs) - distant
    outs = outs[:near] + [pltpu.HBM(v.shape, v.dtype) for v in outs[near:]]
    return pl.pallas_call(
        body,
        in_specs=ins,
        out_specs=[VMEM] * near + [HBM] * distant,
        out_shape=outs,
        scratch_shapes=scratch,
        compiler_params=pltpu.CompilerParams(vmem_limit_bytes=room * 2**20),
        cost_estimate=estimate,
        name=name,
    )


class Streams:
    def __init__(self, total, sems, arrived=(), leaving=()):
        self.bases = range(0, total, TILE)
        self.sems = sems
        self.arriving = [(far_ref, near_ref) for far_ref, near_ref in arrived]
        self.leaving = [(near_ref, far_ref) for near_ref, far_ref in leaving]

    def copies(self, base, pairs, first):
        block = pl.ds(base, TILE)
        return [
            pltpu.make_async_copy(a.at[block, :], b.at[block, :], self.sems.at[first + n, base // TILE])
            for n, (a, b) in enumerate(pairs)
        ]

    def start(self, backwards=False):
        for base in reversed(self.bases) if backwards else self.bases:
            for c in self.copies(base, self.arriving, 0):
                c.start()

    def wait(self, base):
        for c in self.copies(base, self.arriving, 0):
            c.wait()

    def leave(self, base):
        for c in self.copies(base, self.leaving, len(self.arriving)):
            c.start()

    def finish(self):
        for base in self.bases:
            for c in self.copies(base, self.leaving, len(self.arriving)):
                c.wait()


def stream_sems(total, count):
    return pltpu.SemaphoreType.DMA((count, total // TILE))


def recurrent_project(parts, cut, dims):
    total, width, half, size = dims
    wide = 2 * width + half
    packed = wide + LANES

    def kernel(len_ref, me_ref, low_ref, *refs):
        tables, tok_far, refs = refs[:4], refs[4], refs[5:]
        left_pieces, right_pieces = refs[:parts], refs[parts : 2 * parts]
        local, prod, gate, gains, normed, inner_low, gate_low, forget = refs[2 * parts : 2 * parts + 8]
        w, tok, inner, keep, carry, sems, tile_sems = refs[2 * parts + 8 :]
        first = len_ref[0, 0]
        second = first + len_ref[0, 1]
        me = me_ref[0]
        rights = piece_copies(me, right_pieces, w, pl.ds(cut, packed - cut), sems, parts)
        lefts = piece_copies(me, left_pieces, w, pl.ds(0, cut), sems, 0)
        for c in rights + lefts:
            c.start()
        io = Streams(total, tile_sems, [(tok_far, tok)])
        io.start()
        carry[...] = jnp.concatenate([jnp.zeros((16, half), F32), jnp.ones((8, half), F32)], axis=0)
        for c in rights + lefts:
            c.wait()
        gains[...] = jnp.transpose(w[:, wide:packed].astype(F32))[0:8, :]
        bound = low_ref[0:1, :]

        def project(base):
            block = pl.ds(base, TILE)
            io.wait(base)
            gain = gains[0:1, :]

            def norm(at, rows):
                there = span(base + at, rows)
                x = tok[there, :]
                scale = lax.rsqrt(jnp.mean(x * x, axis=-1, keepdims=True) + 1e-06)
                normed[there, :] = (x * scale * gain).astype(BF)

            chunks("norm", norm)
            value = normed[block, :]
            inner[...] = mm(value, w[:, 0:width])
            gate[block, :] = mm(value, w[:, width : 2 * width])
            forget[block, :] = mm(value, w[:, 2 * width : wide])

            def sources(at, rows):
                here = pl.ds(at, rows)
                there = span(base + at, rows)
                time = slot_times(base + at, rows, total)
                start = (time == 0) | (time == first) | (time == second)
                rest = (1.0 - bound) * (1.0 - sigmoid(forget[there, :]))
                keep[here, :] = jnp.where(start, 0.0, 1.0 - rest)
                re = inner[here, 0:half]
                im = inner[here, half:width]
                inner_low[there, 0:half] = re.astype(BF)
                inner_low[there, half:width] = im.astype(BF)
                gate_low[there, :] = gate[there, :].astype(BF)
                re = rest * re * sigmoid(re)
                im = rest * im * sigmoid(im)
                c, s = turned(tables, base + at, rows)
                local[there, 0:half] = c * re + s * im
                local[there, half:width] = c * im - s * re

            chunks("sources", sources)

            def scan(j, held):
                re, im, p = held
                there = span(base + j * 8, 8)
                k = keep[span(j * 8, 8), :]
                re = k * re + local[there, 0:half]
                im = k * im + local[there, half:width]
                p = k * p
                local[there, 0:half] = re
                local[there, half:width] = im
                prod[there, :] = p
                return re, im, p

            held = (carry[0:8, :], carry[8:16, :], carry[16:24, :])
            held = lax.fori_loop(0, TILE // 8, scan, held, unroll=8)
            carry[0:8, :], carry[8:16, :], carry[16:24, :] = held

        tiles_of(total, project)

    return kernel_call(
        kernel,
        "recurrent_project",
        [SMEM, SMEM] + [VMEM] * 5 + [HBM] * (1 + 2 * parts),
        [
            struct((total, width), F32),
            struct((total, half), F32),
            struct((total, width), F32),
            struct((8, width), F32),
            struct((total, width), BF),
            struct((total, width), BF),
            struct((total, width), BF),
            struct((total, half), F32),
        ],
        [
            pltpu.VMEM((width, packed), BF),
            pltpu.VMEM((total, width), F32),
            pltpu.VMEM((TILE, width), F32),
            pltpu.VMEM((TILE, half), F32),
            pltpu.VMEM((24, half), F32),
            pltpu.SemaphoreType.DMA((2 * parts,)),
            stream_sems(total, 1),
        ],
        10,
        cost(10, 24 * total * width),
    )


def recurrent_mix(dims):
    total, width, half, size = dims

    def kernel(local, prod, gate, gains, *refs):
        tables, (gated, state, ends) = refs[:4], refs[4:]
        p = prod[total - 8 : total, :]
        for h in (0, 1):
            z = local[total - 8 : total, h * half : (h + 1) * half]
            rows = [jnp.zeros((1, half), F32)]
            for c in range(1, CHAINS):
                rows.append(z[c - 1 : c, :] + p[c - 1 : c, :] * rows[-1])
            ends[8 * h : 8 * h + 8, :] = jnp.concatenate(rows, axis=0)
        gain = gains[1:2, :]

        def mix_tile(base):
            def mix(at, rows):
                there = span(base + at, rows)
                low = lax.broadcasted_iota(jnp.int32, (rows, LANES), 1) < LANES // 2
                p = prod[there, :]
                re = local[there, 0:half] + p * repeat(ends[0:8, :], rows)
                im = local[there, half:width] + p * repeat(ends[8:16, :], rows)
                state[there, 0:half] = re
                state[there, half:width] = im
                c, s = turned(tables, base + at, rows)
                mixed = strips(c * re - s * im) + strips(c * im + s * re)
                grouped, _ = centre_and_scale(mixed, low, size)
                for n in range(len(grouped)):
                    lanes = slice(n * LANES, (n + 1) * LANES)
                    opened = grouped[n] * gain[:, lanes] * sigmoid(gate[there, lanes])
                    gated[there, lanes] = opened.astype(BF)

            chunks("mix", mix)

        tiles_of(total, mix_tile)

    return kernel_call(
        kernel,
        "recurrent_mix",
        [VMEM] * 8,
        [struct((total, width), BF), struct((total, width), F32)],
        [pltpu.VMEM((16, half), F32)],
        3,
        cost(4, 20 * total * width),
    )


def ffn_up(parts, cut, dims, ff):
    total, width, half, size = dims
    packed = width + 2 * ff

    def kernel(me_ref, gated, gains, tok_far, *refs):
        left_pieces, right_pieces = refs[:parts], refs[parts : 2 * parts]
        middle, ffn_in, left, right, hidden, w, tok, sems, tile_sems = refs[2 * parts :]
        me = me_ref[0]
        ahead = piece_copies(me, left_pieces, w, pl.ds(0, cut), sems, 0)
        behind = piece_copies(me, right_pieces, w, pl.ds(cut, packed - cut), sems, parts)
        for c in ahead:
            c.start()
        io = Streams(total, tile_sems, [(tok_far, tok)])
        io.start()
        for c in behind:
            c.start()
        gain = gains[2:3, :]
        for c in ahead:
            c.wait()

        def enter(base):
            block = pl.ds(base, TILE)
            io.wait(base)
            middle[block, :] = tok[block, :] + mm(gated[block, :], w[:, 0:width])

            def norm(at, rows):
                there = span(base + at, rows)
                x = middle[there, :]
                scale = lax.rsqrt(jnp.mean(x * x, axis=-1, keepdims=True) + 1e-06)
                ffn_in[there, :] = (x * scale * gain).astype(BF)

            chunks("norm", norm)

        tiles_of(total, enter)
        for c in behind:
            c.wait()

        def expand(base):
            block = pl.ds(base, TILE)
            value = ffn_in[block, :]
            for c in range(0, ff, 256):
                lanes = slice(c, c + 256)
                l = mm(value, w[:, width + c : width + c + 256])
                r = mm(value, w[:, width + ff + c : width + ff + c + 256])
                left[block, lanes] = l.astype(BF)
                right[block, lanes] = r.astype(BF)
                hidden[block, lanes] = (l * sigmoid(l) * r).astype(BF)

        tiles_of(total, expand)

    return kernel_call(
        kernel,
        "ffn_up",
        [SMEM, VMEM, VMEM] + [HBM] * (1 + 2 * parts),
        [
            struct((total, width), F32),
            struct((total, width), BF),
            struct((total, ff), BF),
            struct((total, ff), BF),
            struct((total, ff), BF),
            struct((width, packed), BF),
        ],
        [
            pltpu.VMEM((total, width), F32),
            pltpu.SemaphoreType.DMA((2 * parts,)),
            stream_sems(total, 1),
        ],
        6,
        cost(10, 24 * total * width),
    )


def ffn_turn(parts, cut, dims, ff):
    total, width, half, size = dims

    def kernel(len_ref, me_ref, hidden, middle, left, right, cot_far, *refs):
        left_pieces, right_pieces = refs[:parts], refs[parts : 2 * parts]
        grad, d_left, d_right, act_far, w, cot, act, sems, tile_sems = refs[2 * parts :]
        second = len_ref[0, 0] + len_ref[0, 1]
        me = me_ref[0]
        copies = piece_copies(me, left_pieces, w, pl.ds(0, cut), sems, 0)
        copies += piece_copies(me, right_pieces, w, pl.ds(cut, width - cut), sems, parts)
        for c in copies:
            c.start()
        io = Streams(total, tile_sems, [(cot_far, cot)], [(act, act_far)])
        io.start()
        for c in copies:
            c.wait()

        def turn(base):
            block = pl.ds(base, TILE)
            act[block, :] = middle[block, :] + mm(hidden[block, :], w[...])
            io.wait(base)

            def finish(at, rows):
                there = span(base + at, rows)
                valid = (slot_times(base + at, rows, total) < second).astype(F32)
                act[there, :] = valid * act[there, :]
                grad[there, :] = (valid * cot[there, :]).astype(BF)

            chunks("finish", finish)
            io.leave(base)
            value = grad[block, :]
            for c in range(0, ff, 256):
                lanes = slice(c, c + 256)
                dh = mm_nt(value, w[c : c + 256, :])
                l = left[block, lanes].astype(F32)
                s = sigmoid(l)
                d_right[block, lanes] = (dh * (l * s)).astype(BF)
                d_left[block, lanes] = (dh * right[block, lanes].astype(F32) * (s * (1.0 + l * (1.0 - s)))).astype(BF)

        tiles_of(total, turn)
        io.finish()

    return kernel_call(
        kernel,
        "ffn_turn",
        [SMEM, SMEM] + [VMEM] * 4 + [HBM] * (1 + 2 * parts),
        [
            struct((total, width), BF),
            struct((total, ff), BF),
            struct((total, ff), BF),
            struct((total, width), F32),
        ],
        [
            pltpu.VMEM((ff, width), BF),
            pltpu.VMEM((total, width), F32),
            pltpu.VMEM((total, width), F32),
            pltpu.SemaphoreType.DMA((2 * parts,)),
            stream_sems(total, 2),
        ],
        11,
        cost(11, 30 * total * width),
        distant=1,
    )


def products_of(me, refs, counts, products, slot, parts, aligned, store):
    for n, (l, r, begin, end) in enumerate(products):
        if aligned:
            size = refs[l].shape[1] // parts
            left = refs[l][:, pl.ds(pl.multiple_of((me ^ slot) * size, LANES), size)]
        else:
            left = refs[l][...]
        for c in range(begin, end, 512):
            stop = min(c + 512, end)
            store(n, c - begin, stop - begin, mm_tn(left, refs[counts + r][:, c:stop]))


def prepared(me, lefts, slot, parts):
    sizes = [v.shape[1] // parts for v in lefts]
    aligned = all(size % LANES == 0 for size in sizes)
    if not aligned:
        lefts = [
            lax.dynamic_slice_in_dim(v, (me[0] ^ slot) * size, size, axis=1) for v, size in zip(lefts, sizes)
        ]
    return lefts, sizes, aligned


def grads_cost(lefts, sizes, products):
    flops = sum(2 * lefts[l].shape[0] * sizes[l] * (end - begin) for l, r, begin, end in products)
    return cost(flops / 0.6e9, flops // 256)


def weight_grads(name, me, lefts, rights, products, slot, parts):
    lefts, sizes, aligned = prepared(me, lefts, slot, parts)
    given = len(lefts) + len(rights)

    def kernel(me_ref, *refs):
        def store(n, begin, end, value):
            refs[given + n][:, begin:end] = value.astype(BF)

        products_of(me_ref[0], refs, len(lefts), products, slot, parts, aligned, store)

    outs = [struct((sizes[l], end - begin), BF) for l, r, begin, end in products]
    return kernel_call(
        kernel, name, [SMEM] + [VMEM] * given, outs, [], 8, grads_cost(lefts, sizes, products)
    )(me, *lefts, *rights)


def split_grads(name, me, bits, lefts, rights, shares, swapped, parts, deep, rows):
    lefts, sizes, aligned = prepared(me, lefts, 0, parts)
    given = len(lefts) + len(rights)
    base = min(sizes)
    products = [p for share in shares for p in share]
    owner, places, widths = [], [], []
    for n, share in enumerate(shares):
        at = 0
        for l, r, begin, end in share:
            owner.append(n)
            places.append(at)
            at += (end - begin) * (sizes[l] // base)
        widths.append(at)
    outers = (2 * deep, deep)
    count = len(products)

    def kernel(me_ref, bit_ref, *refs):
        others = refs[given : given + count * (parts - 1)]
        outs = refs[given + count * (parts - 1) :]

        def store(n, begin, end, value):
            for k in range(parts - 1):
                value = value + others[k * count + n][:, begin:end].astype(F32)
            share = owner[n]
            outer = outers[share]
            inner = base // (2 * outer)
            high_is_mine = bit_ref[share] == 1
            send, kept = outs[2 * share : 2 * share + 2]
            times = value.shape[0] // base
            value = value.reshape(outer, 2, inner // rows, times, rows, end - begin)
            for t in range(times):
                to = places[n] + t * (products[n][3] - products[n][2]) + begin
                low = value[:, 0, :, t].reshape(outer, inner, end - begin)
                high = value[:, 1, :, t].reshape(outer, inner, end - begin)
                send[:, :, to : to + end - begin] = jnp.where(high_is_mine, low, high).astype(BF)
                kept[:, :, to : to + end - begin] = jnp.where(high_is_mine, high, low)

        products_of(me_ref[0], refs, len(lefts), products, 0, parts, aligned, store)

    outs = []
    for outer, width in zip(outers, widths):
        shape = (outer, base // (2 * outer), width)
        outs += [struct(shape, BF), struct(shape, F32)]
    flat = [v for arrays in swapped for v in arrays]
    made = kernel_call(
        kernel, name, [SMEM, SMEM] + [VMEM] * (given + len(flat)), outs, [], 8, grads_cost(lefts, sizes, products)
    )(me, bits, *lefts, *rights, *flat)
    return [(made[0], made[1]), (made[2], made[3])]


def ffn_back(dims, ff):
    total, width, half, size = dims
    packed = width + 2 * ff

    def kernel(len_ref, d_left, d_right, middle, gains, w, cot_far, d_mid, sums, d_middle, cot, hold, acc, tile_sems):
        second = len_ref[0, 0] + len_ref[0, 1]
        io = Streams(total, tile_sems, [(cot_far, cot)])
        io.start()
        acc[...] = jnp.zeros_like(acc)
        ffn_gain = gains[2:3, :]

        def tile(base):
            block = pl.ds(base, TILE)
            hold[...] = mm_nt(d_left[block, :], w[:, width : width + ff]) + mm_nt(
                d_right[block, :], w[:, width + ff : packed]
            )
            io.wait(base)

            def norm_back(at, rows):
                here = pl.ds(at, rows)
                there = span(base + at, rows)
                valid = (slot_times(base + at, rows, total) < second).astype(F32)
                x = middle[there, :]
                scale = lax.rsqrt(jnp.mean(x * x, axis=-1, keepdims=True) + 1e-06)
                d = hold[here, :]
                unit = x * scale
                acc[...] += fold(d * unit)
                d = d * ffn_gain
                back = scale * (d - unit * jnp.mean(d * unit, axis=-1, keepdims=True))
                back = back + valid * cot[there, :]
                d_middle[there, :] = back
                d_mid[there, :] = back.astype(BF)

            chunks("norm_back", norm_back)

        tiles_of(total, tile)
        sums[...] = jnp.broadcast_to(jnp.sum(acc[...], axis=0, keepdims=True), sums.shape)

    return kernel_call(
        kernel,
        "ffn_back",
        [SMEM] + [VMEM] * 5 + [HBM],
        [struct((total, width), BF), struct((8, width), F32), struct((total, width), F32)],
        [
            pltpu.VMEM((total, width), F32),
            pltpu.VMEM((TILE, width), F32),
            pltpu.VMEM((8, width), F32),
            stream_sems(total, 1),
        ],
        6,
        cost(10, 30 * total * width),
    )


def group_back(dims):
    total, width, half, size = dims

    def kernel(len_ref, d_mid, gains, low_ref, state, gate, forget, w, *refs):
        tables, refs = refs[:4], refs[4:]
        d_gate, local, prod, sums, hold, keep, carry, acc = refs
        first = len_ref[0, 0]
        second = first + len_ref[0, 1]
        bound = low_ref[0:1, :]

        def keeps(base, rows, value):
            time = slot_times(base, rows, total)
            start = (time == 0) | (time == first) | (time == second)
            return jnp.where(start, 0.0, bound + (1.0 - bound) * sigmoid(value))

        acc[...] = jnp.zeros_like(acc)
        k = keeps(0, 8, forget[0:8, :])
        carry[0:16, :] = jnp.zeros((16, half), F32)
        carry[16:24, :] = jnp.ones((8, half), F32)
        carry[24:32, :] = jnp.concatenate([k[1:8, :], jnp.zeros((1, half), F32)], axis=0)
        gain = gains[1:2, :]

        def tile(base):
            block = pl.ds(base, TILE)
            hold[...] = mm_nt(d_mid[block, :], w[:, 0:width])

            def through(at, rows):
                here = pl.ds(at, rows)
                there = span(base + at, rows)
                low = lax.broadcasted_iota(jnp.int32, (rows, LANES), 1) < LANES // 2
                re, im = state[there, 0:half], state[there, half:width]
                c, s = turned(tables, base + at, rows)
                mixed = strips(c * re - s * im) + strips(c * im + s * re)
                grouped, scales = centre_and_scale(mixed, low, size)
                back = []
                for n in range(len(grouped)):
                    lanes = slice(n * LANES, (n + 1) * LANES)
                    opened = sigmoid(gate[there, lanes].astype(F32))
                    d = hold[here, lanes]
                    part = d * grouped[n] * opened
                    acc[:, lanes] += fold(part)
                    d_gate[there, lanes] = (part * gain[:, lanes] * (1.0 - opened)).astype(BF)
                    back.append(d * opened * gain[:, lanes])
                mean = group_spread(group_means(back, low, size), low)
                along = group_spread(group_means([b * g for b, g in zip(back, grouped)], low, size), low)
                back = [t * (b - m - g * a) for t, b, m, g, a in zip(scales, back, mean, grouped, along)]
                for n in range(3):
                    lanes = slice(n * LANES, (n + 1) * LANES)
                    cn, sn = c[:, lanes], s[:, lanes]
                    local[there, lanes] = cn * back[n] + sn * back[n + 3]
                    local[there, half + n * LANES : half + (n + 1) * LANES] = cn * back[n + 3] - sn * back[n]

            chunks("through", through)

            def kept(at, rows):
                there = span(base + at, rows)
                keep[pl.ds(at, rows), :] = keeps(base + at, rows, forget[there, :])

            chunks("kept", kept)

            def scan(i, held):
                re, im, p, k = held
                at = (TILE // 8 - 1 - i) * 8
                there = span(base + at, 8)
                re = k * re + local[there, 0:half]
                im = k * im + local[there, half:width]
                p = k * p
                local[there, 0:half] = re
                local[there, half:width] = im
                prod[there, :] = p
                return re, im, p, keep[span(at, 8), :]

            held = (carry[0:8, :], carry[8:16, :], carry[16:24, :], carry[24:32, :])
            held = lax.fori_loop(0, TILE // 8, scan, held, unroll=8)
            carry[0:8, :], carry[8:16, :], carry[16:24, :], carry[24:32, :] = held

        tiles_of(total, tile, backwards=True)
        sums[...] = jnp.broadcast_to(jnp.sum(acc[...], axis=0, keepdims=True), sums.shape)

    return kernel_call(
        kernel,
        "group_back",
        [SMEM] + [VMEM] * 11,
        [
            struct((total, width), BF),
            struct((total, width), F32),
            struct((total, half), F32),
            struct((8, width), F32),
        ],
        [
            pltpu.VMEM((TILE, width), F32),
            pltpu.VMEM((TILE, half), F32),
            pltpu.VMEM((32, half), F32),
            pltpu.VMEM((8, width), F32),
        ],
        5,
        cost(13, 40 * total * width),
    )


def source_back(dims):
    total, width, half, size = dims
    wide = 2 * width + half

    def kernel(len_ref, local, prod, d_gate, low_ref, state, forget, inner, *refs):
        tables, (d_proj, sums, ends, acc) = refs[:4], refs[4:]
        first = len_ref[0, 0]
        second = first + len_ref[0, 1]
        bound = low_ref[0:1, :]
        acc[...] = jnp.zeros_like(acc)
        p = prod[0:8, :]
        for h in (0, 1):
            z = local[0:8, h * half : (h + 1) * half]
            made = [jnp.zeros((1, half), F32)]
            for c in range(CHAINS - 2, -1, -1):
                made.append(z[c + 1 : c + 2, :] + p[c + 1 : c + 2, :] * made[-1])
            ends[8 * h : 8 * h + 8, 0:half] = jnp.concatenate(made[::-1], axis=0)
        old = state[total - 8 : total, :]
        ends[16:24, :] = jnp.concatenate([old[7:8, :], old[0:7, :]], axis=0)

        def tile(base):
            def back(at, rows):
                row = base + at
                there = span(row, rows)
                p = prod[there, :]
                re = local[there, 0:half] + p * repeat(ends[0:8, 0:half], rows)
                im = local[there, half:width] + p * repeat(ends[8:16, 0:half], rows)
                up = span(jnp.maximum(row - 8, 0), 8)
                stay = pl.ds(pl.multiple_of(row, 8), rows - 8)
                old_re = jnp.concatenate(
                    [jnp.where(row == 0, ends[16:24, 0:half], state[up, 0:half]), state[stay, 0:half]], axis=0
                )
                old_im = jnp.concatenate(
                    [jnp.where(row == 0, ends[16:24, half:width], state[up, half:width]), state[stay, half:width]],
                    axis=0,
                )
                time = slot_times(row, rows, total)
                start = (time == 0) | (time == first) | (time == second)
                sf = sigmoid(forget[there, :])
                rest = (1.0 - bound) * (1.0 - sf)
                turn = (1.0 - rest) * (im * old_re - re * old_im)
                acc[8:16, :] += fold(jnp.where(start, 0.0, turn))
                d_lam = jnp.where(start, 0.0, re * old_re + im * old_im)
                c, s = turned(tables, row, rows)
                d_re = c * re - s * im
                d_im = c * im + s * re
                for lane, d in ((0, d_re), (half, d_im)):
                    v = inner[there, lane : lane + half].astype(F32)
                    sv = sigmoid(v)
                    d_lam = d_lam - d * (v * sv)
                    d_proj[there, lane : lane + half] = (rest * d * (sv * (1.0 + v * (1.0 - sv)))).astype(BF)
                acc[0:8, :] += fold(d_lam * (1.0 - sf))
                d_proj[there, 2 * width : wide] = (d_lam * rest * sf).astype(BF)
                d_proj[there, width : 2 * width] = d_gate[there, :]

            chunks("source_back", back)

        tiles_of(total, tile)
        out = [jnp.sum(acc[8 * n : 8 * n + 8, :], axis=0, keepdims=True) for n in range(2)]
        out = jnp.concatenate(out + [jnp.zeros((6, half), F32)], axis=0)
        sums[...] = jnp.concatenate([out, jnp.zeros((8, width - half), F32)], axis=1)

    return kernel_call(
        kernel,
        "source_back",
        [SMEM] + [VMEM] * 11,
        [struct((total, wide), BF), struct((8, width), F32)],
        [pltpu.VMEM((24, width), F32), pltpu.VMEM((16, half), F32)],
        3,
        cost(6, 40 * total * width),
    )


def input_back(parts, cut, dims):
    total, width, half, size = dims
    wide = 2 * width + half

    def kernel(me_ref, d_proj, gains, d_middle, tok_far, *refs):
        left_pieces, right_pieces = refs[:parts], refs[parts : 2 * parts]
        out, sums, w, tok, hold, acc, sems, tile_sems = refs[2 * parts :]
        me = me_ref[0]
        copies = piece_copies(me, left_pieces, w, pl.ds(0, cut), sems, 0)
        copies += piece_copies(me, right_pieces, w, pl.ds(cut, w.shape[1] - cut), sems, parts)
        for c in copies:
            c.start()
        io = Streams(total, tile_sems, [(tok_far, tok)])
        io.start()
        acc[...] = jnp.zeros_like(acc)
        gain = gains[0:1, :]
        for c in copies:
            c.wait()

        def tile(base):
            hold[...] = mm_nt(d_proj[pl.ds(base, TILE), :], w[:, 0:wide])
            io.wait(base)

            def norm_back(at, rows):
                here = pl.ds(at, rows)
                there = span(base + at, rows)
                x = tok[there, :]
                scale = lax.rsqrt(jnp.mean(x * x, axis=-1, keepdims=True) + 1e-06)
                d = hold[here, :]
                unit = x * scale
                acc[...] += fold(d * unit)
                d = d * gain
                out[there, :] = d_middle[there, :] + scale * (d - unit * jnp.mean(d * unit, axis=-1, keepdims=True))

            chunks("norm_back", norm_back)

        tiles_of(total, tile)
        sums[...] = jnp.broadcast_to(jnp.sum(acc[...], axis=0, keepdims=True), sums.shape)

    return kernel_call(
        kernel,
        "input_back",
        [SMEM, VMEM, VMEM, VMEM] + [HBM] * (1 + 2 * parts),
        [struct((total, width), F32), struct((8, width), F32)],
        [
            pltpu.VMEM((width, wide + LANES), BF),
            pltpu.VMEM((total, width), F32),
            pltpu.VMEM((TILE, width), F32),
            pltpu.VMEM((8, width), F32),
            pltpu.SemaphoreType.DMA((2 * parts,)),
            stream_sems(total, 1),
        ],
        10,
        cost(7, 20 * total * width),
    )


def order_call(at, held, cut):
    rows, columns = held[0].shape
    deep = len(held)

    def kernel(at_ref, *refs):
        for k in range(deep):
            place = at_ref[0] ^ k
            refs[deep][place] = refs[k][:, 0:cut]
            refs[deep + 1][place] = refs[k][:, cut:columns]

    outs = [struct((deep, rows, cut), BF), struct((deep, rows, columns - cut), BF)]
    return kernel_call(kernel, "order_z", [SMEM] + [VMEM] * deep, outs, [], 2, cost(1, 4 * deep * rows * columns))(
        at, *held
    )


def join_call(bits, own, got):
    count = len(own)

    def kernel(bit_ref, *refs):
        for n in range(count):
            bit = bit_ref[n]
            refs[2 * count + n][:, pl.ds(bit, 1)] = refs[n][...][:, None]
            refs[2 * count + n][:, pl.ds(1 - bit, 1)] = refs[count + n][...][:, None]

    outs = [struct((v.shape[0], 2) + v.shape[1:], BF) for v in own]
    moved = sum(8 * v.size for v in own)
    return kernel_call(kernel, "join", [SMEM] + [VMEM] * (2 * count), outs, [], 2, cost(2, moved))(bits, *own, *got)


def halve_call(bits, kept, got):
    count = len(kept)

    def kernel(bit_ref, *refs):
        for n in range(count):
            bit = bit_ref[n]
            for to, half in ((2 * count + 2 * n, 1 - bit), (2 * count + 2 * n + 1, bit)):
                value = refs[n][:, pl.ds(half, 1)] + refs[count + n][:, pl.ds(half, 1)].astype(F32)
                refs[to][...] = value[:, 0].astype(refs[to].dtype)

    outs = []
    for v in kept:
        shape = v.shape[:1] + v.shape[2:]
        outs += [struct(shape, BF), struct(shape, F32)]
    moved = sum(10 * v.size for v in kept)
    made = kernel_call(kernel, "halve", [SMEM] + [VMEM] * (2 * count), outs, [], 4, cost(3, moved))(bits, *kept, *got)
    return [made[2 * n : 2 * n + 2] for n in range(count)]


def deal_call(at, kept, got):
    deep, rows = kept[0].shape[:2]
    widths = [v.shape[2] for v in kept]
    columns = sum(widths)

    def kernel(at_ref, *refs):
        begin = 0
        for n, width in enumerate(widths):
            for k in range(deep):
                place = at_ref[0] ^ k
                value = refs[n][place] + refs[2 + n][place].astype(F32)
                refs[4 + k][:, begin : begin + width] = value.astype(refs[4 + k].dtype)
            begin += width

    outs = [struct((rows, columns), F32 if k == 0 else BF) for k in range(deep)]
    return kernel_call(kernel, "deal_z", [SMEM] + [VMEM] * 4, outs, [], 4, cost(2, 10 * deep * rows * columns))(
        at, *kept, *got
    )


class Exchange:
    def __init__(self, mesh, fine):
        self.parts = mesh.shape["dp"]
        self.count = mesh.shape["fsdp"]
        self.deep = self.count // 4
        me = lax.axis_index("fsdp")
        self.dp = lax.axis_index("dp")
        self.z = me // 4
        self.y_bit = (me // 2) % 2 == 1
        self.x_bit = me % 2 == 1
        self.fine = fine
        self.at = self.z.astype(jnp.int32).reshape(1)
        self.xy = jnp.stack([self.x_bit, self.y_bit]).astype(jnp.int32)
        self.yx = jnp.stack([self.y_bit, self.x_bit]).astype(jnp.int32)

    def swap(self, value, mask):
        return lax.ppermute(value, "fsdp", [(i, i ^ mask) for i in range(self.count)])

    def swap_dp(self, value, mask):
        return lax.ppermute(value, "dp", [(i, i ^ mask) for i in range(self.parts)])

    def send_z(self, shard, k):
        return self.swap(shard, 4 * k)

    def order_z(self, held, cut):
        if self.fine:
            return order_call(self.at, held, cut)
        step = 1
        while step < self.deep:
            bit = (self.z // step) % 2 == 1
            held = [jnp.where(bit, held[k ^ step], held[k]) for k in range(self.deep)]
            step *= 2
        stack = jnp.stack(held)
        return [stack[:, :, :cut], stack[:, :, cut:]]

    def send_first(self, shares):
        return [self.swap(shares[0], 1), self.swap(shares[1], 2)]

    def join_first(self, shares, got):
        if self.fine:
            return join_call(self.xy, shares, got)
        out = []
        for own, other, bit in zip(shares, got, (self.x_bit, self.y_bit)):
            out.append(jnp.stack([jnp.where(bit, other, own), jnp.where(bit, own, other)], axis=1))
        return out

    def send_second(self, shares):
        return [self.swap(shares[0], 2), self.swap(shares[1], 1)]

    def join_second(self, shares, got):
        if self.fine:
            flat = [v.reshape((-1,) + v.shape[2:]) for v in (shares[1], got[1])]
            made = join_call(self.yx, [shares[0], flat[0]], [got[0], flat[1]])
            return [v.reshape(-1, v.shape[-1]) for v in made]
        out = []
        for own, other, bit, place in zip(shares, got, (self.y_bit, self.x_bit), (1, 2)):
            v = jnp.stack([jnp.where(bit, other, own), jnp.where(bit, own, other)], axis=place)
            out.append(v.reshape(-1, v.shape[-1]))
        return out

    def gather_dp(self, shares):
        return [[v] + [self.swap_dp(v, k) for k in range(1, self.parts)] for v in shares]

    def cut_rows(self, own, swapped, outer, bit, rows):
        columns = []
        for n, value in enumerate(own):
            value = value.astype(F32)
            for arrays in swapped:
                value = value + arrays[n].astype(F32)
            value = value.reshape(self.count, -1, rows, value.shape[1])
            columns += [value[:, i] for i in range(value.shape[1])]
        total = jnp.concatenate(columns, axis=-1)
        total = total.reshape(outer, 2, -1, total.shape[-1])
        low, high = total[:, 0], total[:, 1]
        return jnp.where(bit, low, high).astype(BF), jnp.where(bit, high, low)

    def halves(self, total, bit):
        low, high = total[:, 0], total[:, 1]
        return jnp.where(bit, low, high).astype(BF), jnp.where(bit, high, low)

    def scatter_first(self, cuts):
        return [self.swap(cuts[0][0], 1), self.swap(cuts[1][0], 2)]

    def scatter_second(self, cuts, got):
        kept = [c[1].reshape(self.deep, 2, -1, c[1].shape[-1]) for c in cuts]
        got = [g.reshape(k.shape) for g, k in zip(got, kept)]
        if self.fine:
            cuts = halve_call(self.yx, kept, got)
        else:
            cuts = [self.halves(k + g.astype(F32), bit) for k, g, bit in zip(kept, got, (self.y_bit, self.x_bit))]
        return [c[1] for c in cuts], [self.swap(cuts[0][0], 2), self.swap(cuts[1][0], 1)]

    def scatter_z(self, kept, got):
        if self.fine:
            own, *others = deal_call(self.at, kept, got)
        else:
            total = jnp.concatenate([k + g.astype(F32) for k, g in zip(kept, got)], axis=-1)
            own, *others = [
                lax.dynamic_index_in_dim(total, self.z ^ k, 0, keepdims=False) for k in range(self.deep)
            ]
            others = [v.astype(BF) for v in others]
        return own, [self.swap(v, 4 * k) for k, v in enumerate(others, 1)]

    def finish_z(self, own, got):
        for v in got:
            own = own + v.astype(F32)
        return own

    def total(self, value):
        for k in range(self.parts.bit_length() - 1):
            value = value + self.swap_dp(value, 1 << k)
        for k in range(self.count.bit_length() - 1):
            value = value + self.swap(value, 1 << k)
        return value


def after(value, *others):
    return lax.optimization_barrier((value, *others))[0]


def to_chains(value):
    rows, columns = value.shape
    return value.reshape(CHAINS, rows // CHAINS, columns).transpose(1, 0, 2).reshape(rows, columns)


def from_chains(value):
    rows, columns = value.shape
    return value.reshape(rows // CHAINS, CHAINS, columns).transpose(1, 0, 2).reshape(rows, columns)


def turns(phase, rows):
    length = rows // CHAINS
    inside = jnp.arange(length, dtype=F32)[:, None] * phase
    outside = (jnp.arange(CHAINS, dtype=F32) * length)[:, None] * phase
    return [jnp.cos(inside), jnp.sin(inside), jnp.cos(outside), jnp.sin(outside)]


def build(mesh):
    def per_device(
        tokens,
        lengths,
        w_input,
        w_forget,
        w_gate,
        w_output,
        w_up_gate,
        w_up,
        w_down,
        norm_gain,
        group_gain,
        ffn_gain,
        lower_bound,
        phase,
        cotangent,
    ):
        ex = Exchange(mesh, w_input.shape[0] % 8 == 0)
        parts = ex.parts
        total, width = tokens.shape
        half = lower_bound.shape[0]
        ff = w_up.shape[1]
        dims = (total, width, half, width // GROUPS)
        shard = w_input.shape[0]
        me = ex.dp.astype(jnp.int32).reshape(1)

        columns = jnp.stack([norm_gain, group_gain, ffn_gain], axis=1)
        columns = jnp.pad(columns, ((0, 0), (0, LANES - 3)))
        pack1 = jnp.concatenate([w_input, w_gate, w_forget, columns], axis=1)
        cut1 = pack1.shape[1] // 2
        pack2 = jnp.concatenate([w_output, w_up_gate, w_up], axis=1)
        cut2 = pack2.shape[1] // 2
        cut3 = width // 2
        tok = to_chains(tokens)
        cot = to_chains(cotangent)
        tables = turns(phase, total)
        low = jnp.broadcast_to(lower_bound, (8, half))


        others = range(1, ex.deep)
        one = [pack1] + [ex.send_z(pack1, k) for k in others]
        two = [pack2, ex.send_z(pack2, 1)]
        one, two, tok = after((one, two, tok))
        one = ex.order_z(one, cut1)
        got = ex.send_first(one)
        two += [ex.send_z(after(pack2, two), k) for k in others[1:2]]
        one, got, two, cot = after((one, got, two, cot))
        one = ex.join_first(one, got)
        got = ex.send_second(one)
        two += [ex.send_z(after(pack2, two), k) for k in others[2:]]
        one, got, two = after((one, got, two))
        one = ex.gather_dp(ex.join_second(one, got))
        two = ex.order_z(two, cut2)
        got = ex.send_first(two)
        (tok,) = far(tok)
        local, prod, gate, gains, normed, inner, gate_low, forget = recurrent_project(parts, cut1, dims)(
            lengths, me, low, *tables, tok, *far(*one[0]), *far(*one[1])
        )
        two, got, gains = after((two, got, gains))
        two = ex.join_first(two, got)
        got = ex.send_second(two)
        three = [w_down] + [ex.send_z(after(w_down, two), k) for k in others]
        gated, state = recurrent_mix(dims)(local, prod, gate, gains, *tables)
        two, got, three, gated = after((two, got, three, gated))
        two = ex.gather_dp(ex.join_second(two, got))
        three = ex.order_z(three, cut3)
        late = ex.send_first(three)
        two, three, late = after((two, three, late))
        three = ex.join_first(three, late)
        late = ex.send_second(three)
        (cot,) = far(cot)
        middle, ffn_in, left, right, hidden, w_two = ffn_up(parts, cut2, dims, ff)(
            me, gated, gains, tok, *far(*two[0]), *far(*two[1])
        )
        three, late, ffn_in = after((three, late, ffn_in))
        three = ex.gather_dp(ex.join_second(three, late))
        grad, d_left, d_right, act = ffn_turn(parts, cut3, dims, ff)(
            lengths, me, hidden, middle, left, right, cot, *far(*three[0]), *far(*three[1])
        )

        fold_rows = ff // width

        def first_grads(name, turn, lefts, rights, shares):
            products = shares[0] + shares[1]
            swapped = []
            for k in range(1, parts):
                made = weight_grads(name, turn, lefts, rights, products, k, parts)
                turn = after(me, made)
                swapped.append([ex.swap_dp(v, k) for v in made])
            return swapped, turn

        def last_grads(name, turn, lefts, rights, shares, swapped):
            if ex.fine:
                return split_grads(
                    name, turn, ex.xy, lefts, rights, shares, swapped, parts, ex.deep, shard
                )
            made = weight_grads(name, turn, lefts, rights, shares[0] + shares[1], 0, parts)
            cuts, at = [], 0
            for share, outer, bit in zip(shares, (2 * ex.deep, ex.deep), (ex.x_bit, ex.y_bit)):
                to = at + len(share)
                cuts.append(ex.cut_rows(made[at:to], [v[at:to] for v in swapped], outer, bit, shard))
                at = to
            return cuts

        given = (
            [hidden, ffn_in],
            [grad, d_left, d_right],
            [[(1, 1, 0, ff), (0, 0, 0, cut3)], [(1, 2, 0, ff), (0, 0, cut3, width)]],
        )
        swapped, turn = first_grads("ffn_grads", me, *given)
        ready = after(lengths, turn)
        d_mid, sums, d_middle = ffn_back(dims, ff)(ready, d_left, d_right, middle, gains, w_two, cot)
        ffn = last_grads("ffn_grads", after(turn, sums, swapped), *given, swapped)
        ready = after(lengths, [c[0] for c in ffn])
        got = ex.scatter_first(ffn)
        d_gate, local, prod, more = group_back(dims)(
            ready, d_mid, gains, low, state, gate_low, forget, w_two, *tables
        )
        ffn, got, ready = after((ffn, got, lengths), more)
        kept, got = ex.scatter_second(ffn, got)
        d_proj, bounds = source_back(dims)(after(ready, kept), local, prod, d_gate, low, state, forget, inner, *tables)
        share = 10 * LANES
        wide = 2 * width + half
        given = (
            [normed, gated],
            [d_proj, d_mid],
            [[(0, 0, 0, share)], [(0, 0, share, wide), (1, 1, 0, width)]],
        )
        kept, got, turn = after((kept, got, me), bounds)
        ffn, ffn_got = ex.scatter_z(kept, got)
        swapped, turn = first_grads("recurrent_grads", after(turn, ffn), *given)
        rest = last_grads("recurrent_grads", turn, *given, swapped)
        ready = after(gains, [c[0] for c in rest])
        got = ex.scatter_first(rest)
        input_grad, last = input_back(parts, cut1, dims)(
            me, d_proj, ready, d_middle, tok, *far(*one[0]), *far(*one[1])
        )
        rest, got, ffn_got, act, last = after((rest, got, ffn_got, act, last))
        kept, got = ex.scatter_second(rest, got)
        ffn = ex.finish_z(ffn, ffn_got)
        rest = ex.finish_z(*ex.scatter_z(kept, got))
        grad_up_gate = ffn[:, 0:ff]
        middle_at = ff + fold_rows * cut3
        grad_up = ffn[:, middle_at : middle_at + ff]
        halves = []
        for i in range(fold_rows):
            a = ff + i * cut3
            b = middle_at + ff + i * (width - cut3)
            halves.append(jnp.concatenate([ffn[:, a : a + cut3], ffn[:, b : b + width - cut3]], axis=1))
        grad_down = jnp.concatenate(halves, axis=0)
        vector = jnp.concatenate([sums[0:1], more[0:1], bounds[0:2], last[0:4]], axis=0)
        vector = ex.total(vector)
        at = (ex.dp * ex.count + lax.axis_index("fsdp")) * shard
        own = lax.dynamic_slice(vector, (0, at), (8, shard))
        return (
            from_chains(act),
            from_chains(input_grad),
            rest[:, 0:width],
            rest[:, 2 * width : 2 * width + half],
            rest[:, width : 2 * width],
            rest[:, 2 * width + half :],
            grad_up_gate,
            grad_up,
            grad_down,
            own[4],
            own[1],
            own[0],
            vector[2, 0:half],
            vector[3, 0:half],
        )

    return per_device


def solution(mesh):
    rows = P(("dp", "fsdp"), None)
    vec = P(("dp", "fsdp"))
    in_specs = (rows,) * 9 + (vec,) * 3 + (P(), P(), rows)
    out_specs = (rows,) * 9 + (vec,) * 3 + (P(), P())
    return jax.shard_map(build(mesh), mesh=mesh, in_specs=in_specs, out_specs=out_specs, check_vma=False)
```

```python
import jax
import jax.numpy as jnp
from jax import lax
from jax.experimental import pallas as pl
from jax.experimental.pallas import tpu as pltpu
from jax.sharding import PartitionSpec as P

GROUPS = 4
LANES = 128
CHAINS = 8
TILE = 256
BF = jnp.bfloat16
F32 = jnp.float32
TN = (((0,), (0,)), ((), ()))
NT = (((1,), (1,)), ((), ()))


def mm(left, right):
    return jnp.dot(left, right, preferred_element_type=F32)


def mm_nt(left, right):
    return lax.dot_general(left, right, NT, preferred_element_type=F32)


def mm_tn(left, right):
    return lax.dot_general(left, right, TN, preferred_element_type=F32)


def sigmoid(v):
    return 0.5 * jnp.tanh(0.5 * v) + 0.5


STEPS = {
    "norm": (32, 4),
    "sources": (64, 2),
    "mix": (64, 2),
    "units": (32, 4),
    "finish": (32, 4),
    "norm_back": (32, 4),
    "through": (64, 2),
    "kept": (32, 4),
    "source_back": (64, 2),
}


def chunks(name, body):
    rows, unroll = STEPS[name]

    def step(i, carry):
        body(pl.multiple_of(i * rows, rows), rows)
        return carry

    lax.fori_loop(0, TILE // rows, step, 0, unroll=unroll)


def tiles_of(total, body, backwards=False):
    count = total // TILE

    def step(i, carry):
        body(pl.multiple_of(((count - 1 - i) if backwards else i) * TILE, TILE))
        return carry

    lax.fori_loop(0, count, step, 0)


def span(at, rows):
    return pl.ds(pl.multiple_of(at, rows), rows)


def repeat(value, rows):
    return jnp.concatenate([value] * (rows // 8), axis=0)


def fold(value):
    return jnp.sum(value.reshape(value.shape[0] // 8, 8, value.shape[1]), axis=0)


def cost(micros, moved):
    return pl.CostEstimate(flops=int(micros * 1.15e8), bytes_accessed=moved // 10, transcendentals=0)


def slot_times(base, rows, total):
    row = base + lax.broadcasted_iota(jnp.int32, (rows, 1), 0)
    return (row % CHAINS) * (total // CHAINS) + row // CHAINS


def turned(tables, base, rows):
    ci, si, co, so = tables
    inside = span(base // CHAINS, rows // CHAINS)
    half = ci.shape[1]
    c, s = ci[inside, :][:, None, :], si[inside, :][:, None, :]
    oc, os = co[...][None], so[...][None]
    return (c * oc - s * os).reshape(rows, half), (s * oc + c * os).reshape(rows, half)


def strips(value):
    return [value[:, i * LANES : (i + 1) * LANES] for i in range(value.shape[1] // LANES)]


def group_means(parts, low, size):
    zero = jnp.zeros_like(parts[0])
    sums = []
    for h in (0, 3):
        sums.append(parts[h] + jnp.where(low, parts[h + 1], zero))
        sums.append(jnp.where(low, zero, parts[h + 1]) + parts[h + 2])
    return [jnp.sum(s, axis=-1, keepdims=True) * (1.0 / size) for s in sums]


def group_spread(values, low):
    out = []
    for h in (0, 2):
        out += [values[h], jnp.where(low, values[h], values[h + 1]), values[h + 1]]
    return out


def pack(value):
    high = value.astype(BF).astype(F32)
    middle = (value - high).astype(BF).astype(F32)
    return jnp.concatenate([high, middle, value - high - middle], axis=0).astype(BF)


def unpack(value):
    value = value.astype(F32)
    return value[0:8, :] + value[8:16, :] + value[16:24, :]


def centre_and_scale(parts, low, size):
    means = group_spread(group_means(parts, low, size), low)
    parts = [p - m for p, m in zip(parts, means)]
    variances = group_means([p * p for p in parts], low, size)
    scales = group_spread([lax.rsqrt(v + 1e-05) for v in variances], low)
    return [p * s for p, s in zip(parts, scales)], scales


def piece_copies(me, pieces, target, columns, sems, first):
    rows = pieces[0].shape[0]
    out = []
    for k, piece in enumerate(pieces):
        at = pl.multiple_of((me ^ k) * rows, 16)
        out.append(pltpu.make_async_copy(piece, target.at[pl.ds(at, rows), columns], sems.at[first + k]))
    return out


HBM = pl.BlockSpec(memory_space=pltpu.HBM)
ANY = pl.BlockSpec(memory_space=pl.ANY)
SMEM = pl.BlockSpec(memory_space=pltpu.SMEM)


def struct(shape, dtype):
    return jax.ShapeDtypeStruct(shape, dtype)


VMEM = pl.BlockSpec(memory_space=pltpu.VMEM)


def far(*arrays):
    return [pltpu.with_memory_space_constraint(v, pltpu.HBM) for v in arrays]


def kernel_call(body, name, ins, outs, scratch, room, estimate, distant=0):
    near = len(outs) - distant
    outs = outs[:near] + [pltpu.HBM(v.shape, v.dtype) for v in outs[near:]]
    return pl.pallas_call(
        body,
        in_specs=ins,
        out_specs=[VMEM] * near + [HBM] * distant,
        out_shape=outs,
        scratch_shapes=scratch,
        compiler_params=pltpu.CompilerParams(vmem_limit_bytes=room * 2**20),
        cost_estimate=estimate,
        name=name,
    )


class Streams:
    def __init__(self, total, sems, arrived=(), leaving=()):
        self.bases = range(0, total, TILE)
        self.sems = sems
        self.arriving = [(far_ref, near_ref) for far_ref, near_ref in arrived]
        self.leaving = [(near_ref, far_ref) for near_ref, far_ref in leaving]

    def copies(self, base, pairs, first):
        block = pl.ds(base, TILE)
        return [
            pltpu.make_async_copy(a.at[block, :], b.at[block, :], self.sems.at[first + n, base // TILE])
            for n, (a, b) in enumerate(pairs)
        ]

    def start(self, backwards=False):
        for base in reversed(self.bases) if backwards else self.bases:
            for c in self.copies(base, self.arriving, 0):
                c.start()

    def wait(self, base):
        for c in self.copies(base, self.arriving, 0):
            c.wait()

    def leave(self, base):
        for c in self.copies(base, self.leaving, len(self.arriving)):
            c.start()

    def finish(self):
        for base in self.bases:
            for c in self.copies(base, self.leaving, len(self.arriving)):
                c.wait()


def stream_sems(total, count):
    return pltpu.SemaphoreType.DMA((count, total // TILE))


def recurrent_project(parts, cut, dims):
    total, width, half, size = dims
    wide = 2 * width + half
    packed = wide + LANES

    def kernel(len_ref, me_ref, low_ref, *refs):
        tables, tok_far, refs = refs[:4], refs[4], refs[5:]
        left_pieces, right_pieces = refs[:parts], refs[parts : 2 * parts]
        local, prod, gate, gains, normed, inner_low, gate_low, forget = refs[2 * parts : 2 * parts + 8]
        w, tok, inner, keep, carry, sems, tile_sems = refs[2 * parts + 8 :]
        first = len_ref[0, 0]
        second = first + len_ref[0, 1]
        me = me_ref[0]
        rights = piece_copies(me, right_pieces, w, pl.ds(cut, packed - cut), sems, parts)
        lefts = piece_copies(me, left_pieces, w, pl.ds(0, cut), sems, 0)
        for c in rights + lefts:
            c.start()
        io = Streams(total, tile_sems, [(tok_far, tok)])
        io.start()
        carry[...] = jnp.concatenate([jnp.zeros((16, half), F32), jnp.ones((8, half), F32)], axis=0)
        for c in rights + lefts:
            c.wait()
        gains[...] = jnp.transpose(w[:, wide:packed].astype(F32))[0:8, :]
        bound = low_ref[0:1, :]

        def project(base):
            block = pl.ds(base, TILE)
            io.wait(base)
            gain = gains[0:1, :]

            def norm(at, rows):
                there = span(base + at, rows)
                x = tok[there, :]
                scale = lax.rsqrt(jnp.mean(x * x, axis=-1, keepdims=True) + 1e-06)
                normed[there, :] = (x * scale * gain).astype(BF)

            chunks("norm", norm)
            value = normed[block, :]
            inner[...] = mm(value, w[:, 0:width])
            gate[block, :] = mm(value, w[:, width : 2 * width])
            forget[block, :] = mm(value, w[:, 2 * width : wide])

            def sources(at, rows):
                here = pl.ds(at, rows)
                there = span(base + at, rows)
                time = slot_times(base + at, rows, total)
                start = (time == 0) | (time == first) | (time == second)
                rest = (1.0 - bound) * (1.0 - sigmoid(forget[there, :]))
                keep[here, :] = jnp.where(start, 0.0, 1.0 - rest)
                re = inner[here, 0:half]
                im = inner[here, half:width]
                inner_low[there, 0:half] = re.astype(BF)
                inner_low[there, half:width] = im.astype(BF)
                gate_low[there, :] = gate[there, :].astype(BF)
                re = rest * re * sigmoid(re)
                im = rest * im * sigmoid(im)
                c, s = turned(tables, base + at, rows)
                local[there, 0:half] = c * re + s * im
                local[there, half:width] = c * im - s * re

            chunks("sources", sources)

            def scan(j, held):
                re, im, p = held
                there = span(base + j * 8, 8)
                k = keep[span(j * 8, 8), :]
                re = k * re + local[there, 0:half]
                im = k * im + local[there, half:width]
                p = k * p
                local[there, 0:half] = re
                local[there, half:width] = im
                prod[there, :] = p
                return re, im, p

            held = (carry[0:8, :], carry[8:16, :], carry[16:24, :])
            held = lax.fori_loop(0, TILE // 8, scan, held, unroll=8)
            carry[0:8, :], carry[8:16, :], carry[16:24, :] = held

        tiles_of(total, project)

    return kernel_call(
        kernel,
        "recurrent_project",
        [SMEM, SMEM] + [VMEM] * 5 + [HBM] + [ANY] * (2 * parts),
        [
            struct((total, width), F32),
            struct((total, half), F32),
            struct((total, width), F32),
            struct((8, width), F32),
            struct((total, width), BF),
            struct((total, width), BF),
            struct((total, width), BF),
            struct((total, half), F32),
        ],
        [
            pltpu.VMEM((width, packed), BF),
            pltpu.VMEM((total, width), F32),
            pltpu.VMEM((TILE, width), F32),
            pltpu.VMEM((TILE, half), F32),
            pltpu.VMEM((24, half), F32),
            pltpu.SemaphoreType.DMA((2 * parts,)),
            stream_sems(total, 1),
        ],
        10,
        cost(10, 24 * total * width),
    )


def recurrent_mix(dims):
    total, width, half, size = dims

    def kernel(local, prod, gate, gains, *refs):
        tables, (gated, state, ends) = refs[:4], refs[4:]
        p = prod[total - 8 : total, :]
        for h in (0, 1):
            z = local[total - 8 : total, h * half : (h + 1) * half]
            rows = [jnp.zeros((1, half), F32)]
            for c in range(1, CHAINS):
                rows.append(z[c - 1 : c, :] + p[c - 1 : c, :] * rows[-1])
            ends[8 * h : 8 * h + 8, :] = jnp.concatenate(rows, axis=0)
        gain = gains[1:2, :]

        def mix_tile(base):
            def mix(at, rows):
                there = span(base + at, rows)
                low = lax.broadcasted_iota(jnp.int32, (rows, LANES), 1) < LANES // 2
                p = prod[there, :]
                re = local[there, 0:half] + p * repeat(ends[0:8, :], rows)
                im = local[there, half:width] + p * repeat(ends[8:16, :], rows)
                state[there, 0:half] = re
                state[there, half:width] = im
                c, s = turned(tables, base + at, rows)
                mixed = strips(c * re - s * im) + strips(c * im + s * re)
                grouped, _ = centre_and_scale(mixed, low, size)
                for n in range(len(grouped)):
                    lanes = slice(n * LANES, (n + 1) * LANES)
                    opened = grouped[n] * gain[:, lanes] * sigmoid(gate[there, lanes])
                    gated[there, lanes] = opened.astype(BF)

            chunks("mix", mix)

        tiles_of(total, mix_tile)

    return kernel_call(
        kernel,
        "recurrent_mix",
        [VMEM] * 8,
        [struct((total, width), BF), struct((total, width), F32)],
        [pltpu.VMEM((16, half), F32)],
        3,
        cost(4, 20 * total * width),
    )


def ffn_up(parts, cut, dims, ff):
    total, width, half, size = dims
    packed = width + 2 * ff

    def kernel(me_ref, gated, gains, tok_far, *refs):
        left_pieces, right_pieces = refs[:parts], refs[parts : 2 * parts]
        middle, ffn_in, left, right, hidden, w, tok, sems, tile_sems = refs[2 * parts :]
        me = me_ref[0]
        ahead = piece_copies(me, left_pieces, w, pl.ds(0, cut), sems, 0)
        behind = piece_copies(me, right_pieces, w, pl.ds(cut, packed - cut), sems, parts)
        for c in ahead:
            c.start()
        io = Streams(total, tile_sems, [(tok_far, tok)])
        io.start()
        for c in behind:
            c.start()
        gain = gains[2:3, :]
        for c in ahead:
            c.wait()

        def enter(base):
            block = pl.ds(base, TILE)
            io.wait(base)
            middle[block, :] = tok[block, :] + mm(gated[block, :], w[:, 0:width])

            def norm(at, rows):
                there = span(base + at, rows)
                x = middle[there, :]
                scale = lax.rsqrt(jnp.mean(x * x, axis=-1, keepdims=True) + 1e-06)
                ffn_in[there, :] = (x * scale * gain).astype(BF)

            chunks("norm", norm)

        tiles_of(total, enter)
        for c in behind:
            c.wait()

        def expand(base):
            block = pl.ds(base, TILE)
            value = ffn_in[block, :]
            for c in range(0, ff, 256):
                lanes = slice(c, c + 256)
                l = mm(value, w[:, width + c : width + c + 256])
                r = mm(value, w[:, width + ff + c : width + ff + c + 256])
                left[block, lanes] = l.astype(BF)
                right[block, lanes] = r.astype(BF)
                hidden[block, lanes] = (l * sigmoid(l) * r).astype(BF)

        tiles_of(total, expand)

    return kernel_call(
        kernel,
        "ffn_up",
        [SMEM, VMEM, VMEM] + [HBM] + [ANY] * (2 * parts),
        [
            struct((total, width), F32),
            struct((total, width), BF),
            struct((total, ff), BF),
            struct((total, ff), BF),
            struct((total, ff), BF),
            struct((width, packed), BF),
        ],
        [
            pltpu.VMEM((total, width), F32),
            pltpu.SemaphoreType.DMA((2 * parts,)),
            stream_sems(total, 1),
        ],
        6,
        cost(10, 24 * total * width),
    )


def ffn_turn(parts, cut, dims, ff):
    total, width, half, size = dims

    def kernel(len_ref, me_ref, hidden, middle, left, right, cot_far, *refs):
        left_pieces, right_pieces = refs[:parts], refs[parts : 2 * parts]
        grad, d_left, d_right, act_far, w, cot, act, sems, tile_sems = refs[2 * parts :]
        second = len_ref[0, 0] + len_ref[0, 1]
        me = me_ref[0]
        copies = piece_copies(me, left_pieces, w, pl.ds(0, cut), sems, 0)
        copies += piece_copies(me, right_pieces, w, pl.ds(cut, width - cut), sems, parts)
        for c in copies:
            c.start()

        def arrive(base):
            slot = (base // TILE) % 2
            return pltpu.make_async_copy(cot_far.at[pl.ds(base, TILE), :], cot.at[slot], tile_sems.at[0, slot])

        def leave(base):
            slot = (base // TILE) % 2
            return pltpu.make_async_copy(act.at[slot], act_far.at[pl.ds(base, TILE), :], tile_sems.at[1, slot])

        for base in (0, TILE):
            arrive(base).start()
        for c in copies:
            c.wait()

        def turn(base):
            block = pl.ds(base, TILE)
            slot = (base // TILE) % 2

            @pl.when(base >= 2 * TILE)
            def _():
                leave(base - 2 * TILE).wait()

            act[slot] = middle[block, :] + mm(hidden[block, :], w[...])
            arrive(base).wait()

            def finish(at, rows):
                there = span(base + at, rows)
                valid = (slot_times(base + at, rows, total) < second).astype(F32)
                here = pl.ds(at, rows)
                act[slot, here, :] = valid * act[slot, here, :]
                grad[there, :] = (valid * cot[slot, here, :]).astype(BF)

            chunks("finish", finish)
            leave(base).start()

            @pl.when(base + 2 * TILE < total)
            def _():
                arrive(base + 2 * TILE).start()

            value = grad[block, :]
            for c in range(0, ff, 256):
                lanes = slice(c, c + 256)
                dh = mm_nt(value, w[c : c + 256, :])
                l = left[block, lanes].astype(F32)
                s = sigmoid(l)
                d_right[block, lanes] = (dh * (l * s)).astype(BF)
                d_left[block, lanes] = (dh * right[block, lanes].astype(F32) * (s * (1.0 + l * (1.0 - s)))).astype(BF)

        tiles_of(total, turn)
        for base in (total - 2 * TILE, total - TILE):
            leave(base).wait()

    return kernel_call(
        kernel,
        "ffn_turn",
        [SMEM, SMEM] + [VMEM] * 4 + [HBM] + [ANY] * (2 * parts),
        [
            struct((total, width), BF),
            struct((total, ff), BF),
            struct((total, ff), BF),
            struct((total, width), F32),
        ],
        [
            pltpu.VMEM((ff, width), BF),
            pltpu.VMEM((2, TILE, width), F32),
            pltpu.VMEM((2, TILE, width), F32),
            pltpu.SemaphoreType.DMA((2 * parts,)),
            pltpu.SemaphoreType.DMA((2, 2)),
        ],
        7,
        cost(11, 30 * total * width),
        distant=1,
    )


def products_of(me, refs, counts, products, slot, parts, aligned, store):
    for n, (l, r, begin, end) in enumerate(products):
        if aligned:
            size = refs[l].shape[1] // parts
            left = refs[l][:, pl.ds(pl.multiple_of((me ^ slot) * size, LANES), size)]
        else:
            left = refs[l][...]
        for c in range(begin, end, 512):
            stop = min(c + 512, end)
            store(n, c - begin, stop - begin, mm_tn(left, refs[counts + r][:, c:stop]))


def prepared(me, lefts, slot, parts):
    sizes = [v.shape[1] // parts for v in lefts]
    aligned = all(size % LANES == 0 for size in sizes)
    if not aligned:
        lefts = [
            lax.dynamic_slice_in_dim(v, (me[0] ^ slot) * size, size, axis=1) for v, size in zip(lefts, sizes)
        ]
    return lefts, sizes, aligned


def grads_cost(lefts, sizes, products):
    flops = sum(2 * lefts[l].shape[0] * sizes[l] * (end - begin) for l, r, begin, end in products)
    return cost(flops / 0.6e9, flops // 256)


def weight_grads(name, me, lefts, rights, products, slot, parts):
    lefts, sizes, aligned = prepared(me, lefts, slot, parts)
    given = len(lefts) + len(rights)

    def kernel(me_ref, *refs):
        def store(n, begin, end, value):
            refs[given + n][:, begin:end] = value.astype(BF)

        products_of(me_ref[0], refs, len(lefts), products, slot, parts, aligned, store)

    outs = [struct((sizes[l], end - begin), BF) for l, r, begin, end in products]
    return kernel_call(
        kernel, name, [SMEM] + [VMEM] * given, outs, [], 8, grads_cost(lefts, sizes, products)
    )(me, *lefts, *rights)


def split_grads(name, place, axis, lefts, rights, products, swapped, parts, outer, rows, sums=None):
    lefts, sizes, aligned = prepared(place, lefts, 0, parts)
    given = len(lefts) + len(rights)
    base = min(sizes)
    inner = base // (2 * outer)
    places, width = [], 0
    for l, r, begin, end in products:
        places.append(width)
        width += (end - begin) * (sizes[l] // base)
    count = len(products)
    extra = [] if sums is None else [sums]

    def kernel(place_ref, *refs):
        others = refs[given : given + count * (parts - 1)]
        tail = refs[given + count * (parts - 1) :]
        send, kept = tail[len(extra) : len(extra) + 2]
        high_is_mine = place_ref[axis] == 1

        def store(n, begin, end, value):
            for k in range(parts - 1):
                value = value + others[k * count + n][:, begin:end].astype(F32)
            times = value.shape[0] // base
            value = value.reshape(outer, 2, inner // rows, times, rows, end - begin)
            for t in range(times):
                to = places[n] + t * (products[n][3] - products[n][2]) + begin
                low = value[:, 0, :, t].reshape(outer, inner, end - begin)
                high = value[:, 1, :, t].reshape(outer, inner, end - begin)
                send[:, :, to : to + end - begin] = jnp.where(high_is_mine, low, high).astype(BF)
                kept[:, :, to : to + end - begin] = jnp.where(high_is_mine, high, low)

        products_of(place_ref[0], refs, len(lefts), products, 0, parts, aligned, store)
        if extra:
            held = tail[-1]
            held[place_ref[0]] = tail[0][...]
            for k in range(1, parts):
                block = others[(k - 1) * count]
                held[place_ref[0] ^ k] = unpack(block[0:32, block.shape[1] - LANES :])
            value = held[0]
            for k in range(1, parts):
                value = value + held[k]
            columns = slice(width, width + LANES)
            send[:, :, columns] = jnp.zeros((outer, inner, LANES), BF)
            kept[:, :, columns] = jnp.zeros((outer, inner, LANES), F32)
            send[0, :, columns] = pack(value)
            kept[0, 0:8, columns] = value

    shape = (outer, inner, width + LANES * len(extra))
    flat = [v for arrays in swapped for v in arrays]
    return kernel_call(
        kernel,
        name,
        [SMEM] + [VMEM] * (given + len(flat) + len(extra)),
        [struct(shape, BF), struct(shape, F32)],
        [pltpu.VMEM((parts, 8, LANES), F32)] * len(extra),
        8,
        grads_cost(lefts, sizes, products),
    )(place, *lefts, *rights, *flat, *extra)


def middle_back(dims, ff):
    total, width, half, size = dims
    packed = width + 2 * ff

    def kernel(len_ref, d_left, d_right, middle, gains, low_ref, state, gate, forget, w, *refs):
        tables, cot_far, refs = refs[:4], refs[4], refs[5:]
        d_mid, d_middle, d_gate, local, prod, cot, hold, keep, carry, tile_sems = refs
        first = len_ref[0, 0]
        second = first + len_ref[0, 1]
        bound = low_ref[0:1, :]
        io = Streams(total, tile_sems, [(cot_far, cot)])
        io.start(backwards=True)
        ffn_gain = gains[2:3, :]
        gain = gains[1:2, :]

        def keeps(base, rows, value):
            time = slot_times(base, rows, total)
            start = (time == 0) | (time == first) | (time == second)
            return jnp.where(start, 0.0, bound + (1.0 - bound) * sigmoid(value))

        k = keeps(0, 8, forget[0:8, :])
        carry[0:16, :] = jnp.zeros((16, half), F32)
        carry[16:24, :] = jnp.ones((8, half), F32)
        carry[24:32, :] = jnp.concatenate([k[1:8, :], jnp.zeros((1, half), F32)], axis=0)

        def enter(base):
            block = pl.ds(base, TILE)
            hold[...] = mm_nt(d_left[block, :], w[:, width : width + ff]) + mm_nt(
                d_right[block, :], w[:, width + ff : packed]
            )
            io.wait(base)

            def norm_back(at, rows):
                here = pl.ds(at, rows)
                there = span(base + at, rows)
                valid = (slot_times(base + at, rows, total) < second).astype(F32)
                x = middle[there, :]
                scale = lax.rsqrt(jnp.mean(x * x, axis=-1, keepdims=True) + 1e-06)
                d = hold[here, :]
                unit = x * scale
                d = d * ffn_gain
                back = scale * (d - unit * jnp.mean(d * unit, axis=-1, keepdims=True))
                back = back + valid * cot[there, :]
                d_middle[there, :] = back
                d_mid[there, :] = back.astype(BF)

            chunks("norm_back", norm_back)

        def tile(base):
            enter(base)
            block = pl.ds(base, TILE)
            hold[...] = mm_nt(d_mid[block, :], w[:, 0:width])

            def through(at, rows):
                here = pl.ds(at, rows)
                there = span(base + at, rows)
                low = lax.broadcasted_iota(jnp.int32, (rows, LANES), 1) < LANES // 2
                re, im = state[there, 0:half], state[there, half:width]
                c, s = turned(tables, base + at, rows)
                mixed = strips(c * re - s * im) + strips(c * im + s * re)
                grouped, scales = centre_and_scale(mixed, low, size)
                back = []
                for n in range(len(grouped)):
                    lanes = slice(n * LANES, (n + 1) * LANES)
                    opened = sigmoid(gate[there, lanes].astype(F32))
                    d = hold[here, lanes]
                    part = d * grouped[n] * opened
                    d_gate[there, lanes] = (part * gain[:, lanes] * (1.0 - opened)).astype(BF)
                    back.append(d * opened * gain[:, lanes])
                mean = group_spread(group_means(back, low, size), low)
                along = group_spread(group_means([b * g for b, g in zip(back, grouped)], low, size), low)
                back = [t * (b - m - g * a) for t, b, m, g, a in zip(scales, back, mean, grouped, along)]
                for n in range(3):
                    lanes = slice(n * LANES, (n + 1) * LANES)
                    cn, sn = c[:, lanes], s[:, lanes]
                    local[there, lanes] = cn * back[n] + sn * back[n + 3]
                    local[there, half + n * LANES : half + (n + 1) * LANES] = cn * back[n + 3] - sn * back[n]

            chunks("through", through)

            def kept(at, rows):
                there = span(base + at, rows)
                keep[pl.ds(at, rows), :] = keeps(base + at, rows, forget[there, :])

            chunks("kept", kept)

            def scan(i, held):
                re, im, p, k = held
                at = (TILE // 8 - 1 - i) * 8
                there = span(base + at, 8)
                re = k * re + local[there, 0:half]
                im = k * im + local[there, half:width]
                p = k * p
                local[there, 0:half] = re
                local[there, half:width] = im
                prod[there, :] = p
                return re, im, p, keep[span(at, 8), :]

            held = (carry[0:8, :], carry[8:16, :], carry[16:24, :], carry[24:32, :])
            held = lax.fori_loop(0, TILE // 8, scan, held, unroll=8)
            carry[0:8, :], carry[8:16, :], carry[16:24, :], carry[24:32, :] = held

        tiles_of(total, tile, backwards=True)

    return kernel_call(
        kernel,
        "middle_back",
        [SMEM] + [VMEM] * 13 + [HBM],
        [
            struct((total, width), BF),
            struct((total, width), F32),
            struct((total, width), BF),
            struct((total, width), F32),
            struct((total, half), F32),
        ],
        [
            pltpu.VMEM((total, width), F32),
            pltpu.VMEM((TILE, width), F32),
            pltpu.VMEM((TILE, half), F32),
            pltpu.VMEM((32, half), F32),
            stream_sems(total, 1),
        ],
        8,
        cost(19, 60 * total * width),
    )


def source_back(dims, parts, me, lefts, d_mid, products, fine):
    total, width, half, size = dims
    wide = 2 * width + half
    given, sizes, aligned = [], None, True
    for slot in range(1, parts):
        made, sizes, aligned = prepared(me, lefts, slot, parts)
        given.append(list(made))
    if aligned:
        given = [list(lefts)] * max(parts - 1, 0)
        flat = list(lefts)
    else:
        flat = [v for made in given for v in made]
    count = len(products)

    def kernel(len_ref, me_ref, local, prod, d_gate, low_ref, state, forget, inner, *refs):
        tables, refs = refs[:4], refs[4:]
        left_refs, d_mid_ref, refs = refs[: len(flat)], refs[len(flat)], refs[len(flat) + 1 :]
        d_proj, sums = refs[:2]
        slots, (ends, acc) = refs[2 : 2 + count * (parts - 1)], refs[2 + count * (parts - 1) :]
        first = len_ref[0, 0]
        second = first + len_ref[0, 1]
        bound = low_ref[0:1, :]
        acc[...] = jnp.zeros_like(acc)
        p = prod[0:8, :]
        for h in (0, 1):
            z = local[0:8, h * half : (h + 1) * half]
            made = [jnp.zeros((1, half), F32)]
            for c in range(CHAINS - 2, -1, -1):
                made.append(z[c + 1 : c + 2, :] + p[c + 1 : c + 2, :] * made[-1])
            ends[8 * h : 8 * h + 8, 0:half] = jnp.concatenate(made[::-1], axis=0)
        old = state[total - 8 : total, :]
        ends[16:24, :] = jnp.concatenate([old[7:8, :], old[0:7, :]], axis=0)

        def tile(base):
            def back(at, rows):
                row = base + at
                there = span(row, rows)
                p = prod[there, :]
                re = local[there, 0:half] + p * repeat(ends[0:8, 0:half], rows)
                im = local[there, half:width] + p * repeat(ends[8:16, 0:half], rows)
                up = span(jnp.maximum(row - 8, 0), 8)
                stay = pl.ds(pl.multiple_of(row, 8), rows - 8)
                old_re = jnp.concatenate(
                    [jnp.where(row == 0, ends[16:24, 0:half], state[up, 0:half]), state[stay, 0:half]], axis=0
                )
                old_im = jnp.concatenate(
                    [jnp.where(row == 0, ends[16:24, half:width], state[up, half:width]), state[stay, half:width]],
                    axis=0,
                )
                time = slot_times(row, rows, total)
                start = (time == 0) | (time == first) | (time == second)
                sf = sigmoid(forget[there, :])
                rest = (1.0 - bound) * (1.0 - sf)
                turn = (1.0 - rest) * (im * old_re - re * old_im)
                acc[8:16, :] += fold(jnp.where(start, 0.0, turn))
                d_lam = jnp.where(start, 0.0, re * old_re + im * old_im)
                c, s = turned(tables, row, rows)
                d_re = c * re - s * im
                d_im = c * im + s * re
                for lane, d in ((0, d_re), (half, d_im)):
                    v = inner[there, lane : lane + half].astype(F32)
                    sv = sigmoid(v)
                    d_lam = d_lam - d * (v * sv)
                    d_proj[there, lane : lane + half] = (rest * d * (sv * (1.0 + v * (1.0 - sv)))).astype(BF)
                acc[0:8, :] += fold(d_lam * (1.0 - sf))
                d_proj[there, 2 * width : wide] = (d_lam * rest * sf).astype(BF)
                d_proj[there, width : 2 * width] = d_gate[there, :]

            chunks("source_back", back)

        tiles_of(total, tile)
        out = [jnp.sum(acc[8 * n : 8 * n + 8, :], axis=0, keepdims=True) for n in range(2)]
        out = strips(out[0]) + strips(out[1])
        sums[...] = jnp.concatenate(out + [jnp.zeros((8 - len(out), LANES), F32)], axis=0)
        for slot in range(1, parts):
            used = left_refs if aligned else left_refs[(slot - 1) * len(lefts) : slot * len(lefts)]

            def store(n, begin, end, value):
                slots[(slot - 1) * count + n][:, begin:end] = value.astype(BF)

            products_of(
                me_ref[0], [*used, d_proj, d_mid_ref], len(lefts), products, slot, parts, aligned, store
            )
            if fine:
                block = slots[(slot - 1) * count]
                rest = jnp.zeros((block.shape[0] - 24, LANES), F32)
                carried = jnp.concatenate([pack(sums[...]).astype(F32), rest], axis=0)
                block[:, block.shape[1] - LANES :] = carried.astype(BF)

    outs = [struct((total, wide), BF), struct((8, LANES), F32)]
    widths = [end - begin for l, r, begin, end in products]
    widths[0] += LANES if fine else 0
    outs += [struct((width // parts, n), BF) for n in widths] * (parts - 1)
    call = kernel_call(
        kernel,
        "source_back",
        [SMEM, SMEM] + [VMEM] * (12 + len(flat)),
        outs,
        [pltpu.VMEM((24, width), F32), pltpu.VMEM((16, half), F32)],
        6,
        cost(10, 40 * total * width),
    )

    def run(lengths, me, *arrays):
        d_proj, sums, *slots = call(lengths, me, *arrays, *flat, d_mid)
        return d_proj, sums, [slots[k * count : (k + 1) * count] for k in range(parts - 1)]

    return run


def input_back(parts, cut, dims):
    total, width, half, size = dims
    wide = 2 * width + half

    def kernel(me_ref, d_proj, gains, d_middle, tok_far, *refs):
        left_pieces, right_pieces = refs[:parts], refs[parts : 2 * parts]
        out, w, tok, hold, sems, tile_sems = refs[2 * parts :]
        me = me_ref[0]
        copies = piece_copies(me, left_pieces, w, pl.ds(0, cut), sems, 0)
        copies += piece_copies(me, right_pieces, w, pl.ds(cut, w.shape[1] - cut), sems, parts)
        for c in copies:
            c.start()
        io = Streams(total, tile_sems, [(tok_far, tok)])
        io.start()
        gain = gains[0:1, :]
        for c in copies:
            c.wait()

        def tile(base):
            hold[...] = mm_nt(d_proj[pl.ds(base, TILE), :], w[:, 0:wide])
            io.wait(base)

            def norm_back(at, rows):
                here = pl.ds(at, rows)
                there = span(base + at, rows)
                x = tok[there, :]
                scale = lax.rsqrt(jnp.mean(x * x, axis=-1, keepdims=True) + 1e-06)
                d = hold[here, :]
                unit = x * scale
                d = d * gain
                out[there, :] = d_middle[there, :] + scale * (d - unit * jnp.mean(d * unit, axis=-1, keepdims=True))

            chunks("norm_back", norm_back)

        tiles_of(total, tile)

    return kernel_call(
        kernel,
        "input_back",
        [SMEM, VMEM, VMEM, VMEM] + [HBM] + [ANY] * (2 * parts),
        [struct((total, width), F32)],
        [
            pltpu.VMEM((width, wide + LANES), BF),
            pltpu.VMEM((total, width), F32),
            pltpu.VMEM((TILE, width), F32),
            pltpu.SemaphoreType.DMA((2 * parts,)),
            stream_sems(total, 1),
        ],
        10,
        cost(7, 20 * total * width),
    )


def order_call(place, held, cut):
    rows, columns = held[0].shape
    deep = len(held)

    def kernel(place_ref, *refs):
        for k in range(deep):
            at = place_ref[1] ^ k
            refs[deep][at] = refs[k][:, 0:cut]
            refs[deep + 1][at] = refs[k][:, cut:columns]

    outs = [struct((deep, rows, cut), BF), struct((deep, rows, columns - cut), BF)]
    return kernel_call(kernel, "order_z", [SMEM] + [VMEM] * deep, outs, [], 2, cost(1, 4 * deep * rows * columns))(
        place, *held
    )


def join_call(place, axes, own, got):
    count = len(own)

    def kernel(place_ref, *refs):
        for n in range(count):
            bit = place_ref[axes[n]]
            refs[2 * count + n][:, pl.ds(bit, 1)] = refs[n][...][:, None]
            refs[2 * count + n][:, pl.ds(1 - bit, 1)] = refs[count + n][...][:, None]

    outs = [struct((v.shape[0], 2) + v.shape[1:], BF) for v in own]
    moved = sum(8 * v.size for v in own)
    return kernel_call(kernel, "join", [SMEM] + [VMEM] * (2 * count), outs, [], 2, cost(2, moved))(place, *own, *got)


def halve_call(place, axes, kept, got, carried):
    count = len(kept)

    def kernel(place_ref, *refs):
        for n in range(count):
            bit = place_ref[axes[n]]
            for to, half in ((2 * count + 2 * n, 1 - bit), (2 * count + 2 * n + 1, bit)):
                value = refs[n][:, pl.ds(half, 1)] + refs[count + n][:, pl.ds(half, 1)].astype(F32)
                refs[to][...] = value[:, 0].astype(refs[to].dtype)
            if carried and n == 0:
                columns = slice(kept[0].shape[-1] - LANES, None)
                value = refs[0][0, 0, 0:8, columns] + unpack(refs[count][0, 0, :, columns])
                refs[2 * count][0, :, columns] = pack(value)
                refs[2 * count + 1][0, 0:8, columns] = value

    outs = []
    for v in kept:
        shape = v.shape[:1] + v.shape[2:]
        outs += [struct(shape, BF), struct(shape, F32)]
    moved = sum(10 * v.size for v in kept)
    made = kernel_call(kernel, "halve", [SMEM] + [VMEM] * (2 * count), outs, [], 4, cost(3, moved))(place, *kept, *got)
    return [made[2 * n : 2 * n + 2] for n in range(count)]


def deal_call(place, kept, got, carried):
    deep, rows = kept[0].shape[:2]
    widths = [v.shape[2] for v in kept]
    columns = sum(widths)
    widths[0] -= LANES if carried else 0

    def kernel(place_ref, *refs):
        begin = 0
        for n, width in enumerate(widths):
            for k in range(deep):
                at = place_ref[1] ^ k
                value = refs[n][at, :, 0:width] + refs[2 + n][at, :, 0:width].astype(F32)
                refs[4 + k][:, begin : begin + width] = value.astype(refs[4 + k].dtype)
            begin += width
        if carried:
            last = slice(widths[0], widths[0] + LANES)
            value = refs[0][0, 0:8, last] + unpack(refs[2][0, :, last])
            refs[4][:, begin:] = jnp.concatenate([value, jnp.zeros((rows - 8, LANES), F32)], axis=0)
            for k in range(1, deep):
                refs[4 + k][:, begin:] = pack(value)

    outs = [struct((rows, columns), F32 if k == 0 else BF) for k in range(deep)]
    return kernel_call(kernel, "deal_z", [SMEM] + [VMEM] * 4, outs, [], 4, cost(2, 10 * deep * rows * columns))(
        place, *kept, *got
    )


def finish_call(place, own, got, cuts, gains, carried):
    deep = len(got) + 1
    rows, columns = own.shape
    bounds = [0, *cuts, columns - (LANES if carried else 0)]
    pairs = list(zip(bounds[:-1], bounds[1:]))
    flat = [v for gain, weights in gains for v in (gain, *weights.values())]

    def kernel(place_ref, *refs):
        given = list(refs[deep : deep + len(flat)])
        outs = refs[deep + len(flat) :]
        for n, (a, b) in enumerate(pairs):
            value = refs[0][:, a:b]
            for k in range(1, deep):
                value = value + refs[k][:, a:b].astype(F32)
            outs[n][...] = value
        at = len(pairs)
        for gain, weights in gains:
            gain_ref = given.pop(0)
            total = jnp.zeros((rows, 1), F32)
            for n in weights:
                total = total + jnp.sum(given.pop(0)[...].astype(F32) * outs[n][...], axis=1, keepdims=True)
            shape = (rows, LANES)
            diagonal = lax.broadcasted_iota(jnp.int32, shape, 0) == lax.broadcasted_iota(jnp.int32, shape, 1)
            row = jnp.sum(jnp.where(diagonal, total, 0.0), axis=0, keepdims=True)
            outs[at][...] = row[:, 0:rows] / gain_ref[...].astype(F32)
            at += 1
        if carried:
            held = outs[-1]
            held[place_ref[1]] = refs[0][0:8, columns - LANES :]
            for k in range(1, deep):
                held[place_ref[1] ^ k] = unpack(refs[k][:, columns - LANES :])
            value = held[0]
            for k in range(1, deep):
                value = value + held[k]
            for n in range(2):
                strip = [value[3 * n + i : 3 * n + i + 1, :] for i in range(3)]
                outs[at + n][...] = jnp.concatenate(strip, axis=1)

    outs = [struct((rows, b - a), F32) for a, b in pairs] + [struct((1, rows), F32)] * len(gains)
    outs += [struct((1, 3 * LANES), F32)] * (2 * carried)
    scratch = [pltpu.VMEM((deep, 8, LANES), F32)] * carried
    made = kernel_call(
        kernel, "finish", [SMEM] + [VMEM] * (deep + len(flat)), outs, scratch, 2, cost(2, 12 * rows * columns)
    )(place, own, *got, *flat)
    return [v.reshape(-1) if v.shape[0] == 1 else v for v in made]


class Exchange:
    def __init__(self, mesh, fine):
        self.parts = mesh.shape["dp"]
        self.count = mesh.shape["fsdp"]
        self.deep = self.count // 4
        me = lax.axis_index("fsdp")
        self.dp = lax.axis_index("dp")
        self.z = me // 4
        self.y_bit = (me // 2) % 2 == 1
        self.x_bit = me % 2 == 1
        self.fine = fine
        self.place = jnp.stack([self.dp, self.z, (me // 2) % 2, me % 2]).astype(jnp.int32)

    def swap(self, value, mask):
        return lax.ppermute(value, "fsdp", [(i, i ^ mask) for i in range(self.count)])

    def swap_dp(self, value, mask):
        return lax.ppermute(value, "dp", [(i, i ^ mask) for i in range(self.parts)])

    def send_z(self, shard, k):
        return self.swap(shard, 4 * k)

    def order_z(self, held, cut):
        if self.fine:
            return order_call(self.place, held, cut)
        step = 1
        while step < self.deep:
            bit = (self.z // step) % 2 == 1
            held = [jnp.where(bit, held[k ^ step], held[k]) for k in range(self.deep)]
            step *= 2
        stack = jnp.stack(held)
        return [stack[:, :, :cut], stack[:, :, cut:]]

    def send_first(self, shares):
        return [self.swap(shares[0], 1), self.swap(shares[1], 2)]

    def join_first(self, shares, got):
        if self.fine:
            return join_call(self.place, (3, 2), shares, got)
        out = []
        for own, other, bit in zip(shares, got, (self.x_bit, self.y_bit)):
            out.append(jnp.stack([jnp.where(bit, other, own), jnp.where(bit, own, other)], axis=1))
        return out

    def send_second(self, shares):
        return [self.swap(shares[0], 2), self.swap(shares[1], 1)]

    def join_second(self, shares, got):
        if self.fine:
            flat = [v.reshape((-1,) + v.shape[2:]) for v in (shares[1], got[1])]
            made = join_call(self.place, (2, 3), [shares[0], flat[0]], [got[0], flat[1]])
            return [v.reshape(-1, v.shape[-1]) for v in made]
        out = []
        for own, other, bit, place in zip(shares, got, (self.y_bit, self.x_bit), (1, 2)):
            v = jnp.stack([jnp.where(bit, other, own), jnp.where(bit, own, other)], axis=place)
            out.append(v.reshape(-1, v.shape[-1]))
        return out

    def gather_dp(self, shares):
        return [[v] + [self.swap_dp(v, k) for k in range(1, self.parts)] for v in shares]

    def cut_rows(self, own, swapped, outer, bit, rows):
        columns = []
        for n, value in enumerate(own):
            value = value.astype(F32)
            for arrays in swapped:
                value = value + arrays[n].astype(F32)
            value = value.reshape(self.count, -1, rows, value.shape[1])
            columns += [value[:, i] for i in range(value.shape[1])]
        total = jnp.concatenate(columns, axis=-1)
        total = total.reshape(outer, 2, -1, total.shape[-1])
        low, high = total[:, 0], total[:, 1]
        return jnp.where(bit, low, high).astype(BF), jnp.where(bit, high, low)

    def halves(self, total, bit):
        low, high = total[:, 0], total[:, 1]
        return jnp.where(bit, low, high).astype(BF), jnp.where(bit, high, low)

    def halve(self, kept, got, carried=False):
        kept = [v.reshape(self.deep, 2, -1, v.shape[-1]) for v in kept]
        got = [g.reshape(k.shape) for g, k in zip(got, kept)]
        if self.fine:
            return halve_call(self.place, (2, 3), kept, got, carried)
        return [self.halves(k + g.astype(F32), bit) for k, g, bit in zip(kept, got, (self.y_bit, self.x_bit))]

    def send_halves(self, cuts):
        return [c[1] for c in cuts], [self.swap(cuts[0][0], 2), self.swap(cuts[1][0], 1)]

    def deal_z(self, kept, got, carried=False):
        if self.fine:
            own, *others = deal_call(self.place, kept, got, carried)
            return own, others
        total = jnp.concatenate([k + g.astype(F32) for k, g in zip(kept, got)], axis=-1)
        own, *others = [lax.dynamic_index_in_dim(total, self.z ^ k, 0, keepdims=False) for k in range(self.deep)]
        return own, [v.astype(BF) for v in others]

    def send_parts(self, others):
        return [self.swap(v, 4 * k) for k, v in enumerate(others, 1)]

    def finish_z(self, own, got, cuts, gains, carried=False):
        if self.fine:
            return finish_call(self.place, own, got, cuts, gains, carried)
        for v in got:
            own = own + v.astype(F32)
        made = jnp.split(own, cuts, axis=1)
        for gain, weights in gains:
            total = sum(jnp.sum(w.astype(F32) * made[n], axis=1) for n, w in weights.items())
            made.append(total / gain[0].astype(F32))
        return made

    def total(self, value):
        for k in range(self.parts.bit_length() - 1):
            value = value + self.swap_dp(value, 1 << k)
        for k in range(self.count.bit_length() - 1):
            value = value + self.swap(value, 1 << k)
        return value


def after(value, *others):
    return lax.optimization_barrier((value, *others))[0]


def to_chains(value):
    rows, columns = value.shape
    return value.reshape(CHAINS, rows // CHAINS, columns).transpose(1, 0, 2).reshape(rows, columns)


def from_chains(value):
    rows, columns = value.shape
    return value.reshape(rows // CHAINS, CHAINS, columns).transpose(1, 0, 2).reshape(rows, columns)


def turns(phase, rows):
    length = rows // CHAINS
    inside = jnp.arange(length, dtype=F32)[:, None] * phase
    outside = (jnp.arange(CHAINS, dtype=F32) * length)[:, None] * phase
    return [jnp.cos(inside), jnp.sin(inside), jnp.cos(outside), jnp.sin(outside)]


def build(mesh):
    def per_device(
        tokens,
        lengths,
        w_input,
        w_forget,
        w_gate,
        w_output,
        w_up_gate,
        w_up,
        w_down,
        norm_gain,
        group_gain,
        ffn_gain,
        lower_bound,
        phase,
        cotangent,
    ):
        ex = Exchange(mesh, w_input.shape[0] % 24 == 0)
        parts = ex.parts
        total, width = tokens.shape
        half = lower_bound.shape[0]
        ff = w_up.shape[1]
        dims = (total, width, half, width // GROUPS)
        shard = w_input.shape[0]

        columns = jnp.stack([norm_gain, group_gain, ffn_gain], axis=1)
        columns = jnp.pad(columns, ((0, 0), (0, LANES - 3)))
        pack1 = jnp.concatenate([w_input, w_gate, w_forget, columns], axis=1)
        cut1 = pack1.shape[1] // 2
        pack2 = jnp.concatenate([w_output, w_up_gate, w_up], axis=1)
        cut2 = pack2.shape[1] // 2
        cut3 = width // 2
        tok = to_chains(tokens)
        cot = to_chains(cotangent)
        tables = turns(phase, total)
        low = jnp.broadcast_to(lower_bound, (8, half))


        others = range(1, ex.deep)
        one = [pack1] + [ex.send_z(pack1, k) for k in others]
        two = [pack2, ex.send_z(pack2, 1)]
        one, two, ex.place = after((one, two, ex.place))
        one = ex.order_z(one, cut1)
        got = ex.send_first(one)
        two += [ex.send_z(after(pack2, two), k) for k in others[1:2]]
        one, got, two, tok, tables, low = after((one, got, two, tok, tables, low))
        one = ex.join_first(one, got)
        got = ex.send_second(one)
        two += [ex.send_z(after(pack2, two), k) for k in others[2:]]
        one, got, two, cot = after((one, got, two, cot))
        one = ex.gather_dp(ex.join_second(one, got))
        two = ex.order_z(two, cut2)
        got = ex.send_first(two)
        (tok,) = far(tok)
        local, prod, gate, gains, normed, inner, gate_low, forget = recurrent_project(parts, cut1, dims)(
            lengths, ex.place, low, *tables, tok, *one[0], *one[1]
        )
        two, got, gains, w_down = after((two, got, gains, w_down))
        two = ex.join_first(two, got)
        got = ex.send_second(two)
        three = [w_down] + [ex.send_z(w_down, k) for k in others]
        gated, state = recurrent_mix(dims)(local, prod, gate, gains, *tables)
        three, gated = after((three, gated))
        three = ex.order_z(three, cut3)
        late = ex.send_first(three)
        two, got, three, late, gated = after((two, got, three, late, gated))
        two = ex.gather_dp(ex.join_second(two, got))
        three = ex.join_first(three, late)
        late = ex.send_second(three)
        (cot,) = far(cot)
        middle, ffn_in, left, right, hidden, w_two = ffn_up(parts, cut2, dims, ff)(
            ex.place, gated, gains, tok, *two[0], *two[1]
        )
        three, late, ffn_in = after((three, late, ffn_in))
        three = ex.gather_dp(ex.join_second(three, late))
        grad, d_left, d_right, act = ffn_turn(parts, cut3, dims, ff)(
            lengths, ex.place, hidden, middle, left, right, cot, *three[0], *three[1]
        )

        fold_rows = ff // width

        def last_grads(name, turn, lefts, rights, shares, swapped, sums=None):
            kept, got = [], []
            for n, (outer, bit, mask) in enumerate(((2 * ex.deep, ex.x_bit, 1), (ex.deep, ex.y_bit, 2))):
                if ex.fine:
                    send, keep = split_grads(
                        name, turn[0], 3 - n, lefts, rights, shares[n], swapped[n], parts, outer, shard, None if n else sums
                    )
                else:
                    made = weight_grads(name, turn[0], lefts, rights, shares[n], 0, parts)
                    send, keep = ex.cut_rows(made, swapped[n], outer, bit, shard)
                send, keep, turn = after((send, keep, turn))
                kept.append(keep)
                got.append(ex.swap(send, mask))
            return kept, got, turn

        given = (
            [hidden, ffn_in],
            [grad, d_left, d_right],
            [[(1, 1, 0, ff), (0, 0, 0, cut3)], [(1, 2, 0, ff), (0, 0, cut3, width)]],
        )
        swapped, turn = [], (ex.place, lengths)
        for products in given[2]:
            arrays = []
            for k in range(1, parts):
                made = weight_grads("ffn_grads", turn[0], given[0], given[1], products, k, parts)
                made, turn = after((made, turn))
                arrays.append([ex.swap_dp(v, k) for v in made])
            swapped.append(arrays)
        kept, got, turn = last_grads("ffn_grads", turn, *given, swapped)
        d_mid, d_middle, d_gate, local, prod = middle_back(dims, ff)(
            turn[1], d_left, d_right, middle, gains, low, state, gate_low, forget, w_two, *tables, cot
        )
        kept, got, local, turn = after((kept, got, local, turn))
        cuts, turn = after((ex.halve(kept, got), turn))
        kept, got = ex.send_halves(cuts)
        share = 10 * LANES
        wide = 2 * width + half
        shares = [[(0, 0, 0, share)], [(0, 0, share, wide), (1, 1, 0, width)]]
        d_proj, sums, made = source_back(dims, parts, ex.place, [normed, gated], d_mid, shares[0] + shares[1], ex.fine)(
            turn[1], turn[0], local, prod, d_gate, low, state, forget, inner, *tables
        )
        made, kept, got, sums, turn = after((made, kept, got, sums, turn))
        swapped = [[], []]
        for k, arrays in enumerate(made, 1):
            arrays = [ex.swap_dp(v, k) for v in arrays]
            swapped[0].append(arrays[: len(shares[0])])
            swapped[1].append(arrays[len(shares[0]) :])
        ffn, others = ex.deal_z(kept, got)
        ffn, others, turn = after((ffn, others, turn))
        ffn_got = ex.send_parts(others)
        kept, got, turn = last_grads(
            "recurrent_grads", turn, [normed, gated], [d_proj, d_mid], shares, swapped, sums
        )
        (input_grad,) = input_back(parts, cut1, dims)(
            turn[0], d_proj, gains, d_middle, tok, *one[0], *one[1]
        )
        input_grad, act = after((input_grad, act))
        act = from_chains(act)
        input_grad, ffn_got, kept, got, act = after((input_grad, ffn_got, kept, got, act))
        kept, got = ex.send_halves(ex.halve(kept, got, ex.fine))
        middle_at = ff + fold_rows * cut3
        bounds = [ff, middle_at, middle_at + ff]
        grad_up_gate, down_a, grad_up, down_b, grad_ffn_gain = ex.finish_z(
            ffn, ffn_got, bounds, [(ffn_gain[None], {0: w_up_gate, 2: w_up})]
        )
        kept, got, input_grad = after((kept, got, input_grad))
        rest, others = ex.deal_z(kept, got, ex.fine)
        rest, others, input_grad = after((rest, others, input_grad))
        got = ex.send_parts(others)
        input_grad = from_chains(input_grad)
        if not ex.fine:
            sums = ex.total(sums)
        norm_weights = {0: w_input, 1: w_gate, 2: w_forget}
        made = ex.finish_z(
            rest,
            got,
            [width, 2 * width, wide],
            [(norm_gain[None], norm_weights), (group_gain[None], {3: w_output})],
            ex.fine,
        )
        grad_input, grad_gate, grad_forget, grad_output, grad_norm_gain, grad_group_gain = made[:6]
        if ex.fine:
            grad_lower, grad_phase = made[6:]
        else:
            ahead = half // LANES
            grad_lower, grad_phase = sums[0:ahead].reshape(half), sums[ahead : 2 * ahead].reshape(half)

        halves = []
        for i in range(fold_rows):
            left_half = down_a[:, i * cut3 : (i + 1) * cut3]
            right_half = down_b[:, i * (width - cut3) : (i + 1) * (width - cut3)]
            halves.append(jnp.concatenate([left_half, right_half], axis=1))
        grad_down = jnp.concatenate(halves, axis=0)
        return (
            act,
            input_grad,
            grad_input,
            grad_forget,
            grad_gate,
            grad_output,
            grad_up_gate,
            grad_up,
            grad_down,
            grad_norm_gain,
            grad_group_gain,
            grad_ffn_gain,
            grad_lower,
            grad_phase,
        )

    return per_device


def solution(mesh):
    rows = P(("dp", "fsdp"), None)
    vec = P(("dp", "fsdp"))
    in_specs = (rows,) * 9 + (vec,) * 3 + (P(), P(), rows)
    out_specs = (rows,) * 9 + (vec,) * 3 + (P(), P())
    return jax.shard_map(build(mesh), mesh=mesh, in_specs=in_specs, out_specs=out_specs, check_vma=False)
```

```python
import jax
import jax.numpy as jnp
from jax import lax
from jax.experimental import pallas as pl
from jax.experimental.pallas import tpu as pltpu
from jax.sharding import PartitionSpec as P

GROUPS = 4
LANES = 128
CHAINS = 8
TILE = 256
BF = jnp.bfloat16
F32 = jnp.float32
TN = (((0,), (0,)), ((), ()))
NT = (((1,), (1,)), ((), ()))


def mm(left, right):
    return jnp.dot(left, right, preferred_element_type=F32)


def mm_nt(left, right):
    return lax.dot_general(left, right, NT, preferred_element_type=F32)


def mm_tn(left, right):
    return lax.dot_general(left, right, TN, preferred_element_type=F32)


def sigmoid(v):
    return 0.5 * jnp.tanh(0.5 * v) + 0.5


STEPS = {
    "norm": (256, 1),
    "sources": (64, 4),
    "mix": (64, 2),
    "finish": (256, 1),
    "norm_back": (256, 1),
    "through": (64, 4),
    "kept": (256, 1),
    "source_back": (64, 1),
}


def chunks(name, body):
    rows, unroll = STEPS[name]

    def step(i, carry):
        body(pl.multiple_of(i * rows, rows), rows)
        return carry

    lax.fori_loop(0, TILE // rows, step, 0, unroll=unroll)


def tiles_of(total, body, backwards=False):
    count = total // TILE

    def step(i, carry):
        body(pl.multiple_of(((count - 1 - i) if backwards else i) * TILE, TILE))
        return carry

    lax.fori_loop(0, count, step, 0)


def span(at, rows):
    return pl.ds(pl.multiple_of(at, rows), rows)


def repeat(value, rows):
    return jnp.concatenate([value] * (rows // 8), axis=0)


def fold(value):
    return jnp.sum(value.reshape(value.shape[0] // 8, 8, value.shape[1]), axis=0)


def cost(micros, moved):
    return pl.CostEstimate(flops=int(micros * 1.15e8), bytes_accessed=moved // 10, transcendentals=0)


def slot_times(base, rows, total):
    row = base + lax.broadcasted_iota(jnp.int32, (rows, 1), 0)
    return (row % CHAINS) * (total // CHAINS) + row // CHAINS


def turned(tables, base, rows):
    ci, si, co, so = tables
    inside = span(base // CHAINS, rows // CHAINS)
    half = ci.shape[1]
    c, s = ci[inside, :][:, None, :], si[inside, :][:, None, :]
    oc, os = co[...][None], so[...][None]
    return (c * oc - s * os).reshape(rows, half), (s * oc + c * os).reshape(rows, half)


def strips(value):
    return [value[:, i * LANES : (i + 1) * LANES] for i in range(value.shape[1] // LANES)]


def group_means(parts, low, size):
    zero = jnp.zeros_like(parts[0])
    sums = []
    for h in (0, 3):
        sums.append(parts[h] + jnp.where(low, parts[h + 1], zero))
        sums.append(jnp.where(low, zero, parts[h + 1]) + parts[h + 2])
    return [jnp.sum(s, axis=-1, keepdims=True) * (1.0 / size) for s in sums]


def group_spread(values, low):
    out = []
    for h in (0, 2):
        out += [values[h], jnp.where(low, values[h], values[h + 1]), values[h + 1]]
    return out


def pack(value):
    high = value.astype(BF).astype(F32)
    middle = (value - high).astype(BF).astype(F32)
    return jnp.concatenate([high, middle, value - high - middle], axis=0).astype(BF)


def unpack(value):
    value = value.astype(F32)
    return value[0:8, :] + value[8:16, :] + value[16:24, :]


def centre_and_scale(parts, low, size):
    means = group_spread(group_means(parts, low, size), low)
    parts = [p - m for p, m in zip(parts, means)]
    variances = group_means([p * p for p in parts], low, size)
    scales = group_spread([lax.rsqrt(v + 1e-05) for v in variances], low)
    return [p * s for p, s in zip(parts, scales)], scales


def piece_copies(me, pieces, target, columns, sems, first):
    rows = pieces[0].shape[0]
    out = []
    for k, piece in enumerate(pieces):
        at = pl.multiple_of((me ^ k) * rows, 16)
        out.append(pltpu.make_async_copy(piece, target.at[pl.ds(at, rows), columns], sems.at[first + k]))
    return out


HBM = pl.BlockSpec(memory_space=pltpu.HBM)
ANY = pl.BlockSpec(memory_space=pl.ANY)
SMEM = pl.BlockSpec(memory_space=pltpu.SMEM)


def struct(shape, dtype):
    return jax.ShapeDtypeStruct(shape, dtype)


VMEM = pl.BlockSpec(memory_space=pltpu.VMEM)


def far(*arrays):
    return [pltpu.with_memory_space_constraint(v, pltpu.HBM) for v in arrays]


def kernel_call(body, name, ins, outs, scratch, room, estimate, distant=0):
    near = len(outs) - distant
    outs = outs[:near] + [pltpu.HBM(v.shape, v.dtype) for v in outs[near:]]
    return pl.pallas_call(
        body,
        in_specs=ins,
        out_specs=[VMEM] * near + [HBM] * distant,
        out_shape=outs,
        scratch_shapes=scratch,
        compiler_params=pltpu.CompilerParams(vmem_limit_bytes=room * 2**20),
        cost_estimate=estimate,
        name=name,
    )


class Streams:
    def __init__(self, total, sems, arrived=(), leaving=()):
        self.bases = range(0, total, TILE)
        self.sems = sems
        self.arriving = [(far_ref, near_ref) for far_ref, near_ref in arrived]
        self.leaving = [(near_ref, far_ref) for near_ref, far_ref in leaving]

    def copies(self, base, pairs, first):
        block = pl.ds(base, TILE)
        return [
            pltpu.make_async_copy(a.at[block, :], b.at[block, :], self.sems.at[first + n, base // TILE])
            for n, (a, b) in enumerate(pairs)
        ]

    def start(self, backwards=False):
        for base in reversed(self.bases) if backwards else self.bases:
            for c in self.copies(base, self.arriving, 0):
                c.start()

    def wait(self, base):
        for c in self.copies(base, self.arriving, 0):
            c.wait()

    def leave(self, base):
        for c in self.copies(base, self.leaving, len(self.arriving)):
            c.start()

    def finish(self):
        for base in self.bases:
            for c in self.copies(base, self.leaving, len(self.arriving)):
                c.wait()


def stream_sems(total, count):
    return pltpu.SemaphoreType.DMA((count, total // TILE))


def recurrent_project(parts, cut, dims):
    total, width, half, size = dims
    wide = 2 * width + half
    packed = wide + LANES

    def kernel(place_ref, tok_far, *refs):
        left_pieces, right_pieces = refs[:parts], refs[parts : 2 * parts]
        inner, gate, forget, gains, normed, inner_low, gate_low, w, tok, sems, tile_sems = refs[2 * parts :]
        me = place_ref[0]
        small = [v.at[:, pl.ds(wide - cut, LANES)] for v in right_pieces]
        large = [v.at[:, pl.ds(0, wide - cut)] for v in right_pieces]
        ahead = piece_copies(me, small, w, pl.ds(wide, LANES), sems, 0)
        behind = piece_copies(me, left_pieces, w, pl.ds(0, cut), sems, parts)
        behind += piece_copies(me, large, w, pl.ds(cut, wide - cut), sems, 2 * parts)
        io = Streams(total, tile_sems, [(tok_far, tok)])
        for c in ahead:
            c.start()
        io.start()
        for c in behind:
            c.start()
        for c in ahead:
            c.wait()
        gains[...] = jnp.transpose(w[:, wide:packed].astype(F32))[0:8, :]

        def project(base):
            block = pl.ds(base, TILE)
            io.wait(base)
            gain = gains[0:1, :]

            def norm(at, rows):
                there = span(base + at, rows)
                x = tok[there, :]
                scale = lax.rsqrt(jnp.mean(x * x, axis=-1, keepdims=True) + 1e-06)
                normed[there, :] = (x * scale * gain).astype(BF)

            chunks("norm", norm)

            @pl.when(base == 0)
            def _():
                for c in behind:
                    c.wait()

            value = normed[block, :]
            for n in range(0, width, 256):
                lanes = slice(n, n + 256)
                made = mm(value, w[:, n : n + 256])
                inner[block, lanes] = made
                inner_low[block, lanes] = made.astype(BF)
                made = mm(value, w[:, width + n : width + n + 256])
                gate[block, lanes] = made
                gate_low[block, lanes] = made.astype(BF)
            forget[block, :] = mm(value, w[:, 2 * width : wide])

        tiles_of(total, project)

    return kernel_call(
        kernel,
        "recurrent_project",
        [SMEM] + [HBM] + [ANY] * (2 * parts),
        [
            struct((total, width), F32),
            struct((total, width), F32),
            struct((total, half), F32),
            struct((8, width), F32),
            struct((total, width), BF),
            struct((total, width), BF),
            struct((total, width), BF),
        ],
        [
            pltpu.VMEM((width, packed), BF),
            pltpu.VMEM((total, width), F32),
            pltpu.SemaphoreType.DMA((3 * parts,)),
            stream_sems(total, 1),
        ],
        10,
        cost(6, 24 * total * width),
    )


def recurrent_mix(dims):
    total, width, half, size = dims

    def kernel(len_ref, inner, gate, forget, gains, low_ref, *refs):
        tables, (gated, state, prod, keep, carry, ends) = refs[:4], refs[4:]
        first = len_ref[0, 0]
        second = first + len_ref[0, 1]
        carry[...] = jnp.concatenate([jnp.zeros((16, half), F32), jnp.ones((8, half), F32)], axis=0)
        bound = low_ref[0:1, :]

        def chain_tile(base):
            def sources(at, rows):
                here = pl.ds(at, rows)
                there = span(base + at, rows)
                time = slot_times(base + at, rows, total)
                start = (time == 0) | (time == first) | (time == second)
                rest = (1.0 - bound) * (1.0 - sigmoid(forget[there, :]))
                keep[here, :] = jnp.where(start, 0.0, 1.0 - rest)
                re = inner[there, 0:half]
                im = inner[there, half:width]
                re = rest * re * sigmoid(re)
                im = rest * im * sigmoid(im)
                c, s = turned(tables, base + at, rows)
                state[there, 0:half] = c * re + s * im
                state[there, half:width] = c * im - s * re

            chunks("sources", sources)

            def scan(j, held):
                re, im, p = held
                there = span(base + j * 8, 8)
                k = keep[span(j * 8, 8), :]
                re = k * re + state[there, 0:half]
                im = k * im + state[there, half:width]
                p = k * p
                state[there, 0:half] = re
                state[there, half:width] = im
                prod[there, :] = p
                return re, im, p

            held = (carry[0:8, :], carry[8:16, :], carry[16:24, :])
            held = lax.fori_loop(0, TILE // 8, scan, held, unroll=8)
            carry[0:8, :], carry[8:16, :], carry[16:24, :] = held

        tiles_of(total, chain_tile)
        p = carry[16:24, :]
        for h in (0, 8):
            z = carry[h : h + 8, :]
            rows = [jnp.zeros((1, half), F32)]
            for c in range(1, CHAINS):
                rows.append(z[c - 1 : c, :] + p[c - 1 : c, :] * rows[-1])
            ends[h : h + 8, :] = jnp.concatenate(rows, axis=0)
        gain = gains[1:2, :]

        def mix_tile(base):
            def mix(at, rows):
                there = span(base + at, rows)
                low = lax.broadcasted_iota(jnp.int32, (rows, LANES), 1) < LANES // 2
                p = prod[there, :]
                re = state[there, 0:half] + p * repeat(ends[0:8, :], rows)
                im = state[there, half:width] + p * repeat(ends[8:16, :], rows)
                state[there, 0:half] = re
                state[there, half:width] = im
                c, s = turned(tables, base + at, rows)
                mixed = strips(c * re - s * im) + strips(c * im + s * re)
                grouped, _ = centre_and_scale(mixed, low, size)
                for n in range(len(grouped)):
                    lanes = slice(n * LANES, (n + 1) * LANES)
                    opened = grouped[n] * gain[:, lanes] * sigmoid(gate[there, lanes])
                    gated[there, lanes] = opened.astype(BF)

            chunks("mix", mix)

        tiles_of(total, mix_tile)

    return kernel_call(
        kernel,
        "recurrent_mix",
        [SMEM] + [VMEM] * 9,
        [struct((total, width), BF), struct((total, width), F32)],
        [
            pltpu.VMEM((total, half), F32),
            pltpu.VMEM((TILE, half), F32),
            pltpu.VMEM((24, half), F32),
            pltpu.VMEM((16, half), F32),
        ],
        5,
        cost(8, 20 * total * width),
    )


def ffn_up(parts, cut, dims, ff):
    total, width, half, size = dims
    packed = width + 2 * ff

    def kernel(me_ref, gated, gains, tok_far, *refs):
        left_pieces, right_pieces = refs[:parts], refs[parts : 2 * parts]
        middle, ffn_in, to_left, to_right, hidden, w, tok, sems, tile_sems = refs[2 * parts :]
        me = me_ref[0]
        first = [v.at[:, pl.ds(0, width)] for v in left_pieces]
        then = [v.at[:, pl.ds(width, cut - width)] for v in left_pieces]
        ahead = piece_copies(me, first, w, pl.ds(0, width), sems, 0)
        behind = piece_copies(me, then, w, pl.ds(width, cut - width), sems, parts)
        behind += piece_copies(me, right_pieces, w, pl.ds(cut, packed - cut), sems, 2 * parts)
        for c in ahead:
            c.start()
        io = Streams(total, tile_sems, [(tok_far, tok)])
        io.start()
        for c in behind:
            c.start()
        gain = gains[2:3, :]
        for c in ahead:
            c.wait()

        def enter(base):
            block = pl.ds(base, TILE)
            io.wait(base)
            middle[block, :] = tok[block, :] + mm(gated[block, :], w[:, 0:width])

            def norm(at, rows):
                there = span(base + at, rows)
                x = middle[there, :]
                scale = lax.rsqrt(jnp.mean(x * x, axis=-1, keepdims=True) + 1e-06)
                ffn_in[there, :] = (x * scale * gain).astype(BF)

            chunks("norm", norm)

        tiles_of(total, enter)
        for c in behind:
            c.wait()

        def expand(base):
            block = pl.ds(base, TILE)
            value = ffn_in[block, :]
            for c in range(0, ff, 256):
                lanes = slice(c, c + 256)
                l = mm(value, w[:, width + c : width + c + 256])
                r = mm(value, w[:, width + ff + c : width + ff + c + 256])
                g = sigmoid(l)
                u = l * g
                to_right[block, lanes] = u.astype(BF)
                to_left[block, lanes] = ((g + u - u * g) * r).astype(BF)
                hidden[block, lanes] = (u * r).astype(BF)

        tiles_of(total, expand)

    return kernel_call(
        kernel,
        "ffn_up",
        [SMEM, VMEM, VMEM] + [HBM] + [ANY] * (2 * parts),
        [
            struct((total, width), F32),
            struct((total, width), BF),
            struct((total, ff), BF),
            struct((total, ff), BF),
            struct((total, ff), BF),
            struct((width, packed), BF),
        ],
        [
            pltpu.VMEM((total, width), F32),
            pltpu.SemaphoreType.DMA((3 * parts,)),
            stream_sems(total, 1),
        ],
        6,
        cost(10, 24 * total * width),
    )


def ffn_turn(parts, cut, dims, ff):
    total, width, half, size = dims

    def kernel(len_ref, me_ref, to_left, to_right, cot_far, *refs):
        left_pieces, right_pieces = refs[:parts], refs[parts : 2 * parts]
        grad, d_left, d_right, w, cot, sems, tile_sems = refs[2 * parts :]
        second = len_ref[0, 0] + len_ref[0, 1]
        me = me_ref[0]
        copies = piece_copies(me, left_pieces, w, pl.ds(0, cut), sems, 0)
        copies += piece_copies(me, right_pieces, w, pl.ds(cut, width - cut), sems, parts)

        def arrive(base):
            slot = (base // TILE) % 2
            return pltpu.make_async_copy(cot_far.at[pl.ds(base, TILE), :], cot.at[slot], tile_sems.at[slot])

        for base in (0, TILE):
            arrive(base).start()
        for c in copies:
            c.start()

        def turn(base):
            block = pl.ds(base, TILE)
            slot = (base // TILE) % 2
            arrive(base).wait()

            def finish(at, rows):
                there = span(base + at, rows)
                valid = (slot_times(base + at, rows, total) < second).astype(F32)
                grad[there, :] = (valid * cot[slot, pl.ds(at, rows), :]).astype(BF)

            chunks("finish", finish)

            @pl.when(base + 2 * TILE < total)
            def _():
                arrive(base + 2 * TILE).start()

            @pl.when(base == 0)
            def _():
                for c in copies:
                    c.wait()

            value = grad[block, :]
            for c in range(0, ff, 256):
                lanes = slice(c, c + 256)
                dh = mm_nt(value, w[c : c + 256, :])
                d_right[block, lanes] = (dh * to_right[block, lanes].astype(F32)).astype(BF)
                d_left[block, lanes] = (dh * to_left[block, lanes].astype(F32)).astype(BF)

        tiles_of(total, turn)

    return kernel_call(
        kernel,
        "ffn_turn",
        [SMEM, SMEM] + [VMEM] * 2 + [HBM] + [ANY] * (2 * parts),
        [
            struct((total, width), BF),
            struct((total, ff), BF),
            struct((total, ff), BF),
            struct((ff, width), BF),
        ],
        [
            pltpu.VMEM((2, TILE, width), F32),
            pltpu.SemaphoreType.DMA((2 * parts,)),
            pltpu.SemaphoreType.DMA((2,)),
        ],
        4,
        cost(6, 20 * total * width),
    )


def ffn_out(dims, ff):
    total, width, half, size = dims

    def kernel(len_ref, hidden, middle, w, act_far, act, tile_sems):
        second = len_ref[0, 0] + len_ref[0, 1]

        def leave(base):
            slot = (base // TILE) % 2
            return pltpu.make_async_copy(act.at[slot], act_far.at[pl.ds(base, TILE), :], tile_sems.at[slot])

        def tile(base):
            block = pl.ds(base, TILE)
            slot = (base // TILE) % 2

            @pl.when(base >= 2 * TILE)
            def _():
                leave(base - 2 * TILE).wait()

            valid = (slot_times(base, TILE, total) < second).astype(F32)
            act[slot] = valid * (middle[block, :] + mm(hidden[block, :], w[...]))
            leave(base).start()

        tiles_of(total, tile)
        for base in (total - 2 * TILE, total - TILE):
            leave(base).wait()

    return kernel_call(
        kernel,
        "ffn_out",
        [SMEM] + [VMEM] * 3,
        [struct((total, width), F32)],
        [pltpu.VMEM((2, TILE, width), F32), pltpu.SemaphoreType.DMA((2,))],
        4,
        cost(4, 10 * total * width),
        distant=1,
    )


def products_of(me, refs, counts, products, slot, parts, aligned, store):
    for n, (l, r, begin, end) in enumerate(products):
        if aligned:
            size = refs[l].shape[1] // parts
            left = refs[l][:, pl.ds(pl.multiple_of((me ^ slot) * size, LANES), size)]
        else:
            left = refs[l][...]
        for c in range(begin, end, 512):
            stop = min(c + 512, end)
            store(n, c - begin, stop - begin, mm_tn(left, refs[counts + r][:, c:stop]))


def prepared(me, lefts, slot, parts):
    sizes = [v.shape[1] // parts for v in lefts]
    aligned = all(size % LANES == 0 for size in sizes)
    if not aligned:
        lefts = [
            lax.dynamic_slice_in_dim(v, (me[0] ^ slot) * size, size, axis=1) for v, size in zip(lefts, sizes)
        ]
    return lefts, sizes, aligned


def grads_cost(lefts, sizes, products):
    flops = sum(2 * lefts[l].shape[0] * sizes[l] * (end - begin) for l, r, begin, end in products)
    return cost(flops / 0.6e9, flops // 256)


def weight_grads(name, me, lefts, rights, products, slot, parts):
    lefts, sizes, aligned = prepared(me, lefts, slot, parts)
    given = len(lefts) + len(rights)

    def kernel(me_ref, *refs):
        def store(n, begin, end, value):
            refs[given + n][:, begin:end] = value.astype(BF)

        products_of(me_ref[0], refs, len(lefts), products, slot, parts, aligned, store)

    outs = [struct((sizes[l], end - begin), BF) for l, r, begin, end in products]
    return kernel_call(
        kernel, name, [SMEM] + [VMEM] * given, outs, [], 8, grads_cost(lefts, sizes, products)
    )(me, *lefts, *rights)


def split_grads(name, place, axis, lefts, rights, products, swapped, parts, outer, rows, sums=None):
    lefts, sizes, aligned = prepared(place, lefts, 0, parts)
    given = len(lefts) + len(rights)
    base = min(sizes)
    inner = base // (2 * outer)
    places, width = [], 0
    for l, r, begin, end in products:
        places.append(width)
        width += (end - begin) * (sizes[l] // base)
    count = len(products)
    extra = [] if sums is None else [sums]
    flat = [v for arrays in swapped for v in arrays]
    per = len(flat) // max(parts - 1, 1)

    def kernel(place_ref, *refs):
        others = refs[given : given + per * (parts - 1)]
        tail = refs[given + per * (parts - 1) :]
        send, kept = tail[len(extra) : len(extra) + 2]
        high_is_mine = place_ref[axis] == 1

        def store(n, begin, end, value):
            for k in range(parts - 1):
                block, at = (k * per + n, 0) if per == count else (k, places[n])
                value = value + others[block][:, at + begin : at + end].astype(F32)
            times = value.shape[0] // base
            value = value.reshape(outer, 2, inner // rows, times, rows, end - begin)
            for t in range(times):
                to = places[n] + t * (products[n][3] - products[n][2]) + begin
                low = value[:, 0, :, t].reshape(outer, inner, end - begin)
                high = value[:, 1, :, t].reshape(outer, inner, end - begin)
                send[:, :, to : to + end - begin] = jnp.where(high_is_mine, low, high).astype(BF)
                kept[:, :, to : to + end - begin] = jnp.where(high_is_mine, high, low)

        products_of(place_ref[0], refs, len(lefts), products, 0, parts, aligned, store)
        if extra:
            held = tail[-1]
            held[place_ref[0]] = tail[0][...]
            for k in range(1, parts):
                block = others[(k - 1) * per]
                held[place_ref[0] ^ k] = unpack(block[0:32, block.shape[1] - LANES :])
            value = held[0]
            for k in range(1, parts):
                value = value + held[k]
            columns = slice(width, width + LANES)
            send[:, :, columns] = jnp.zeros((outer, inner, LANES), BF)
            kept[:, :, columns] = jnp.zeros((outer, inner, LANES), F32)
            send[0, :, columns] = pack(value)
            kept[0, 0:8, columns] = value

    shape = (outer, inner, width + LANES * len(extra))
    return kernel_call(
        kernel,
        name,
        [SMEM] + [VMEM] * (given + len(flat) + len(extra)),
        [struct(shape, BF), struct(shape, F32)],
        [pltpu.VMEM((parts, 8, LANES), F32)] * len(extra),
        8,
        grads_cost(lefts, sizes, products),
    )(place, *lefts, *rights, *flat, *extra)


def middle_back(dims, ff):
    total, width, half, size = dims
    packed = width + 2 * ff

    def kernel(len_ref, d_left, d_right, middle, gains, low_ref, state, gate, forget, w, *refs):
        tables, cot_far, refs = refs[:4], refs[4], refs[5:]
        d_mid, d_middle, d_gate, local, prod, cot, hold, keep, carry, tile_sems = refs
        first = len_ref[0, 0]
        second = first + len_ref[0, 1]
        bound = low_ref[0:1, :]
        io = Streams(total, tile_sems, [(cot_far, cot)])
        io.start(backwards=True)
        ffn_gain = gains[2:3, :]
        gain = gains[1:2, :]

        def keeps(base, rows, value):
            time = slot_times(base, rows, total)
            start = (time == 0) | (time == first) | (time == second)
            return jnp.where(start, 0.0, bound + (1.0 - bound) * sigmoid(value))

        k = keeps(0, 8, forget[0:8, :])
        carry[0:16, :] = jnp.zeros((16, half), F32)
        carry[16:24, :] = jnp.ones((8, half), F32)
        carry[24:32, :] = jnp.concatenate([k[1:8, :], jnp.zeros((1, half), F32)], axis=0)

        def enter(base):
            block = pl.ds(base, TILE)
            hold[...] = mm_nt(d_left[block, :], w[:, width : width + ff]) + mm_nt(
                d_right[block, :], w[:, width + ff : packed]
            )
            io.wait(base)

            def norm_back(at, rows):
                here = pl.ds(at, rows)
                there = span(base + at, rows)
                valid = (slot_times(base + at, rows, total) < second).astype(F32)
                x = middle[there, :]
                scale = lax.rsqrt(jnp.mean(x * x, axis=-1, keepdims=True) + 1e-06)
                d = hold[here, :]
                unit = x * scale
                d = d * ffn_gain
                back = scale * (d - unit * jnp.mean(d * unit, axis=-1, keepdims=True))
                back = back + valid * cot[there, :]
                d_middle[there, :] = back
                d_mid[there, :] = back.astype(BF)

            chunks("norm_back", norm_back)

        def tile(base):
            enter(base)
            block = pl.ds(base, TILE)
            hold[...] = mm_nt(d_mid[block, :], w[:, 0:width])

            def through(at, rows):
                here = pl.ds(at, rows)
                there = span(base + at, rows)
                low = lax.broadcasted_iota(jnp.int32, (rows, LANES), 1) < LANES // 2
                re, im = state[there, 0:half], state[there, half:width]
                c, s = turned(tables, base + at, rows)
                mixed = strips(c * re - s * im) + strips(c * im + s * re)
                grouped, scales = centre_and_scale(mixed, low, size)
                back = []
                for n in range(len(grouped)):
                    lanes = slice(n * LANES, (n + 1) * LANES)
                    opened = sigmoid(gate[there, lanes].astype(F32))
                    d = hold[here, lanes]
                    part = d * grouped[n] * opened
                    d_gate[there, lanes] = (part * gain[:, lanes] * (1.0 - opened)).astype(BF)
                    back.append(d * opened * gain[:, lanes])
                mean = group_spread(group_means(back, low, size), low)
                along = group_spread(group_means([b * g for b, g in zip(back, grouped)], low, size), low)
                back = [t * (b - m - g * a) for t, b, m, g, a in zip(scales, back, mean, grouped, along)]
                for n in range(3):
                    lanes = slice(n * LANES, (n + 1) * LANES)
                    cn, sn = c[:, lanes], s[:, lanes]
                    local[there, lanes] = cn * back[n] + sn * back[n + 3]
                    local[there, half + n * LANES : half + (n + 1) * LANES] = cn * back[n + 3] - sn * back[n]

            chunks("through", through)

            def kept(at, rows):
                there = span(base + at, rows)
                keep[pl.ds(at, rows), :] = keeps(base + at, rows, forget[there, :])

            chunks("kept", kept)

            def scan(i, held):
                re, im, p, k = held
                at = (TILE // 8 - 1 - i) * 8
                there = span(base + at, 8)
                re = k * re + local[there, 0:half]
                im = k * im + local[there, half:width]
                p = k * p
                local[there, 0:half] = re
                local[there, half:width] = im
                prod[there, :] = p
                return re, im, p, keep[span(at, 8), :]

            held = (carry[0:8, :], carry[8:16, :], carry[16:24, :], carry[24:32, :])
            held = lax.fori_loop(0, TILE // 8, scan, held, unroll=8)
            carry[0:8, :], carry[8:16, :], carry[16:24, :], carry[24:32, :] = held

        tiles_of(total, tile, backwards=True)

    return kernel_call(
        kernel,
        "middle_back",
        [SMEM] + [VMEM] * 13 + [HBM],
        [
            struct((total, width), BF),
            struct((total, width), F32),
            struct((total, width), BF),
            struct((total, width), F32),
            struct((total, half), F32),
        ],
        [
            pltpu.VMEM((total, width), F32),
            pltpu.VMEM((TILE, width), F32),
            pltpu.VMEM((TILE, half), F32),
            pltpu.VMEM((32, half), F32),
            stream_sems(total, 1),
        ],
        8,
        cost(19, 60 * total * width),
    )


def source_back(dims, parts, me, lefts, d_mid, shares, fine):
    total, width, half, size = dims
    wide = 2 * width + half
    given, sizes, aligned = [], None, True
    for slot in range(1, parts):
        made, sizes, aligned = prepared(me, lefts, slot, parts)
        given.append(list(made))
    if aligned:
        given = [list(lefts)] * max(parts - 1, 0)
        flat = list(lefts)
    else:
        flat = [v for made in given for v in made]
    products = [p for share in shares for p in share]
    count = len(shares)
    owner, widths = [], []
    for n, share in enumerate(shares):
        widths.append(0)
        for l, r, begin, end in share:
            owner.append((n, widths[n]))
            widths[n] += end - begin
    widths[0] += LANES if fine else 0

    def kernel(len_ref, me_ref, local, prod, d_gate, low_ref, state, forget, inner, *refs):
        tables, refs = refs[:4], refs[4:]
        left_refs, d_mid_ref, refs = refs[: len(flat)], refs[len(flat)], refs[len(flat) + 1 :]
        d_proj, sums = refs[:2]
        slots, (ends, acc) = refs[2 : 2 + count * (parts - 1)], refs[2 + count * (parts - 1) :]
        first = len_ref[0, 0]
        second = first + len_ref[0, 1]
        bound = low_ref[0:1, :]
        acc[...] = jnp.zeros_like(acc)
        p = prod[0:8, :]
        for h in (0, 1):
            z = local[0:8, h * half : (h + 1) * half]
            made = [jnp.zeros((1, half), F32)]
            for c in range(CHAINS - 2, -1, -1):
                made.append(z[c + 1 : c + 2, :] + p[c + 1 : c + 2, :] * made[-1])
            ends[8 * h : 8 * h + 8, 0:half] = jnp.concatenate(made[::-1], axis=0)
        old = state[total - 8 : total, :]
        ends[16:24, :] = jnp.concatenate([old[7:8, :], old[0:7, :]], axis=0)

        def tile(base):
            def back(at, rows):
                row = base + at
                there = span(row, rows)
                p = prod[there, :]
                re = local[there, 0:half] + p * repeat(ends[0:8, 0:half], rows)
                im = local[there, half:width] + p * repeat(ends[8:16, 0:half], rows)
                up = span(jnp.maximum(row - 8, 0), 8)
                stay = pl.ds(pl.multiple_of(row, 8), rows - 8)
                old_re = jnp.concatenate(
                    [jnp.where(row == 0, ends[16:24, 0:half], state[up, 0:half]), state[stay, 0:half]], axis=0
                )
                old_im = jnp.concatenate(
                    [jnp.where(row == 0, ends[16:24, half:width], state[up, half:width]), state[stay, half:width]],
                    axis=0,
                )
                time = slot_times(row, rows, total)
                start = (time == 0) | (time == first) | (time == second)
                sf = sigmoid(forget[there, :])
                rest = (1.0 - bound) * (1.0 - sf)
                turn = (1.0 - rest) * (im * old_re - re * old_im)
                acc[8:16, :] += fold(jnp.where(start, 0.0, turn))
                d_lam = jnp.where(start, 0.0, re * old_re + im * old_im)
                c, s = turned(tables, row, rows)
                d_re = c * re - s * im
                d_im = c * im + s * re
                for lane, d in ((0, d_re), (half, d_im)):
                    v = inner[there, lane : lane + half].astype(F32)
                    sv = sigmoid(v)
                    d_lam = d_lam - d * (v * sv)
                    d_proj[there, lane : lane + half] = (rest * d * (sv * (1.0 + v * (1.0 - sv)))).astype(BF)
                acc[0:8, :] += fold(d_lam * (1.0 - sf))
                d_proj[there, 2 * width : wide] = (d_lam * rest * sf).astype(BF)
                d_proj[there, width : 2 * width] = d_gate[there, :]

            chunks("source_back", back)

        tiles_of(total, tile)
        out = [jnp.sum(acc[8 * n : 8 * n + 8, :], axis=0, keepdims=True) for n in range(2)]
        out = strips(out[0]) + strips(out[1])
        sums[...] = jnp.concatenate(out + [jnp.zeros((8 - len(out), LANES), F32)], axis=0)
        for slot in range(1, parts):
            used = left_refs if aligned else left_refs[(slot - 1) * len(lefts) : slot * len(lefts)]

            def store(n, begin, end, value):
                share, at = owner[n]
                slots[(slot - 1) * count + share][:, at + begin : at + end] = value.astype(BF)

            products_of(
                me_ref[0], [*used, d_proj, d_mid_ref], len(lefts), products, slot, parts, aligned, store
            )
            if fine:
                block = slots[(slot - 1) * count]
                rest = jnp.zeros((block.shape[0] - 24, LANES), F32)
                carried = jnp.concatenate([pack(sums[...]).astype(F32), rest], axis=0)
                block[:, block.shape[1] - LANES :] = carried.astype(BF)

    outs = [struct((total, wide), BF), struct((8, LANES), F32)]
    outs += [struct((width // parts, n), BF) for n in widths] * (parts - 1)
    call = kernel_call(
        kernel,
        "source_back",
        [SMEM, SMEM] + [VMEM] * (12 + len(flat)),
        outs,
        [pltpu.VMEM((24, width), F32), pltpu.VMEM((16, half), F32)],
        6,
        cost(10, 40 * total * width),
    )

    def run(lengths, me, *arrays):
        d_proj, sums, *slots = call(lengths, me, *arrays, *flat, d_mid)
        return d_proj, sums, [slots[k * count : (k + 1) * count] for k in range(parts - 1)]

    return run


def input_back(parts, cut, dims):
    total, width, half, size = dims
    wide = 2 * width + half

    def kernel(me_ref, d_proj, gains, d_middle, tok_far, *refs):
        left_pieces, right_pieces = refs[:parts], refs[parts : 2 * parts]
        out, w, tok, hold, sems, tile_sems = refs[2 * parts :]
        me = me_ref[0]
        copies = piece_copies(me, left_pieces, w, pl.ds(0, cut), sems, 0)
        copies += piece_copies(me, right_pieces, w, pl.ds(cut, w.shape[1] - cut), sems, parts)
        for c in copies:
            c.start()
        io = Streams(total, tile_sems, [(tok_far, tok)])
        io.start()
        gain = gains[0:1, :]
        for c in copies:
            c.wait()

        def tile(base):
            hold[...] = mm_nt(d_proj[pl.ds(base, TILE), :], w[:, 0:wide])
            io.wait(base)

            def norm_back(at, rows):
                here = pl.ds(at, rows)
                there = span(base + at, rows)
                x = tok[there, :]
                scale = lax.rsqrt(jnp.mean(x * x, axis=-1, keepdims=True) + 1e-06)
                d = hold[here, :]
                unit = x * scale
                d = d * gain
                out[there, :] = d_middle[there, :] + scale * (d - unit * jnp.mean(d * unit, axis=-1, keepdims=True))

            chunks("norm_back", norm_back)

        tiles_of(total, tile)

    return kernel_call(
        kernel,
        "input_back",
        [SMEM, VMEM, VMEM, VMEM] + [HBM] + [ANY] * (2 * parts),
        [struct((total, width), F32)],
        [
            pltpu.VMEM((width, wide + LANES), BF),
            pltpu.VMEM((total, width), F32),
            pltpu.VMEM((TILE, width), F32),
            pltpu.SemaphoreType.DMA((2 * parts,)),
            stream_sems(total, 1),
        ],
        10,
        cost(7, 20 * total * width),
    )


def order_call(place, held, cut):
    rows, columns = held[0].shape
    deep = len(held)

    def kernel(place_ref, *refs):
        for k in range(deep):
            at = place_ref[1] ^ k
            refs[deep][at] = refs[k][:, 0:cut]
            refs[deep + 1][at] = refs[k][:, cut:columns]

    outs = [struct((deep, rows, cut), BF), struct((deep, rows, columns - cut), BF)]
    return kernel_call(kernel, "order_z", [SMEM] + [VMEM] * deep, outs, [], 2, cost(1, 4 * deep * rows * columns))(
        place, *held
    )


def join_call(place, axes, own, got):
    count = len(own)

    def kernel(place_ref, *refs):
        for n in range(count):
            bit = place_ref[axes[n]]
            refs[2 * count + n][:, pl.ds(bit, 1)] = refs[n][...][:, None]
            refs[2 * count + n][:, pl.ds(1 - bit, 1)] = refs[count + n][...][:, None]

    outs = [struct((v.shape[0], 2) + v.shape[1:], BF) for v in own]
    moved = sum(8 * v.size for v in own)
    return kernel_call(kernel, "join", [SMEM] + [VMEM] * (2 * count), outs, [], 2, cost(2, moved))(place, *own, *got)


def halve_call(place, axes, kept, got, carried):
    count = len(kept)

    def kernel(place_ref, *refs):
        for n in range(count):
            bit = place_ref[axes[n]]
            for to, half in ((2 * count + 2 * n, 1 - bit), (2 * count + 2 * n + 1, bit)):
                value = refs[n][:, pl.ds(half, 1)] + refs[count + n][:, pl.ds(half, 1)].astype(F32)
                refs[to][...] = value[:, 0].astype(refs[to].dtype)
            if carried and n == 0:
                columns = slice(kept[0].shape[-1] - LANES, None)
                value = refs[0][0, 0, 0:8, columns] + unpack(refs[count][0, 0, :, columns])
                refs[2 * count][0, :, columns] = pack(value)
                refs[2 * count + 1][0, 0:8, columns] = value

    outs = []
    for v in kept:
        shape = v.shape[:1] + v.shape[2:]
        outs += [struct(shape, BF), struct(shape, F32)]
    moved = sum(10 * v.size for v in kept)
    made = kernel_call(kernel, "halve", [SMEM] + [VMEM] * (2 * count), outs, [], 4, cost(3, moved))(place, *kept, *got)
    return [made[2 * n : 2 * n + 2] for n in range(count)]


def deal_call(place, kept, got, carried):
    deep, rows = kept[0].shape[:2]
    widths = [v.shape[2] for v in kept]
    columns = sum(widths)
    widths[0] -= LANES if carried else 0

    def kernel(place_ref, *refs):
        begin = 0
        for n, width in enumerate(widths):
            for k in range(deep):
                at = place_ref[1] ^ k
                value = refs[n][at, :, 0:width] + refs[2 + n][at, :, 0:width].astype(F32)
                refs[4 + k][:, begin : begin + width] = value.astype(refs[4 + k].dtype)
            begin += width
        if carried:
            last = slice(widths[0], widths[0] + LANES)
            value = refs[0][0, 0:8, last] + unpack(refs[2][0, :, last])
            refs[4][:, begin:] = jnp.concatenate([value, jnp.zeros((rows - 8, LANES), F32)], axis=0)
            for k in range(1, deep):
                refs[4 + k][:, begin:] = pack(value)

    outs = [struct((rows, columns), F32 if k == 0 else BF) for k in range(deep)]
    return kernel_call(kernel, "deal_z", [SMEM] + [VMEM] * 4, outs, [], 4, cost(2, 10 * deep * rows * columns))(
        place, *kept, *got
    )


def finish_call(place, own, got, cuts, gains, carried):
    deep = len(got) + 1
    rows, columns = own.shape
    bounds = [0, *cuts, columns - (LANES if carried else 0)]
    pairs = list(zip(bounds[:-1], bounds[1:]))
    flat = [v for gain, weights in gains for v in (gain, *weights.values())]

    def kernel(place_ref, *refs):
        given = list(refs[deep : deep + len(flat)])
        outs = refs[deep + len(flat) :]
        for n, (a, b) in enumerate(pairs):
            value = refs[0][:, a:b]
            for k in range(1, deep):
                value = value + refs[k][:, a:b].astype(F32)
            outs[n][...] = value
        at = len(pairs)
        for gain, weights in gains:
            gain_ref = given.pop(0)
            total = jnp.zeros((rows, 1), F32)
            for n in weights:
                total = total + jnp.sum(given.pop(0)[...].astype(F32) * outs[n][...], axis=1, keepdims=True)
            shape = (rows, LANES)
            diagonal = lax.broadcasted_iota(jnp.int32, shape, 0) == lax.broadcasted_iota(jnp.int32, shape, 1)
            row = jnp.sum(jnp.where(diagonal, total, 0.0), axis=0, keepdims=True)
            outs[at][...] = (row[:, 0:rows] / gain_ref[...].astype(F32))[0]
            at += 1
        if carried:
            held = outs[-1]
            held[place_ref[1]] = refs[0][0:8, columns - LANES :]
            for k in range(1, deep):
                held[place_ref[1] ^ k] = unpack(refs[k][:, columns - LANES :])
            value = held[0]
            for k in range(1, deep):
                value = value + held[k]
            for n in range(2):
                strip = [value[3 * n + i : 3 * n + i + 1, :] for i in range(3)]
                outs[at + n][...] = jnp.concatenate(strip, axis=1)[0]

    outs = [struct((rows, b - a), F32) for a, b in pairs] + [struct((rows,), F32)] * len(gains)
    outs += [struct((3 * LANES,), F32)] * (2 * carried)
    scratch = [pltpu.VMEM((deep, 8, LANES), F32)] * carried
    return kernel_call(
        kernel, "finish", [SMEM] + [VMEM] * (deep + len(flat)), outs, scratch, 2, cost(2, 12 * rows * columns)
    )(place, own, *got, *flat)


class Exchange:
    def __init__(self, mesh, fine):
        self.parts = mesh.shape["dp"]
        self.count = mesh.shape["fsdp"]
        self.deep = self.count // 4
        me = lax.axis_index("fsdp")
        self.dp = lax.axis_index("dp")
        self.z = me // 4
        self.y_bit = (me // 2) % 2 == 1
        self.x_bit = me % 2 == 1
        self.fine = fine
        self.place = jnp.stack([self.dp, self.z, (me // 2) % 2, me % 2]).astype(jnp.int32)

    def swap(self, value, mask):
        return lax.ppermute(value, "fsdp", [(i, i ^ mask) for i in range(self.count)])

    def swap_dp(self, value, mask):
        return lax.ppermute(value, "dp", [(i, i ^ mask) for i in range(self.parts)])

    def send_z(self, shard, k):
        return self.swap(shard, 4 * k)

    def order_z(self, held, cut):
        if self.fine:
            return order_call(self.place, held, cut)
        step = 1
        while step < self.deep:
            bit = (self.z // step) % 2 == 1
            held = [jnp.where(bit, held[k ^ step], held[k]) for k in range(self.deep)]
            step *= 2
        stack = jnp.stack(held)
        return [stack[:, :, :cut], stack[:, :, cut:]]

    def send_first(self, shares):
        return [self.swap(shares[0], 1), self.swap(shares[1], 2)]

    def join_first(self, shares, got):
        if self.fine:
            return join_call(self.place, (3, 2), shares, got)
        out = []
        for own, other, bit in zip(shares, got, (self.x_bit, self.y_bit)):
            out.append(jnp.stack([jnp.where(bit, other, own), jnp.where(bit, own, other)], axis=1))
        return out

    def send_second(self, shares):
        return [self.swap(shares[0], 2), self.swap(shares[1], 1)]

    def join_second(self, shares, got):
        if self.fine:
            flat = [v.reshape((-1,) + v.shape[2:]) for v in (shares[1], got[1])]
            made = join_call(self.place, (2, 3), [shares[0], flat[0]], [got[0], flat[1]])
            return [v.reshape(-1, v.shape[-1]) for v in made]
        out = []
        for own, other, bit, place in zip(shares, got, (self.y_bit, self.x_bit), (1, 2)):
            v = jnp.stack([jnp.where(bit, other, own), jnp.where(bit, own, other)], axis=place)
            out.append(v.reshape(-1, v.shape[-1]))
        return out

    def gather_dp(self, shares):
        return [[v] + [self.swap_dp(v, k) for k in range(1, self.parts)] for v in shares]

    def cut_rows(self, own, swapped, outer, bit, rows):
        columns = []
        for n, value in enumerate(own):
            value = value.astype(F32)
            for arrays in swapped:
                value = value + arrays[n].astype(F32)
            value = value.reshape(self.count, -1, rows, value.shape[1])
            columns += [value[:, i] for i in range(value.shape[1])]
        total = jnp.concatenate(columns, axis=-1)
        total = total.reshape(outer, 2, -1, total.shape[-1])
        low, high = total[:, 0], total[:, 1]
        return jnp.where(bit, low, high).astype(BF), jnp.where(bit, high, low)

    def halves(self, total, bit):
        low, high = total[:, 0], total[:, 1]
        return jnp.where(bit, low, high).astype(BF), jnp.where(bit, high, low)

    def halve(self, kept, got, carried=False):
        kept = [v.reshape(self.deep, 2, -1, v.shape[-1]) for v in kept]
        got = [g.reshape(k.shape) for g, k in zip(got, kept)]
        if self.fine:
            return halve_call(self.place, (2, 3), kept, got, carried)
        return [self.halves(k + g.astype(F32), bit) for k, g, bit in zip(kept, got, (self.y_bit, self.x_bit))]

    def send_halves(self, cuts):
        return [c[1] for c in cuts], [self.swap(cuts[0][0], 2), self.swap(cuts[1][0], 1)]

    def deal_z(self, kept, got, carried=False):
        if self.fine:
            own, *others = deal_call(self.place, kept, got, carried)
            return own, others
        total = jnp.concatenate([k + g.astype(F32) for k, g in zip(kept, got)], axis=-1)
        own, *others = [lax.dynamic_index_in_dim(total, self.z ^ k, 0, keepdims=False) for k in range(self.deep)]
        return own, [v.astype(BF) for v in others]

    def send_parts(self, others):
        return [self.swap(v, 4 * k) for k, v in enumerate(others, 1)]

    def finish_z(self, own, got, cuts, gains, carried=False):
        if self.fine:
            return finish_call(self.place, own, got, cuts, gains, carried)
        for v in got:
            own = own + v.astype(F32)
        made = jnp.split(own, cuts, axis=1)
        for gain, weights in gains:
            total = sum(jnp.sum(w.astype(F32) * made[n], axis=1) for n, w in weights.items())
            made.append(total / gain[0].astype(F32))
        return made

    def total(self, value):
        for k in range(self.parts.bit_length() - 1):
            value = value + self.swap_dp(value, 1 << k)
        for k in range(self.count.bit_length() - 1):
            value = value + self.swap(value, 1 << k)
        return value


def after(value, *others):
    return lax.optimization_barrier((value, *others))[0]


def to_chains(value):
    rows, columns = value.shape
    length = rows // CHAINS
    parts = range(columns // LANES)

    def kernel(source, out, natural, kept, sems):
        arriving = [
            pltpu.make_async_copy(source.at[:, pl.ds(n * LANES, LANES)], natural.at[n], sems.at[0, n]) for n in parts
        ]
        leaving = [
            pltpu.make_async_copy(kept.at[n], out.at[:, pl.ds(n * LANES, LANES)], sems.at[1, n]) for n in parts
        ]
        for c in arriving:
            c.start()
        for n in parts:
            arriving[n].wait()

            def move(j, carry):
                kept[n, span(j * CHAINS, CHAINS), :] = natural[n, pl.ds(j, CHAINS, stride=length), :]
                return carry

            lax.fori_loop(0, length, move, 0, unroll=16)
            leaving[n].start()
        for c in leaving:
            c.wait()

    place = pltpu.VMEM((columns // LANES, rows, LANES), F32)
    (made,) = kernel_call(
        kernel,
        "to_chains",
        [HBM],
        [struct((rows, columns), F32)],
        [place, place, pltpu.SemaphoreType.DMA((2, columns // LANES))],
        8,
        cost(4, 8 * rows * columns),
        distant=1,
    )(*far(value))
    return made


def from_chains(value):
    rows, columns = value.shape
    return value.reshape(rows // CHAINS, CHAINS, columns).transpose(1, 0, 2).reshape(rows, columns)


def turns(phase, rows):
    length = rows // CHAINS
    inside = jnp.arange(length, dtype=F32)[:, None] * phase
    outside = (jnp.arange(CHAINS, dtype=F32) * length)[:, None] * phase
    return [jnp.cos(inside), jnp.sin(inside), jnp.cos(outside), jnp.sin(outside)]


def build(mesh):
    def per_device(
        tokens,
        lengths,
        w_input,
        w_forget,
        w_gate,
        w_output,
        w_up_gate,
        w_up,
        w_down,
        norm_gain,
        group_gain,
        ffn_gain,
        lower_bound,
        phase,
        cotangent,
    ):
        ex = Exchange(mesh, w_input.shape[0] % 24 == 0)
        parts = ex.parts
        total, width = tokens.shape
        half = lower_bound.shape[0]
        ff = w_up.shape[1]
        dims = (total, width, half, width // GROUPS)
        shard = w_input.shape[0]

        columns = jnp.stack([norm_gain, group_gain, ffn_gain], axis=1)
        columns = jnp.pad(columns, ((0, 0), (0, LANES - 3)))
        pack1 = jnp.concatenate([w_input, w_gate, w_forget, columns], axis=1)
        pack1, tokens, rest = after((pack1, tokens, [w_output, w_up_gate, w_up]))
        pack2 = jnp.concatenate(rest, axis=1)
        cut1, cut2, cut3 = pack1.shape[1] // 2, pack2.shape[1] // 2, width // 2

        others = range(1, ex.deep)
        one = [pack1] + [ex.send_z(pack1, k) for k in others]
        one, pack2, ex.place, tokens = after((one, pack2, ex.place, tokens))
        tok = to_chains(tokens)
        one = ex.order_z(one, cut1)
        got = ex.send_first(one)
        two = [pack2] + [ex.send_z(pack2, k) for k in others[:2]]
        one, got, two, tok, phase, lower_bound = after((one, got, two, tok, phase, lower_bound))
        tables = turns(phase, total)
        low = jnp.broadcast_to(lower_bound, (8, half))
        one = ex.join_first(one, got)
        got = ex.send_second(one)
        two += [ex.send_z(two[0], k) for k in others[2:]]
        one, got, two, tables, low = after((one, got, two, tables, low))
        one = ex.gather_dp(ex.join_second(one, got))
        two = ex.order_z(two, cut2)
        got = ex.send_first(two)
        (tok,) = far(tok)
        inner, gate, forget, gains, normed, inner_low, gate_low = recurrent_project(parts, cut1, dims)(
            ex.place, tok, *one[0], *one[1]
        )
        two, got, gains, w_down, cotangent = after((two, got, gains, w_down, cotangent))
        cot = to_chains(cotangent)
        two = ex.join_first(two, got)
        got = ex.send_second(two)
        three = [w_down] + [ex.send_z(w_down, k) for k in others]
        gated, state = recurrent_mix(dims)(lengths, inner, gate, forget, gains, low, *tables)
        three, gated = after((three, gated))
        three = ex.order_z(three, cut3)
        late = ex.send_first(three)
        two, got, three, late, gated, cot = after((two, got, three, late, gated, cot))
        two = ex.gather_dp(ex.join_second(two, got))
        three = ex.join_first(three, late)
        late = ex.send_second(three)
        (cot,) = far(cot)
        middle, ffn_in, to_left, to_right, hidden, w_two = ffn_up(parts, cut2, dims, ff)(
            ex.place, gated, gains, tok, *two[0], *two[1]
        )
        three, late, ffn_in = after((three, late, ffn_in))
        three = ex.gather_dp(ex.join_second(three, late))
        grad, d_left, d_right, w_three = ffn_turn(parts, cut3, dims, ff)(
            lengths, ex.place, to_left, to_right, cot, *three[0], *three[1]
        )

        fold_rows = ff // width

        def last_grads(name, n, turn, lefts, rights, products, swapped, sums=None):
            outer, bit = ((2 * ex.deep, ex.x_bit), (ex.deep, ex.y_bit))[n]
            if ex.fine:
                return split_grads(
                    name, turn[0], 3 - n, lefts, rights, products, swapped, parts, outer, shard, sums
                )
            made = weight_grads(name, turn[0], lefts, rights, products, 0, parts)
            return ex.cut_rows(made, swapped, outer, bit, shard)

        given = (
            [hidden, ffn_in],
            [grad, d_left, d_right],
            [[(1, 1, 0, ff), (0, 0, 0, cut3)], [(1, 2, 0, ff), (0, 0, cut3, width)]],
        )
        swapped, turn = [], (ex.place, lengths)
        for products in given[2]:
            arrays = []
            for k in range(1, parts):
                made = weight_grads("ffn_grads", turn[0], given[0], given[1], products, k, parts)
                made, turn = after((made, turn))
                arrays.append([ex.swap_dp(v, k) for v in made])
            swapped.append(arrays)
        (act,) = ffn_out(dims, ff)(turn[1], hidden, middle, w_three)
        act, turn = after((act, turn))
        kept, got = [], []
        for n in range(2):
            send, keep = last_grads("ffn_grads", n, turn, given[0], given[1], given[2][n], swapped[n])
            send, keep, turn = after((send, keep, turn))
            kept.append(keep)
            got.append(ex.swap(send, n + 1))
        d_mid, d_middle, d_gate, local, prod = middle_back(dims, ff)(
            turn[1], d_left, d_right, middle, gains, low, state, gate_low, forget, w_two, *tables, cot
        )
        wide = 2 * width + half
        shares = [[(0, 0, 0, width), (0, 0, 2 * width, wide)], [(0, 0, 0, width), (1, 1, 0, width)]]
        local, turn = after((local, turn))
        swapped_b = []
        for k in range(1, parts):
            made = weight_grads("recurrent_grads", turn[0], [normed, gated], [d_gate, d_mid], shares[1], k, parts)
            made, turn = after((made, turn))
            swapped_b.append([ex.swap_dp(v, k) for v in made])
        kept, got, swapped_b, turn = after((kept, got, swapped_b, turn))
        cuts, turn = after((ex.halve(kept, got), turn))
        kept, got = ex.send_halves(cuts)
        send_b, kept_b = last_grads(
            "recurrent_grads", 1, turn, [normed, gated], [d_gate, d_mid], shares[1], swapped_b
        )
        send_b, kept_b, turn = after((send_b, kept_b, turn))
        d_proj, sums, made = source_back(dims, parts, ex.place, [normed], d_mid, shares[:1], ex.fine)(
            turn[1], turn[0], local, prod, d_gate, low, state, forget, inner_low, *tables
        )
        made, kept, got, sums, send_b, turn = after((made, kept, got, sums, send_b, turn))
        swapped_a = []
        for k, (v,) in enumerate(made, 1):
            v = ex.swap_dp(v, k)
            swapped_a.append([v] if ex.fine else [v[:, :width], v[:, width:]])
        ffn, others = ex.deal_z(kept, got)
        ffn, others, send_b, turn = after((ffn, others, send_b, turn))
        ffn_got = ex.send_parts(others)
        got_b = ex.swap(send_b, 2)
        send_a, kept_a = last_grads(
            "recurrent_grads", 0, turn, [normed], [d_proj], shares[0], swapped_a, sums if ex.fine else None
        )
        send_a, kept_a, turn = after((send_a, kept_a, turn))
        got_a = ex.swap(send_a, 1)
        kept, got = [kept_a, kept_b], [got_a, got_b]
        (input_grad,) = input_back(parts, cut1, dims)(
            turn[0], d_proj, gains, d_middle, tok, *one[0], *one[1]
        )
        input_grad, act = after((input_grad, act))
        act = from_chains(act)
        input_grad, ffn_got, kept, got, act = after((input_grad, ffn_got, kept, got, act))
        kept, got = ex.send_halves(ex.halve(kept, got, ex.fine))
        middle_at = ff + fold_rows * cut3
        bounds = [ff, middle_at, middle_at + ff]
        grad_up_gate, down_a, grad_up, down_b, grad_ffn_gain = ex.finish_z(
            ffn, ffn_got, bounds, [(ffn_gain[None], {0: w_up_gate, 2: w_up})]
        )
        kept, got, input_grad = after((kept, got, input_grad))
        rest, others = ex.deal_z(kept, got, ex.fine)
        rest, others, input_grad = after((rest, others, input_grad))
        got = ex.send_parts(others)
        input_grad = from_chains(input_grad)
        if not ex.fine:
            sums = ex.total(sums)
        norm_weights = {0: w_input, 1: w_forget, 2: w_gate}
        made = ex.finish_z(
            rest,
            got,
            [width, width + half, wide],
            [(norm_gain[None], norm_weights), (group_gain[None], {3: w_output})],
            ex.fine,
        )
        grad_input, grad_forget, grad_gate, grad_output, grad_norm_gain, grad_group_gain = made[:6]
        if ex.fine:
            grad_lower, grad_phase = made[6:]
        else:
            ahead = half // LANES
            grad_lower, grad_phase = sums[0:ahead].reshape(half), sums[ahead : 2 * ahead].reshape(half)

        halves = []
        for i in range(fold_rows):
            left_half = down_a[:, i * cut3 : (i + 1) * cut3]
            right_half = down_b[:, i * (width - cut3) : (i + 1) * (width - cut3)]
            halves.append(jnp.concatenate([left_half, right_half], axis=1))
        grad_down = jnp.concatenate(halves, axis=0)
        return (
            act,
            input_grad,
            grad_input,
            grad_forget,
            grad_gate,
            grad_output,
            grad_up_gate,
            grad_up,
            grad_down,
            grad_norm_gain,
            grad_group_gain,
            grad_ffn_gain,
            grad_lower,
            grad_phase,
        )

    return per_device


def solution(mesh):
    rows = P(("dp", "fsdp"), None)
    vec = P(("dp", "fsdp"))
    in_specs = (rows,) * 9 + (vec,) * 3 + (P(), P(), rows)
    out_specs = (rows,) * 9 + (vec,) * 3 + (P(), P())
    return jax.shard_map(build(mesh), mesh=mesh, in_specs=in_specs, out_specs=out_specs, check_vma=False)
```

```python
import jax
import jax.numpy as jnp
from jax import lax
from jax.experimental import pallas as pl
from jax.experimental.pallas import tpu as pltpu
from jax.sharding import PartitionSpec as P

GROUPS = 4
LANES = 128
CHAINS = 8
TILE = 256
BF = jnp.bfloat16
F32 = jnp.float32
TN = (((0,), (0,)), ((), ()))
NT = (((1,), (1,)), ((), ()))


def mm(left, right):
    return jnp.dot(left, right, preferred_element_type=F32)


def mm_nt(left, right):
    return lax.dot_general(left, right, NT, preferred_element_type=F32)


def mm_tn(left, right):
    return lax.dot_general(left, right, TN, preferred_element_type=F32)


def sigmoid(v):
    return 0.5 * jnp.tanh(0.5 * v) + 0.5


STEPS = {
    "norm": (256, 1),
    "sources": (64, 4),
    "mix": (64, 2),
    "finish": (256, 1),
    "norm_back": (256, 1),
    "through": (64, 4),
    "kept": (256, 1),
    "source_back": (64, 1),
}


def chunks(name, body):
    rows, unroll = STEPS[name]

    def step(i, carry):
        body(pl.multiple_of(i * rows, rows), rows)
        return carry

    lax.fori_loop(0, TILE // rows, step, 0, unroll=unroll)


def tiles_of(total, body, backwards=False):
    count = total // TILE

    def step(i, carry):
        body(pl.multiple_of(((count - 1 - i) if backwards else i) * TILE, TILE))
        return carry

    lax.fori_loop(0, count, step, 0)


def span(at, rows):
    return pl.ds(pl.multiple_of(at, rows), rows)


def repeat(value, rows):
    return jnp.concatenate([value] * (rows // 8), axis=0)


def fold(value):
    return jnp.sum(value.reshape(value.shape[0] // 8, 8, value.shape[1]), axis=0)


def cost(micros, moved):
    return pl.CostEstimate(flops=int(micros * 1.15e8), bytes_accessed=moved // 10, transcendentals=0)


def slot_times(base, rows, total):
    row = base + lax.broadcasted_iota(jnp.int32, (rows, 1), 0)
    return (row % CHAINS) * (total // CHAINS) + row // CHAINS


def turned(tables, base, rows):
    ci, si, co, so = tables
    inside = span(base // CHAINS, rows // CHAINS)
    half = ci.shape[1]
    c, s = ci[inside, :][:, None, :], si[inside, :][:, None, :]
    oc, os = co[...][None], so[...][None]
    return (c * oc - s * os).reshape(rows, half), (s * oc + c * os).reshape(rows, half)


def strips(value):
    return [value[:, i * LANES : (i + 1) * LANES] for i in range(value.shape[1] // LANES)]


def group_means(parts, low, size):
    zero = jnp.zeros_like(parts[0])
    sums = []
    for h in (0, 3):
        sums.append(parts[h] + jnp.where(low, parts[h + 1], zero))
        sums.append(jnp.where(low, zero, parts[h + 1]) + parts[h + 2])
    return [jnp.sum(s, axis=-1, keepdims=True) * (1.0 / size) for s in sums]


def group_spread(values, low):
    out = []
    for h in (0, 2):
        out += [values[h], jnp.where(low, values[h], values[h + 1]), values[h + 1]]
    return out


def pack(value):
    high = value.astype(BF).astype(F32)
    middle = (value - high).astype(BF).astype(F32)
    return jnp.concatenate([high, middle, value - high - middle], axis=0).astype(BF)


def unpack(value):
    value = value.astype(F32)
    return value[0:8, :] + value[8:16, :] + value[16:24, :]


def centre_and_scale(parts, low, size):
    means = group_spread(group_means(parts, low, size), low)
    parts = [p - m for p, m in zip(parts, means)]
    variances = group_means([p * p for p in parts], low, size)
    scales = group_spread([lax.rsqrt(v + 1e-05) for v in variances], low)
    return [p * s for p, s in zip(parts, scales)], scales


def piece_copies(me, pieces, target, columns, sems, first):
    rows = pieces[0].shape[0]
    out = []
    for k, piece in enumerate(pieces):
        at = pl.multiple_of((me ^ k) * rows, 16)
        out.append(pltpu.make_async_copy(piece, target.at[pl.ds(at, rows), columns], sems.at[first + k]))
    return out


HBM = pl.BlockSpec(memory_space=pltpu.HBM)
ANY = pl.BlockSpec(memory_space=pl.ANY)
SMEM = pl.BlockSpec(memory_space=pltpu.SMEM)


def struct(shape, dtype):
    return jax.ShapeDtypeStruct(shape, dtype)


VMEM = pl.BlockSpec(memory_space=pltpu.VMEM)


def far(*arrays):
    return [pltpu.with_memory_space_constraint(v, pltpu.HBM) for v in arrays]


def kernel_call(body, name, ins, outs, scratch, room, estimate, distant=0):
    near = len(outs) - distant
    outs = outs[:near] + [pltpu.HBM(v.shape, v.dtype) for v in outs[near:]]
    return pl.pallas_call(
        body,
        in_specs=ins,
        out_specs=[VMEM] * near + [HBM] * distant,
        out_shape=outs,
        scratch_shapes=scratch,
        compiler_params=pltpu.CompilerParams(vmem_limit_bytes=room * 2**20),
        cost_estimate=estimate,
        name=name,
    )


class Streams:
    def __init__(self, total, sems, arrived=(), leaving=()):
        self.bases = range(0, total, TILE)
        self.sems = sems
        self.arriving = [(far_ref, near_ref) for far_ref, near_ref in arrived]
        self.leaving = [(near_ref, far_ref) for near_ref, far_ref in leaving]

    def copies(self, base, pairs, first):
        block = pl.ds(base, TILE)
        return [
            pltpu.make_async_copy(a.at[block, :], b.at[block, :], self.sems.at[first + n, base // TILE])
            for n, (a, b) in enumerate(pairs)
        ]

    def start(self, backwards=False):
        for base in reversed(self.bases) if backwards else self.bases:
            for c in self.copies(base, self.arriving, 0):
                c.start()

    def wait(self, base):
        for c in self.copies(base, self.arriving, 0):
            c.wait()

    def leave(self, base):
        for c in self.copies(base, self.leaving, len(self.arriving)):
            c.start()

    def finish(self):
        for base in self.bases:
            for c in self.copies(base, self.leaving, len(self.arriving)):
                c.wait()


def stream_sems(total, count):
    return pltpu.SemaphoreType.DMA((count, total // TILE))


def recurrent_project(parts, cut, dims):
    total, width, half, size = dims
    wide = 2 * width + half
    packed = wide + LANES

    def kernel(place_ref, tok_far, *refs):
        left_pieces, right_pieces = refs[:parts], refs[parts : 2 * parts]
        inner, gate, forget, gains, normed, inner_low, gate_low, w, tok, sems, tile_sems = refs[2 * parts :]
        me = place_ref[0]
        small = [v.at[:, pl.ds(wide - cut, LANES)] for v in right_pieces]
        large = [v.at[:, pl.ds(0, wide - cut)] for v in right_pieces]
        ahead = piece_copies(me, small, w, pl.ds(wide, LANES), sems, 0)
        behind = piece_copies(me, left_pieces, w, pl.ds(0, cut), sems, parts)
        behind += piece_copies(me, large, w, pl.ds(cut, wide - cut), sems, 2 * parts)
        io = Streams(total, tile_sems, [(tok_far, tok)])
        for c in ahead:
            c.start()
        io.start()
        for c in behind:
            c.start()
        for c in ahead:
            c.wait()
        gains[...] = jnp.transpose(w[:, wide:packed].astype(F32))[0:8, :]

        def project(base):
            block = pl.ds(base, TILE)
            io.wait(base)
            gain = gains[0:1, :]

            def norm(at, rows):
                there = span(base + at, rows)
                x = tok[there, :]
                scale = lax.rsqrt(jnp.mean(x * x, axis=-1, keepdims=True) + 1e-06)
                normed[there, :] = (x * scale * gain).astype(BF)

            chunks("norm", norm)

            @pl.when(base == 0)
            def _():
                for c in behind:
                    c.wait()

            value = normed[block, :]
            for n in range(0, width, 256):
                lanes = slice(n, n + 256)
                made = mm(value, w[:, n : n + 256])
                inner[block, lanes] = made
                inner_low[block, lanes] = made.astype(BF)
                made = mm(value, w[:, width + n : width + n + 256])
                gate[block, lanes] = made
                gate_low[block, lanes] = made.astype(BF)
            forget[block, :] = mm(value, w[:, 2 * width : wide])

        tiles_of(total, project)

    return kernel_call(
        kernel,
        "recurrent_project",
        [SMEM] + [HBM] + [ANY] * (2 * parts),
        [
            struct((total, width), F32),
            struct((total, width), F32),
            struct((total, half), F32),
            struct((8, width), F32),
            struct((total, width), BF),
            struct((total, width), BF),
            struct((total, width), BF),
        ],
        [
            pltpu.VMEM((width, packed), BF),
            pltpu.VMEM((total, width), F32),
            pltpu.SemaphoreType.DMA((3 * parts,)),
            stream_sems(total, 1),
        ],
        10,
        cost(6, 24 * total * width),
    )


def recurrent_mix(dims):
    total, width, half, size = dims

    def kernel(len_ref, inner, gate, forget, gains, low_ref, *refs):
        tables, (gated, state, prod, keep, carry, ends) = refs[:4], refs[4:]
        first = len_ref[0, 0]
        second = first + len_ref[0, 1]
        carry[...] = jnp.concatenate([jnp.zeros((16, half), F32), jnp.ones((8, half), F32)], axis=0)
        bound = low_ref[0:1, :]

        def chain_tile(base):
            def sources(at, rows):
                here = pl.ds(at, rows)
                there = span(base + at, rows)
                time = slot_times(base + at, rows, total)
                start = (time == 0) | (time == first) | (time == second)
                rest = (1.0 - bound) * (1.0 - sigmoid(forget[there, :]))
                keep[here, :] = jnp.where(start, 0.0, 1.0 - rest)
                re = inner[there, 0:half]
                im = inner[there, half:width]
                re = rest * re * sigmoid(re)
                im = rest * im * sigmoid(im)
                c, s = turned(tables, base + at, rows)
                state[there, 0:half] = c * re + s * im
                state[there, half:width] = c * im - s * re

            chunks("sources", sources)

            def scan(j, held):
                re, im, p = held
                there = span(base + j * 8, 8)
                k = keep[span(j * 8, 8), :]
                re = k * re + state[there, 0:half]
                im = k * im + state[there, half:width]
                p = k * p
                state[there, 0:half] = re
                state[there, half:width] = im
                prod[there, :] = p
                return re, im, p

            held = (carry[0:8, :], carry[8:16, :], carry[16:24, :])
            held = lax.fori_loop(0, TILE // 8, scan, held, unroll=8)
            carry[0:8, :], carry[8:16, :], carry[16:24, :] = held

        tiles_of(total, chain_tile)
        p = carry[16:24, :]
        for h in (0, 8):
            z = carry[h : h + 8, :]
            rows = [jnp.zeros((1, half), F32)]
            for c in range(1, CHAINS):
                rows.append(z[c - 1 : c, :] + p[c - 1 : c, :] * rows[-1])
            ends[h : h + 8, :] = jnp.concatenate(rows, axis=0)
        gain = gains[1:2, :]

        def mix_tile(base):
            def mix(at, rows):
                there = span(base + at, rows)
                low = lax.broadcasted_iota(jnp.int32, (rows, LANES), 1) < LANES // 2
                p = prod[there, :]
                re = state[there, 0:half] + p * repeat(ends[0:8, :], rows)
                im = state[there, half:width] + p * repeat(ends[8:16, :], rows)
                state[there, 0:half] = re
                state[there, half:width] = im
                c, s = turned(tables, base + at, rows)
                mixed = strips(c * re - s * im) + strips(c * im + s * re)
                grouped, _ = centre_and_scale(mixed, low, size)
                for n in range(len(grouped)):
                    lanes = slice(n * LANES, (n + 1) * LANES)
                    opened = grouped[n] * gain[:, lanes] * sigmoid(gate[there, lanes])
                    gated[there, lanes] = opened.astype(BF)

            chunks("mix", mix)

        tiles_of(total, mix_tile)

    return kernel_call(
        kernel,
        "recurrent_mix",
        [SMEM] + [VMEM] * 9,
        [struct((total, width), BF), struct((total, width), F32)],
        [
            pltpu.VMEM((total, half), F32),
            pltpu.VMEM((TILE, half), F32),
            pltpu.VMEM((24, half), F32),
            pltpu.VMEM((16, half), F32),
        ],
        5,
        cost(8, 20 * total * width),
    )


def ffn_up(parts, cut, dims, ff):
    total, width, half, size = dims
    packed = width + 2 * ff

    def kernel(me_ref, gated, gains, tok_far, *refs):
        left_pieces, right_pieces = refs[:parts], refs[parts : 2 * parts]
        middle, ffn_in, to_left, to_right, hidden, w, middle_far, hidden_far, tok, sems, tile_sems = refs[2 * parts :]
        me = me_ref[0]
        first = [v.at[:, pl.ds(0, width)] for v in left_pieces]
        then = [v.at[:, pl.ds(width, cut - width)] for v in left_pieces]
        ahead = piece_copies(me, first, w, pl.ds(0, width), sems, 0)
        behind = piece_copies(me, then, w, pl.ds(width, cut - width), sems, parts)
        behind += piece_copies(me, right_pieces, w, pl.ds(cut, packed - cut), sems, 2 * parts)
        for c in ahead:
            c.start()
        io = Streams(total, tile_sems, [(tok_far, tok)], [(middle, middle_far), (hidden, hidden_far)])
        io.start()
        for c in behind:
            c.start()
        gain = gains[2:3, :]
        for c in ahead:
            c.wait()

        def enter(base):
            block = pl.ds(base, TILE)
            io.wait(base)
            middle[block, :] = tok[block, :] + mm(gated[block, :], w[:, 0:width])

            def norm(at, rows):
                there = span(base + at, rows)
                x = middle[there, :]
                scale = lax.rsqrt(jnp.mean(x * x, axis=-1, keepdims=True) + 1e-06)
                ffn_in[there, :] = (x * scale * gain).astype(BF)

            chunks("norm", norm)

        tiles_of(total, enter)
        for c in behind:
            c.wait()

        def expand(base):
            block = pl.ds(base, TILE)
            value = ffn_in[block, :]
            for c in range(0, ff, 256):
                lanes = slice(c, c + 256)
                l = mm(value, w[:, width + c : width + c + 256])
                r = mm(value, w[:, width + ff + c : width + ff + c + 256])
                g = sigmoid(l)
                u = l * g
                to_right[block, lanes] = u.astype(BF)
                to_left[block, lanes] = ((g + u - u * g) * r).astype(BF)
                hidden[block, lanes] = (u * r).astype(BF)
            io.leave(base)

        tiles_of(total, expand)
        io.finish()

    return kernel_call(
        kernel,
        "ffn_up",
        [SMEM, VMEM, VMEM] + [HBM] + [ANY] * (2 * parts),
        [
            struct((total, width), F32),
            struct((total, width), BF),
            struct((total, ff), BF),
            struct((total, ff), BF),
            struct((total, ff), BF),
            struct((width, packed), BF),
            struct((total, width), F32),
            struct((total, ff), BF),
        ],
        [
            pltpu.VMEM((total, width), F32),
            pltpu.SemaphoreType.DMA((3 * parts,)),
            stream_sems(total, 3),
        ],
        6,
        cost(10, 24 * total * width),
        distant=2,
    )


def ffn_turn(parts, cut, dims, ff):
    total, width, half, size = dims

    def kernel(me_ref, grad, to_left, to_right, *refs):
        left_pieces, right_pieces = refs[:parts], refs[parts : 2 * parts]
        d_left, d_right, w_far, w, sems = refs[2 * parts :]
        me = me_ref[0]
        copies = piece_copies(me, left_pieces, w, pl.ds(0, cut), sems, 0)
        copies += piece_copies(me, right_pieces, w, pl.ds(cut, width - cut), sems, parts)
        for c in copies:
            c.start()
        for c in copies:
            c.wait()
        out = pltpu.make_async_copy(w, w_far, sems.at[2 * parts])
        out.start()

        def turn(base):
            block = pl.ds(base, TILE)
            value = grad[block, :]
            for c in range(0, ff, 256):
                lanes = slice(c, c + 256)
                dh = mm_nt(value, w[c : c + 256, :])
                d_right[block, lanes] = (dh * to_right[block, lanes].astype(F32)).astype(BF)
                d_left[block, lanes] = (dh * to_left[block, lanes].astype(F32)).astype(BF)

        tiles_of(total, turn)
        out.wait()

    return kernel_call(
        kernel,
        "ffn_turn",
        [SMEM] + [VMEM] * 3 + [ANY] * (2 * parts),
        [struct((total, ff), BF), struct((total, ff), BF), struct((ff, width), BF)],
        [pltpu.VMEM((ff, width), BF), pltpu.SemaphoreType.DMA((2 * parts + 1,))],
        5,
        cost(5, 20 * total * width),
        distant=1,
    )


def ffn_out(dims, ff):
    total, width, half, size = dims

    def kernel(len_ref, hidden_far, middle_far, w_far, act_far, hidden, middle, w, act, sem, tile_sems):
        second = len_ref[0, 0] + len_ref[0, 1]
        io = Streams(total, tile_sems, [(hidden_far, hidden), (middle_far, middle)], [(act, act_far)])
        weight = pltpu.make_async_copy(w_far, w, sem.at[0])
        weight.start()
        io.start()
        weight.wait()

        def tile(base):
            block = pl.ds(base, TILE)
            io.wait(base)
            valid = (slot_times(base, TILE, total) < second).astype(F32)
            act[block, :] = valid * (middle[block, :] + mm(hidden[block, :], w[...]))
            io.leave(base)

        tiles_of(total, tile)
        io.finish()

    return kernel_call(
        kernel,
        "ffn_out",
        [SMEM] + [HBM] * 3,
        [struct((total, width), F32)],
        [
            pltpu.VMEM((total, ff), BF),
            pltpu.VMEM((total, width), F32),
            pltpu.VMEM((ff, width), BF),
            pltpu.VMEM((total, width), F32),
            pltpu.SemaphoreType.DMA((1,)),
            stream_sems(total, 3),
        ],
        15,
        cost(6, 10 * total * width),
        distant=1,
    )


def products_of(me, refs, counts, products, slot, parts, aligned, store):
    for n, (l, r, begin, end) in enumerate(products):
        if aligned:
            size = refs[l].shape[1] // parts
            left = refs[l][:, pl.ds(pl.multiple_of((me ^ slot) * size, LANES), size)]
        else:
            left = refs[l][...]
        for c in range(begin, end, 512):
            stop = min(c + 512, end)
            store(n, c - begin, stop - begin, mm_tn(left, refs[counts + r][:, c:stop]))


def prepared(me, lefts, slot, parts):
    sizes = [v.shape[1] // parts for v in lefts]
    aligned = all(size % LANES == 0 for size in sizes)
    if not aligned:
        lefts = [
            lax.dynamic_slice_in_dim(v, (me[0] ^ slot) * size, size, axis=1) for v, size in zip(lefts, sizes)
        ]
    return lefts, sizes, aligned


def grads_cost(lefts, sizes, products):
    flops = sum(2 * lefts[l].shape[0] * sizes[l] * (end - begin) for l, r, begin, end in products)
    return cost(flops / 0.6e9, flops // 256)


def weight_grads(name, me, lefts, rights, products, slot, parts):
    lefts, sizes, aligned = prepared(me, lefts, slot, parts)
    given = len(lefts) + len(rights)

    def kernel(me_ref, *refs):
        def store(n, begin, end, value):
            refs[given + n][:, begin:end] = value.astype(BF)

        products_of(me_ref[0], refs, len(lefts), products, slot, parts, aligned, store)

    outs = [struct((sizes[l], end - begin), BF) for l, r, begin, end in products]
    return kernel_call(
        kernel, name, [SMEM] + [VMEM] * given, outs, [], 8, grads_cost(lefts, sizes, products)
    )(me, *lefts, *rights)


def split_grads(name, place, axis, lefts, rights, products, swapped, parts, outer, rows, sums=None):
    lefts, sizes, aligned = prepared(place, lefts, 0, parts)
    given = len(lefts) + len(rights)
    base = rows * outer * (2 if axis == 3 else 4)
    inner = base // (2 * outer)
    places, width = [], 0
    for l, r, begin, end in products:
        places.append(width)
        width += (end - begin) * (sizes[l] // base)
    count = len(products)
    extra = [] if sums is None else [sums]
    flat = [v for arrays in swapped for v in arrays]
    per = len(flat) // max(parts - 1, 1)

    def kernel(place_ref, *refs):
        others = refs[given : given + per * (parts - 1)]
        tail = refs[given + per * (parts - 1) :]
        send, kept = tail[len(extra) : len(extra) + 2]
        high_is_mine = place_ref[axis] == 1

        def store(n, begin, end, value):
            for k in range(parts - 1):
                block, at = (k * per + n, 0) if per == count else (k, places[n])
                value = value + others[block][:, at + begin : at + end].astype(F32)
            times = value.shape[0] // base
            value = value.reshape(outer, 2, inner // rows, times, rows, end - begin)
            for t in range(times):
                to = places[n] + t * (products[n][3] - products[n][2]) + begin
                low = value[:, 0, :, t].reshape(outer, inner, end - begin)
                high = value[:, 1, :, t].reshape(outer, inner, end - begin)
                send[:, :, to : to + end - begin] = jnp.where(high_is_mine, low, high).astype(BF)
                kept[:, :, to : to + end - begin] = jnp.where(high_is_mine, high, low)

        products_of(place_ref[0], refs, len(lefts), products, 0, parts, aligned, store)
        if extra:
            held = tail[-1]
            held[place_ref[0]] = tail[0][...]
            for k in range(1, parts):
                block = others[(k - 1) * per]
                held[place_ref[0] ^ k] = unpack(block[0:32, block.shape[1] - LANES :])
            value = held[0]
            for k in range(1, parts):
                value = value + held[k]
            columns = slice(width, width + LANES)
            send[:, :, columns] = jnp.zeros((outer, inner, LANES), BF)
            kept[:, :, columns] = jnp.zeros((outer, inner, LANES), F32)
            send[0, :, columns] = pack(value)
            kept[0, 0:8, columns] = value

    shape = (outer, inner, width + LANES * len(extra))
    return kernel_call(
        kernel,
        name,
        [SMEM] + [VMEM] * (given + len(flat) + len(extra)),
        [struct(shape, BF), struct(shape, F32)],
        [pltpu.VMEM((parts, 8, LANES), F32)] * len(extra),
        8,
        grads_cost(lefts, sizes, products),
    )(place, *lefts, *rights, *flat, *extra)


def middle_back(dims, ff):
    total, width, half, size = dims
    packed = width + 2 * ff

    def kernel(len_ref, d_left, d_right, middle, gains, low_ref, state, gate, forget, w, *refs):
        tables, cot_far, refs = refs[:4], refs[4], refs[5:]
        d_mid, d_middle, d_gate, local, prod, cot, hold, keep, carry, tile_sems = refs
        first = len_ref[0, 0]
        second = first + len_ref[0, 1]
        bound = low_ref[0:1, :]
        io = Streams(total, tile_sems, [(cot_far, cot)])
        io.start(backwards=True)
        ffn_gain = gains[2:3, :]
        gain = gains[1:2, :]

        def keeps(base, rows, value):
            time = slot_times(base, rows, total)
            start = (time == 0) | (time == first) | (time == second)
            return jnp.where(start, 0.0, bound + (1.0 - bound) * sigmoid(value))

        k = keeps(0, 8, forget[0:8, :])
        carry[0:16, :] = jnp.zeros((16, half), F32)
        carry[16:24, :] = jnp.ones((8, half), F32)
        carry[24:32, :] = jnp.concatenate([k[1:8, :], jnp.zeros((1, half), F32)], axis=0)

        def enter(base):
            block = pl.ds(base, TILE)
            hold[...] = mm_nt(d_left[block, :], w[:, width : width + ff]) + mm_nt(
                d_right[block, :], w[:, width + ff : packed]
            )
            io.wait(base)

            def norm_back(at, rows):
                here = pl.ds(at, rows)
                there = span(base + at, rows)
                valid = (slot_times(base + at, rows, total) < second).astype(F32)
                x = middle[there, :]
                scale = lax.rsqrt(jnp.mean(x * x, axis=-1, keepdims=True) + 1e-06)
                d = hold[here, :]
                unit = x * scale
                d = d * ffn_gain
                back = scale * (d - unit * jnp.mean(d * unit, axis=-1, keepdims=True))
                back = back + valid * cot[there, :]
                d_middle[there, :] = back
                d_mid[there, :] = back.astype(BF)

            chunks("norm_back", norm_back)

        def tile(base):
            enter(base)
            block = pl.ds(base, TILE)
            hold[...] = mm_nt(d_mid[block, :], w[:, 0:width])

            def through(at, rows):
                here = pl.ds(at, rows)
                there = span(base + at, rows)
                low = lax.broadcasted_iota(jnp.int32, (rows, LANES), 1) < LANES // 2
                re, im = state[there, 0:half], state[there, half:width]
                c, s = turned(tables, base + at, rows)
                mixed = strips(c * re - s * im) + strips(c * im + s * re)
                grouped, scales = centre_and_scale(mixed, low, size)
                back = []
                for n in range(len(grouped)):
                    lanes = slice(n * LANES, (n + 1) * LANES)
                    opened = sigmoid(gate[there, lanes].astype(F32))
                    d = hold[here, lanes]
                    part = d * grouped[n] * opened
                    d_gate[there, lanes] = (part * gain[:, lanes] * (1.0 - opened)).astype(BF)
                    back.append(d * opened * gain[:, lanes])
                mean = group_spread(group_means(back, low, size), low)
                along = group_spread(group_means([b * g for b, g in zip(back, grouped)], low, size), low)
                back = [t * (b - m - g * a) for t, b, m, g, a in zip(scales, back, mean, grouped, along)]
                for n in range(3):
                    lanes = slice(n * LANES, (n + 1) * LANES)
                    cn, sn = c[:, lanes], s[:, lanes]
                    local[there, lanes] = cn * back[n] + sn * back[n + 3]
                    local[there, half + n * LANES : half + (n + 1) * LANES] = cn * back[n + 3] - sn * back[n]

            chunks("through", through)

            def kept(at, rows):
                there = span(base + at, rows)
                keep[pl.ds(at, rows), :] = keeps(base + at, rows, forget[there, :])

            chunks("kept", kept)

            def scan(i, held):
                re, im, p, k = held
                at = (TILE // 8 - 1 - i) * 8
                there = span(base + at, 8)
                re = k * re + local[there, 0:half]
                im = k * im + local[there, half:width]
                p = k * p
                local[there, 0:half] = re
                local[there, half:width] = im
                prod[there, :] = p
                return re, im, p, keep[span(at, 8), :]

            held = (carry[0:8, :], carry[8:16, :], carry[16:24, :], carry[24:32, :])
            held = lax.fori_loop(0, TILE // 8, scan, held, unroll=8)
            carry[0:8, :], carry[8:16, :], carry[16:24, :], carry[24:32, :] = held

        tiles_of(total, tile, backwards=True)

    return kernel_call(
        kernel,
        "middle_back",
        [SMEM] + [VMEM] * 13 + [HBM],
        [
            struct((total, width), BF),
            struct((total, width), F32),
            struct((total, width), BF),
            struct((total, width), F32),
            struct((total, half), F32),
        ],
        [
            pltpu.VMEM((total, width), F32),
            pltpu.VMEM((TILE, width), F32),
            pltpu.VMEM((TILE, half), F32),
            pltpu.VMEM((32, half), F32),
            stream_sems(total, 1),
        ],
        8,
        cost(19, 60 * total * width),
    )


def source_back(dims, parts, me, lefts, d_mid, shares, fine):
    total, width, half, size = dims
    wide = 2 * width + half
    given, sizes, aligned = [], None, True
    for slot in range(1, parts):
        made, sizes, aligned = prepared(me, lefts, slot, parts)
        given.append(list(made))
    if aligned:
        given = [list(lefts)] * max(parts - 1, 0)
        flat = list(lefts)
    else:
        flat = [v for made in given for v in made]
    products = [p for share in shares for p in share]
    count = len(shares)
    owner, widths = [], []
    for n, share in enumerate(shares):
        widths.append(0)
        for l, r, begin, end in share:
            owner.append((n, widths[n]))
            widths[n] += end - begin
    widths[0] += LANES if fine else 0

    def kernel(len_ref, me_ref, local, prod, d_gate, low_ref, state, forget, inner, *refs):
        tables, refs = refs[:4], refs[4:]
        left_refs, d_mid_ref, refs = refs[: len(flat)], refs[len(flat)], refs[len(flat) + 1 :]
        d_proj, sums = refs[:2]
        slots, (ends, acc) = refs[2 : 2 + count * (parts - 1)], refs[2 + count * (parts - 1) :]
        first = len_ref[0, 0]
        second = first + len_ref[0, 1]
        bound = low_ref[0:1, :]
        acc[...] = jnp.zeros_like(acc)
        p = prod[0:8, :]
        for h in (0, 1):
            z = local[0:8, h * half : (h + 1) * half]
            made = [jnp.zeros((1, half), F32)]
            for c in range(CHAINS - 2, -1, -1):
                made.append(z[c + 1 : c + 2, :] + p[c + 1 : c + 2, :] * made[-1])
            ends[8 * h : 8 * h + 8, 0:half] = jnp.concatenate(made[::-1], axis=0)
        old = state[total - 8 : total, :]
        ends[16:24, :] = jnp.concatenate([old[7:8, :], old[0:7, :]], axis=0)

        def tile(base):
            def back(at, rows):
                row = base + at
                there = span(row, rows)
                p = prod[there, :]
                re = local[there, 0:half] + p * repeat(ends[0:8, 0:half], rows)
                im = local[there, half:width] + p * repeat(ends[8:16, 0:half], rows)
                up = span(jnp.maximum(row - 8, 0), 8)
                stay = pl.ds(pl.multiple_of(row, 8), rows - 8)
                old_re = jnp.concatenate(
                    [jnp.where(row == 0, ends[16:24, 0:half], state[up, 0:half]), state[stay, 0:half]], axis=0
                )
                old_im = jnp.concatenate(
                    [jnp.where(row == 0, ends[16:24, half:width], state[up, half:width]), state[stay, half:width]],
                    axis=0,
                )
                time = slot_times(row, rows, total)
                start = (time == 0) | (time == first) | (time == second)
                sf = sigmoid(forget[there, :])
                rest = (1.0 - bound) * (1.0 - sf)
                turn = (1.0 - rest) * (im * old_re - re * old_im)
                acc[8:16, :] += fold(jnp.where(start, 0.0, turn))
                d_lam = jnp.where(start, 0.0, re * old_re + im * old_im)
                c, s = turned(tables, row, rows)
                d_re = c * re - s * im
                d_im = c * im + s * re
                for lane, d in ((0, d_re), (half, d_im)):
                    v = inner[there, lane : lane + half].astype(F32)
                    sv = sigmoid(v)
                    d_lam = d_lam - d * (v * sv)
                    d_proj[there, lane : lane + half] = (rest * d * (sv * (1.0 + v * (1.0 - sv)))).astype(BF)
                acc[0:8, :] += fold(d_lam * (1.0 - sf))
                d_proj[there, 2 * width : wide] = (d_lam * rest * sf).astype(BF)
                d_proj[there, width : 2 * width] = d_gate[there, :]

            chunks("source_back", back)

        tiles_of(total, tile)
        out = [jnp.sum(acc[8 * n : 8 * n + 8, :], axis=0, keepdims=True) for n in range(2)]
        out = strips(out[0]) + strips(out[1])
        sums[...] = jnp.concatenate(out + [jnp.zeros((8 - len(out), LANES), F32)], axis=0)
        for slot in range(1, parts):
            used = left_refs if aligned else left_refs[(slot - 1) * len(lefts) : slot * len(lefts)]

            def store(n, begin, end, value):
                share, at = owner[n]
                slots[(slot - 1) * count + share][:, at + begin : at + end] = value.astype(BF)

            products_of(
                me_ref[0], [*used, d_proj, d_mid_ref], len(lefts), products, slot, parts, aligned, store
            )
            if fine:
                block = slots[(slot - 1) * count]
                rest = jnp.zeros((block.shape[0] - 24, LANES), F32)
                carried = jnp.concatenate([pack(sums[...]).astype(F32), rest], axis=0)
                block[:, block.shape[1] - LANES :] = carried.astype(BF)

    outs = [struct((total, wide), BF), struct((8, LANES), F32)]
    outs += [struct((width // parts, n), BF) for n in widths] * (parts - 1)
    call = kernel_call(
        kernel,
        "source_back",
        [SMEM, SMEM] + [VMEM] * (12 + len(flat)),
        outs,
        [pltpu.VMEM((24, width), F32), pltpu.VMEM((16, half), F32)],
        6,
        cost(10, 40 * total * width),
    )

    def run(lengths, me, *arrays):
        d_proj, sums, *slots = call(lengths, me, *arrays, *flat, d_mid)
        return d_proj, sums, [slots[k * count : (k + 1) * count] for k in range(parts - 1)]

    return run


def input_back(parts, cut, dims):
    total, width, half, size = dims
    wide = 2 * width + half

    def kernel(me_ref, d_proj, gains, d_middle, tok_far, *refs):
        left_pieces, right_pieces = refs[:parts], refs[parts : 2 * parts]
        out, w, tok, hold, sems, tile_sems = refs[2 * parts :]
        me = me_ref[0]
        copies = piece_copies(me, left_pieces, w, pl.ds(0, cut), sems, 0)
        copies += piece_copies(me, right_pieces, w, pl.ds(cut, w.shape[1] - cut), sems, parts)
        for c in copies:
            c.start()
        io = Streams(total, tile_sems, [(tok_far, tok)])
        io.start()
        gain = gains[0:1, :]
        for c in copies:
            c.wait()

        def tile(base):
            hold[...] = mm_nt(d_proj[pl.ds(base, TILE), :], w[:, 0:wide])
            io.wait(base)

            def norm_back(at, rows):
                here = pl.ds(at, rows)
                there = span(base + at, rows)
                x = tok[there, :]
                scale = lax.rsqrt(jnp.mean(x * x, axis=-1, keepdims=True) + 1e-06)
                d = hold[here, :]
                unit = x * scale
                d = d * gain
                out[there, :] = d_middle[there, :] + scale * (d - unit * jnp.mean(d * unit, axis=-1, keepdims=True))

            chunks("norm_back", norm_back)

        tiles_of(total, tile)

    return kernel_call(
        kernel,
        "input_back",
        [SMEM, VMEM, VMEM, VMEM] + [HBM] + [ANY] * (2 * parts),
        [struct((total, width), F32)],
        [
            pltpu.VMEM((width, wide + LANES), BF),
            pltpu.VMEM((total, width), F32),
            pltpu.VMEM((TILE, width), F32),
            pltpu.SemaphoreType.DMA((2 * parts,)),
            stream_sems(total, 1),
        ],
        10,
        cost(7, 20 * total * width),
    )


def order_call(place, held, cut):
    rows, columns = held[0].shape
    deep = len(held)

    def kernel(place_ref, *refs):
        for k in range(deep):
            at = place_ref[1] ^ k
            refs[deep][at] = refs[k][:, 0:cut]
            refs[deep + 1][at] = refs[k][:, cut:columns]

    outs = [struct((deep, rows, cut), BF), struct((deep, rows, columns - cut), BF)]
    return kernel_call(kernel, "order_z", [SMEM] + [VMEM] * deep, outs, [], 2, cost(1, 4 * deep * rows * columns))(
        place, *held
    )


def join_call(place, axes, own, got):
    count = len(own)

    def kernel(place_ref, *refs):
        for n in range(count):
            bit = place_ref[axes[n]]
            refs[2 * count + n][:, pl.ds(bit, 1)] = refs[n][...][:, None]
            refs[2 * count + n][:, pl.ds(1 - bit, 1)] = refs[count + n][...][:, None]

    outs = [struct((v.shape[0], 2) + v.shape[1:], BF) for v in own]
    moved = sum(8 * v.size for v in own)
    return kernel_call(kernel, "join", [SMEM] + [VMEM] * (2 * count), outs, [], 2, cost(2, moved))(place, *own, *got)


def halve_call(place, axes, kept, got, carried):
    flat_kept = [v for share in kept for v in share]
    flat_got = [v for share in got for v in share]
    count = len(flat_kept)

    def kernel(place_ref, *refs):
        outs = refs[2 * count :]
        at = 0
        for n, share in enumerate(kept):
            bit = place_ref[axes[n]]
            begin = 0
            for v in share:
                end = begin + v.shape[-1]
                for out, half in ((outs[2 * n], 1 - bit), (outs[2 * n + 1], bit)):
                    value = refs[at][:, pl.ds(half, 1)] + refs[count + at][:, pl.ds(half, 1)].astype(F32)
                    out[:, :, begin:end] = value[:, 0].astype(out.dtype)
                at += 1
                begin = end
        if carried:
            columns = slice(flat_kept[0].shape[-1] - LANES, None)
            value = refs[0][0, 0, 0:8, columns] + unpack(refs[count][0, 0, :, columns])
            outs[0][0, :, columns] = pack(value)
            outs[1][0, 0:8, columns] = value

    outs = []
    for share in kept:
        shape = share[0].shape[:1] + share[0].shape[2:-1] + (sum(v.shape[-1] for v in share),)
        outs += [struct(shape, BF), struct(shape, F32)]
    moved = sum(10 * v.size for v in flat_kept)
    made = kernel_call(kernel, "halve", [SMEM] + [VMEM] * (2 * count), outs, [], 4, cost(3, moved))(
        place, *flat_kept, *flat_got
    )
    return [made[2 * n : 2 * n + 2] for n in range(len(kept))]


def deal_call(place, kept, got, carried):
    deep, rows = kept[0].shape[:2]
    widths = [v.shape[2] for v in kept]
    columns = sum(widths)
    widths[0] -= LANES if carried else 0

    def kernel(place_ref, *refs):
        begin = 0
        for n, width in enumerate(widths):
            for k in range(deep):
                at = place_ref[1] ^ k
                value = refs[n][at, :, 0:width] + refs[2 + n][at, :, 0:width].astype(F32)
                refs[4 + k][:, begin : begin + width] = value.astype(refs[4 + k].dtype)
            begin += width
        if carried:
            last = slice(widths[0], widths[0] + LANES)
            value = refs[0][0, 0:8, last] + unpack(refs[2][0, :, last])
            refs[4][:, begin:] = jnp.concatenate([value, jnp.zeros((rows - 8, LANES), F32)], axis=0)
            for k in range(1, deep):
                refs[4 + k][:, begin:] = pack(value)

    outs = [struct((rows, columns), F32 if k == 0 else BF) for k in range(deep)]
    return kernel_call(kernel, "deal_z", [SMEM] + [VMEM] * 4, outs, [], 4, cost(2, 10 * deep * rows * columns))(
        place, *kept, *got
    )


def finish_call(place, own, got, cuts, gains, carried):
    deep = len(got) + 1
    rows, columns = own.shape
    bounds = [0, *cuts, columns - (LANES if carried else 0)]
    pairs = list(zip(bounds[:-1], bounds[1:]))
    flat = [v for gain, weights in gains for v in (gain, *weights.values())]

    def kernel(place_ref, *refs):
        given = list(refs[deep : deep + len(flat)])
        outs = refs[deep + len(flat) :]
        for n, (a, b) in enumerate(pairs):
            value = refs[0][:, a:b]
            for k in range(1, deep):
                value = value + refs[k][:, a:b].astype(F32)
            outs[n][...] = value
        at = len(pairs)
        for gain, weights in gains:
            gain_ref = given.pop(0)
            total = jnp.zeros((rows, 1), F32)
            for n in weights:
                total = total + jnp.sum(given.pop(0)[...].astype(F32) * outs[n][...], axis=1, keepdims=True)
            shape = (rows, LANES)
            diagonal = lax.broadcasted_iota(jnp.int32, shape, 0) == lax.broadcasted_iota(jnp.int32, shape, 1)
            row = jnp.sum(jnp.where(diagonal, total, 0.0), axis=0, keepdims=True)
            outs[at][...] = (row[:, 0:rows] / gain_ref[...].astype(F32))[0]
            at += 1
        if carried:
            held = outs[-1]
            held[place_ref[1]] = refs[0][0:8, columns - LANES :]
            for k in range(1, deep):
                held[place_ref[1] ^ k] = unpack(refs[k][:, columns - LANES :])
            value = held[0]
            for k in range(1, deep):
                value = value + held[k]
            for n in range(2):
                strip = [value[3 * n + i : 3 * n + i + 1, :] for i in range(3)]
                outs[at + n][...] = jnp.concatenate(strip, axis=1)[0]

    outs = [struct((rows, b - a), F32) for a, b in pairs] + [struct((rows,), F32)] * len(gains)
    outs += [struct((3 * LANES,), F32)] * (2 * carried)
    scratch = [pltpu.VMEM((deep, 8, LANES), F32)] * carried
    return kernel_call(
        kernel, "finish", [SMEM] + [VMEM] * (deep + len(flat)), outs, scratch, 2, cost(2, 12 * rows * columns)
    )(place, own, *got, *flat)


class Exchange:
    def __init__(self, mesh, fine):
        self.parts = mesh.shape["dp"]
        self.count = mesh.shape["fsdp"]
        self.deep = self.count // 4
        me = lax.axis_index("fsdp")
        self.dp = lax.axis_index("dp")
        self.z = me // 4
        self.y_bit = (me // 2) % 2 == 1
        self.x_bit = me % 2 == 1
        self.fine = fine
        self.place = jnp.stack([self.dp, self.z, (me // 2) % 2, me % 2]).astype(jnp.int32)

    def swap(self, value, mask):
        return lax.ppermute(value, "fsdp", [(i, i ^ mask) for i in range(self.count)])

    def swap_dp(self, value, mask):
        return lax.ppermute(value, "dp", [(i, i ^ mask) for i in range(self.parts)])

    def send_z(self, shard, k):
        return self.swap(shard, 4 * k)

    def order_z(self, held, cut):
        if self.fine:
            return order_call(self.place, held, cut)
        step = 1
        while step < self.deep:
            bit = (self.z // step) % 2 == 1
            held = [jnp.where(bit, held[k ^ step], held[k]) for k in range(self.deep)]
            step *= 2
        stack = jnp.stack(held)
        return [stack[:, :, :cut], stack[:, :, cut:]]

    def send_first(self, shares):
        return [self.swap(shares[0], 1), self.swap(shares[1], 2)]

    def join_first(self, shares, got):
        if self.fine:
            return join_call(self.place, (3, 2), shares, got)
        out = []
        for own, other, bit in zip(shares, got, (self.x_bit, self.y_bit)):
            out.append(jnp.stack([jnp.where(bit, other, own), jnp.where(bit, own, other)], axis=1))
        return out

    def send_second(self, shares):
        return [self.swap(shares[0], 2), self.swap(shares[1], 1)]

    def join_second(self, shares, got):
        if self.fine:
            flat = [v.reshape((-1,) + v.shape[2:]) for v in (shares[1], got[1])]
            made = join_call(self.place, (2, 3), [shares[0], flat[0]], [got[0], flat[1]])
            return [v.reshape(-1, v.shape[-1]) for v in made]
        out = []
        for own, other, bit, place in zip(shares, got, (self.y_bit, self.x_bit), (1, 2)):
            v = jnp.stack([jnp.where(bit, other, own), jnp.where(bit, own, other)], axis=place)
            out.append(v.reshape(-1, v.shape[-1]))
        return out

    def gather_dp(self, shares):
        return [[v] + [self.swap_dp(v, k) for k in range(1, self.parts)] for v in shares]

    def cut_rows(self, own, swapped, outer, bit, rows):
        columns = []
        for n, value in enumerate(own):
            value = value.astype(F32)
            for arrays in swapped:
                value = value + arrays[n].astype(F32)
            value = value.reshape(self.count, -1, rows, value.shape[1])
            columns += [value[:, i] for i in range(value.shape[1])]
        total = jnp.concatenate(columns, axis=-1)
        total = total.reshape(outer, 2, -1, total.shape[-1])
        low, high = total[:, 0], total[:, 1]
        return jnp.where(bit, low, high).astype(BF), jnp.where(bit, high, low)

    def halves(self, total, bit):
        low, high = total[:, 0], total[:, 1]
        return jnp.where(bit, low, high).astype(BF), jnp.where(bit, high, low)

    def halve(self, kept, got, carried=False):
        kept = [[v.reshape(self.deep, 2, -1, v.shape[-1]) for v in share] for share in kept]
        got = [[g.reshape(k.shape) for g, k in zip(*pair)] for pair in zip(got, kept)]
        if self.fine:
            return halve_call(self.place, (2, 3), kept, got, carried)
        totals = [
            jnp.concatenate([k + g.astype(F32) for k, g in zip(*pair)], axis=-1) for pair in zip(kept, got)
        ]
        return [self.halves(total, bit) for total, bit in zip(totals, (self.y_bit, self.x_bit))]

    def send_halves(self, cuts):
        return [c[1] for c in cuts], [self.swap(cuts[0][0], 2), self.swap(cuts[1][0], 1)]

    def deal_z(self, kept, got, carried=False):
        if self.fine:
            own, *others = deal_call(self.place, kept, got, carried)
            return own, others
        total = jnp.concatenate([k + g.astype(F32) for k, g in zip(kept, got)], axis=-1)
        own, *others = [lax.dynamic_index_in_dim(total, self.z ^ k, 0, keepdims=False) for k in range(self.deep)]
        return own, [v.astype(BF) for v in others]

    def send_parts(self, others):
        return [self.swap(v, 4 * k) for k, v in enumerate(others, 1)]

    def finish_z(self, own, got, cuts, gains, carried=False):
        if self.fine:
            return finish_call(self.place, own, got, cuts, gains, carried)
        for v in got:
            own = own + v.astype(F32)
        made = jnp.split(own, cuts, axis=1)
        for gain, weights in gains:
            total = sum(jnp.sum(w.astype(F32) * made[n], axis=1) for n, w in weights.items())
            made.append(total / gain[0].astype(F32))
        return made

    def total(self, value):
        for k in range(self.parts.bit_length() - 1):
            value = value + self.swap_dp(value, 1 << k)
        for k in range(self.count.bit_length() - 1):
            value = value + self.swap(value, 1 << k)
        return value


def after(value, *others):
    return lax.optimization_barrier((value, *others))[0]


def to_chains(value, lengths=None):
    rows, columns = value.shape
    length = rows // CHAINS
    parts = range(columns // LANES)
    masked = 0 if lengths is None else 1

    def kernel(*refs):
        source = refs[masked]
        low, (out, natural, kept, sems) = refs[masked + 1 : 2 * masked + 1], refs[2 * masked + 1 :]
        arriving = [
            pltpu.make_async_copy(source.at[:, pl.ds(n * LANES, LANES)], natural.at[n], sems.at[0, n]) for n in parts
        ]
        leaving = [
            pltpu.make_async_copy(kept.at[n], out.at[:, pl.ds(n * LANES, LANES)], sems.at[1, n]) for n in parts
        ]
        for c in arriving:
            c.start()
        if masked:
            valid = (slot_times(0, rows, rows) < refs[0][0, 0] + refs[0][0, 1]).astype(F32)
        for n in parts:
            arriving[n].wait()

            def move(j, carry):
                kept[n, span(j * CHAINS, CHAINS), :] = natural[n, pl.ds(j, CHAINS, stride=length), :]
                return carry

            lax.fori_loop(0, length, move, 0, unroll=16)
            leaving[n].start()
            if masked:
                low[0][:, n * LANES : (n + 1) * LANES] = (valid * kept[n]).astype(BF)
        for c in leaving:
            c.wait()

    place = pltpu.VMEM((columns // LANES, rows, LANES), F32)
    made = kernel_call(
        kernel,
        "to_chains",
        [SMEM] * masked + [HBM],
        [struct((rows, columns), BF)] * masked + [struct((rows, columns), F32)],
        [place, place, pltpu.SemaphoreType.DMA((2, columns // LANES))],
        8,
        cost(4, 8 * rows * columns),
        distant=1,
    )(*([lengths] * masked), *far(value))
    return made if masked else made[0]


def from_chains(value):
    rows, columns = value.shape
    return value.reshape(rows // CHAINS, CHAINS, columns).transpose(1, 0, 2).reshape(rows, columns)


def turns(phase, rows):
    length = rows // CHAINS
    inside = jnp.arange(length, dtype=F32)[:, None] * phase
    outside = (jnp.arange(CHAINS, dtype=F32) * length)[:, None] * phase
    return [jnp.cos(inside), jnp.sin(inside), jnp.cos(outside), jnp.sin(outside)]


def build(mesh):
    def per_device(
        tokens,
        lengths,
        w_input,
        w_forget,
        w_gate,
        w_output,
        w_up_gate,
        w_up,
        w_down,
        norm_gain,
        group_gain,
        ffn_gain,
        lower_bound,
        phase,
        cotangent,
    ):
        ex = Exchange(mesh, w_input.shape[0] % 24 == 0)
        parts = ex.parts
        total, width = tokens.shape
        half = lower_bound.shape[0]
        ff = w_up.shape[1]
        dims = (total, width, half, width // GROUPS)
        shard = w_input.shape[0]

        columns = jnp.stack([norm_gain, group_gain, ffn_gain], axis=1)
        columns = jnp.pad(columns, ((0, 0), (0, LANES - 3)))
        pack1 = jnp.concatenate([w_input, w_gate, w_forget, columns], axis=1)
        pack1, tokens, rest = after((pack1, tokens, [w_output, w_up_gate, w_up]))
        pack2 = jnp.concatenate(rest, axis=1)
        cut1, cut2, cut3 = pack1.shape[1] // 2, pack2.shape[1] // 2, width // 2

        others = range(1, ex.deep)
        one = [pack1] + [ex.send_z(pack1, k) for k in others]
        one, pack2, ex.place, tokens = after((one, pack2, ex.place, tokens))
        tok = to_chains(tokens)
        one = ex.order_z(one, cut1)
        got = ex.send_first(one)
        two = [pack2] + [ex.send_z(pack2, k) for k in others[:2]]
        one, got, two, tok, phase, lower_bound = after((one, got, two, tok, phase, lower_bound))
        tables = turns(phase, total)
        low = jnp.broadcast_to(lower_bound, (8, half))
        one = ex.join_first(one, got)
        got = ex.send_second(one)
        two += [ex.send_z(two[0], k) for k in others[2:]]
        one, got, two, tables, low = after((one, got, two, tables, low))
        one = ex.gather_dp(ex.join_second(one, got))
        two = ex.order_z(two, cut2)
        got = ex.send_first(two)
        (tok,) = far(tok)
        inner, gate, forget, gains, normed, inner_low, gate_low = recurrent_project(parts, cut1, dims)(
            ex.place, tok, *one[0], *one[1]
        )
        two, got, gains, w_down, cotangent = after((two, got, gains, w_down, cotangent))
        grad, cot = to_chains(cotangent, lengths)
        two = ex.join_first(two, got)
        got = ex.send_second(two)
        three = [w_down] + [ex.send_z(w_down, k) for k in others]
        gated, state = recurrent_mix(dims)(lengths, inner, gate, forget, gains, low, *tables)
        three, gated = after((three, gated))
        three = ex.order_z(three, cut3)
        late = ex.send_first(three)
        two, got, three, late, gated, cot, grad = after((two, got, three, late, gated, cot, grad))
        two = ex.gather_dp(ex.join_second(two, got))
        three = ex.join_first(three, late)
        late = ex.send_second(three)
        (cot,) = far(cot)
        middle, ffn_in, to_left, to_right, hidden, w_two, middle_far, hidden_far = ffn_up(parts, cut2, dims, ff)(
            ex.place, gated, gains, tok, *two[0], *two[1]
        )
        turn = (ex.place, lengths)
        three, late, ffn_in = after((three, late, ffn_in))
        three, turn = after((ex.join_second(three, late), turn))
        three = ex.gather_dp(three)
        fold_rows = ff // width

        def last_grads(name, n, turn, lefts, rights, products, swapped, sums=None):
            outer, bit = ((2 * ex.deep, ex.x_bit), (ex.deep, ex.y_bit))[n]
            if ex.fine:
                return split_grads(
                    name, turn[0], 3 - n, lefts, rights, products, swapped, parts, outer, shard, sums
                )
            made = weight_grads(name, turn[0], lefts, rights, products, 0, parts)
            return ex.cut_rows(made, swapped, outer, bit, shard)

        def grads_of(name, turn, lefts, rights, products):
            swapped = []
            for k in range(1, parts):
                made = weight_grads(name, turn[0], lefts, rights, products, k, parts)
                made, turn = after((made, turn))
                swapped.append([ex.swap_dp(v, k) for v in made])
            return swapped, turn

        halves = [(0, 0, 0, cut3), (0, 0, cut3, width)]
        swapped_down, turn = grads_of("down_grads", turn, [hidden], [grad], halves)
        d_left, d_right, w_three = ffn_turn(parts, cut3, dims, ff)(
            turn[0], grad, to_left, to_right, *three[0], *three[1]
        )
        d_left, swapped_down, turn = after((d_left, swapped_down, turn))
        swapped = []
        for n, right in enumerate((d_left, d_right)):
            made, turn = grads_of("up_grads", turn, [ffn_in], [right], [(0, 0, 0, ff)])
            swapped.append([up + down[n : n + 1] for up, down in zip(made, swapped_down)])
        kept, got = [], []
        for n, right in enumerate((d_left, d_right)):
            products = [(0, 0, 0, ff), (1, 1) + halves[n][2:]]
            send, keep = last_grads("ffn_grads", n, turn, [ffn_in, hidden], [right, grad], products, swapped[n])
            send, keep, turn = after((send, keep, turn))
            kept.append([keep])
            got.append([ex.swap(send, n + 1)])
        d_mid, d_middle, d_gate, local, prod = middle_back(dims, ff)(
            turn[1], d_left, d_right, middle, gains, low, state, gate_low, forget, w_two, *tables, cot
        )
        wide = 2 * width + half
        shares = [[(0, 0, 0, width), (0, 0, 2 * width, wide)], [(0, 0, 0, width), (1, 1, 0, width)]]
        local, turn = after((local, turn))
        swapped_b, turn = grads_of("recurrent_grads", turn, [normed, gated], [d_gate, d_mid], shares[1])
        kept, got, turn = after((kept, got, turn))
        cuts, turn = after((ex.halve(kept, got), turn))
        kept, got = ex.send_halves(cuts)
        d_proj, sums, made = source_back(dims, parts, ex.place, [normed], d_mid, shares[:1], ex.fine)(
            turn[1], turn[0], local, prod, d_gate, low, state, forget, inner_low, *tables
        )
        sums, turn = after((sums, turn))
        send_b, kept_b = last_grads(
            "recurrent_grads", 1, turn, [normed, gated], [d_gate, d_mid], shares[1], swapped_b
        )
        made, kept, got, sums, send_b, kept_b, turn = after((made, kept, got, sums, send_b, kept_b, turn))
        swapped_a = []
        for k, (v,) in enumerate(made, 1):
            v = ex.swap_dp(v, k)
            swapped_a.append([v] if ex.fine else [v[:, :width], v[:, width:]])
        ffn, others = ex.deal_z(kept, got)
        ffn, others, send_b, turn = after((ffn, others, send_b, turn))
        ffn_got = ex.send_parts(others)
        got_b = ex.swap(send_b, 2)
        send_a, kept_a = last_grads(
            "recurrent_grads", 0, turn, [normed], [d_proj], shares[0], swapped_a, sums if ex.fine else None
        )
        send_a, kept_a, turn = after((send_a, kept_a, turn))
        got_a = ex.swap(send_a, 1)
        kept, got = [[kept_a], [kept_b]], [[got_a], [got_b]]
        (input_grad,) = input_back(parts, cut1, dims)(
            turn[0], d_proj, gains, d_middle, tok, *one[0], *one[1]
        )
        input_grad, turn = after((input_grad, turn))
        (act,) = ffn_out(dims, ff)(turn[1], *far(hidden_far, middle_far, w_three))
        input_grad, ffn_got, kept, got, act = after((input_grad, ffn_got, kept, got, act))
        cuts, act = after((ex.halve(kept, got, ex.fine), act))
        kept, got = ex.send_halves(cuts)
        act = from_chains(act)
        middle_at = ff + fold_rows * cut3
        bounds = [ff, middle_at, middle_at + ff]
        grad_up_gate, down_a, grad_up, down_b, grad_ffn_gain = ex.finish_z(
            ffn, ffn_got, bounds, [(ffn_gain[None], {0: w_up_gate, 2: w_up})]
        )
        kept, got, input_grad, act = after((kept, got, input_grad, act))
        rest, others = ex.deal_z(kept, got, ex.fine)
        rest, others, input_grad = after((rest, others, input_grad))
        got = ex.send_parts(others)
        input_grad = from_chains(input_grad)
        if not ex.fine:
            sums = ex.total(sums)
        norm_weights = {0: w_input, 1: w_forget, 2: w_gate}
        made = ex.finish_z(
            rest,
            got,
            [width, width + half, wide],
            [(norm_gain[None], norm_weights), (group_gain[None], {3: w_output})],
            ex.fine,
        )
        grad_input, grad_forget, grad_gate, grad_output, grad_norm_gain, grad_group_gain = made[:6]
        if ex.fine:
            grad_lower, grad_phase = made[6:]
        else:
            ahead = half // LANES
            grad_lower, grad_phase = sums[0:ahead].reshape(half), sums[ahead : 2 * ahead].reshape(half)

        halves = []
        for i in range(fold_rows):
            left_half = down_a[:, i * cut3 : (i + 1) * cut3]
            right_half = down_b[:, i * (width - cut3) : (i + 1) * (width - cut3)]
            halves.append(jnp.concatenate([left_half, right_half], axis=1))
        grad_down = jnp.concatenate(halves, axis=0)
        return (
            act,
            input_grad,
            grad_input,
            grad_forget,
            grad_gate,
            grad_output,
            grad_up_gate,
            grad_up,
            grad_down,
            grad_norm_gain,
            grad_group_gain,
            grad_ffn_gain,
            grad_lower,
            grad_phase,
        )

    return per_device


def solution(mesh):
    rows = P(("dp", "fsdp"), None)
    vec = P(("dp", "fsdp"))
    in_specs = (rows,) * 9 + (vec,) * 3 + (P(), P(), rows)
    out_specs = (rows,) * 9 + (vec,) * 3 + (P(), P())
    return jax.shard_map(build(mesh), mesh=mesh, in_specs=in_specs, out_specs=out_specs, check_vma=False)
```

```python
import jax
import jax.numpy as jnp
from jax import lax
from jax.experimental import pallas as pl
from jax.experimental.pallas import tpu as pltpu
from jax.sharding import PartitionSpec as P

GROUPS = 4
LANES = 128
CHAINS = 8
TILE = 256
BF = jnp.bfloat16
F32 = jnp.float32
TN = (((0,), (0,)), ((), ()))
NT = (((1,), (1,)), ((), ()))


def mm(left, right):
    return jnp.dot(left, right, preferred_element_type=F32)


def mm_nt(left, right):
    return lax.dot_general(left, right, NT, preferred_element_type=F32)


def mm_tn(left, right):
    return lax.dot_general(left, right, TN, preferred_element_type=F32)


def sigmoid(v):
    return 0.5 * jnp.tanh(0.5 * v) + 0.5


STEPS = {
    "norm": (256, 1),
    "sources": (64, 4),
    "mix": (64, 2),
    "finish": (256, 1),
    "norm_back": (256, 1),
    "through": (64, 4),
    "kept": (256, 1),
    "source_back": (64, 1),
}


def chunks(name, body):
    rows, unroll = STEPS[name]

    def step(i, carry):
        body(pl.multiple_of(i * rows, rows), rows)
        return carry

    lax.fori_loop(0, TILE // rows, step, 0, unroll=unroll)


def tiles_of(total, body, backwards=False, tile=TILE):
    count = total // tile

    def step(i, carry):
        body(pl.multiple_of(((count - 1 - i) if backwards else i) * tile, tile))
        return carry

    lax.fori_loop(0, count, step, 0)


def span(at, rows):
    return pl.ds(pl.multiple_of(at, rows), rows)


def repeat(value, rows):
    return jnp.concatenate([value] * (rows // 8), axis=0)


def fold(value):
    return jnp.sum(value.reshape(value.shape[0] // 8, 8, value.shape[1]), axis=0)


def cost(micros, moved):
    return pl.CostEstimate(flops=int(micros * 1.15e8), bytes_accessed=moved // 10, transcendentals=0)


def slot_times(base, rows, total):
    row = base + lax.broadcasted_iota(jnp.int32, (rows, 1), 0)
    return (row % CHAINS) * (total // CHAINS) + row // CHAINS


def turned(tables, base, rows):
    ci, si, co, so = tables
    inside = span(base // CHAINS, rows // CHAINS)
    half = ci.shape[1]
    c, s = ci[inside, :][:, None, :], si[inside, :][:, None, :]
    oc, os = co[...][None], so[...][None]
    return (c * oc - s * os).reshape(rows, half), (s * oc + c * os).reshape(rows, half)


def strips(value):
    return [value[:, i * LANES : (i + 1) * LANES] for i in range(value.shape[1] // LANES)]


def group_means(parts, low, size):
    zero = jnp.zeros_like(parts[0])
    sums = []
    for h in (0, 3):
        sums.append(parts[h] + jnp.where(low, parts[h + 1], zero))
        sums.append(jnp.where(low, zero, parts[h + 1]) + parts[h + 2])
    return [jnp.sum(s, axis=-1, keepdims=True) * (1.0 / size) for s in sums]


def group_spread(values, low):
    out = []
    for h in (0, 2):
        out += [values[h], jnp.where(low, values[h], values[h + 1]), values[h + 1]]
    return out


def pack(value):
    high = value.astype(BF).astype(F32)
    middle = (value - high).astype(BF).astype(F32)
    return jnp.concatenate([high, middle, value - high - middle], axis=0).astype(BF)


def unpack(value):
    value = value.astype(F32)
    return value[0:8, :] + value[8:16, :] + value[16:24, :]


def centre_and_scale(parts, low, size):
    means = group_spread(group_means(parts, low, size), low)
    parts = [p - m for p, m in zip(parts, means)]
    variances = group_means([p * p for p in parts], low, size)
    scales = group_spread([lax.rsqrt(v + 1e-05) for v in variances], low)
    return [p * s for p, s in zip(parts, scales)], scales


def piece_copies(me, pieces, target, columns, sems, first):
    rows = pieces[0].shape[0]
    out = []
    for k, piece in enumerate(pieces):
        at = pl.multiple_of((me ^ k) * rows, 16)
        out.append(pltpu.make_async_copy(piece, target.at[pl.ds(at, rows), columns], sems.at[first + k]))
    return out


HBM = pl.BlockSpec(memory_space=pltpu.HBM)
ANY = pl.BlockSpec(memory_space=pl.ANY)
SMEM = pl.BlockSpec(memory_space=pltpu.SMEM)


def struct(shape, dtype):
    return jax.ShapeDtypeStruct(shape, dtype)


VMEM = pl.BlockSpec(memory_space=pltpu.VMEM)


def far(*arrays):
    return [pltpu.with_memory_space_constraint(v, pltpu.HBM) for v in arrays]


def kernel_call(body, name, ins, outs, scratch, room, estimate, distant=0):
    near = len(outs) - distant
    outs = outs[:near] + [pltpu.HBM(v.shape, v.dtype) for v in outs[near:]]
    return pl.pallas_call(
        body,
        in_specs=ins,
        out_specs=[VMEM] * near + [HBM] * distant,
        out_shape=outs,
        scratch_shapes=scratch,
        compiler_params=pltpu.CompilerParams(vmem_limit_bytes=room * 2**20),
        cost_estimate=estimate,
        name=name,
    )


class Streams:
    def __init__(self, total, sems, arrived=(), leaving=()):
        self.bases = range(0, total, TILE)
        self.sems = sems
        self.arriving = [(far_ref, near_ref) for far_ref, near_ref in arrived]
        self.leaving = [(near_ref, far_ref) for near_ref, far_ref in leaving]

    def copies(self, base, pairs, first):
        block = pl.ds(base, TILE)
        return [
            pltpu.make_async_copy(a.at[block, :], b.at[block, :], self.sems.at[first + n, base // TILE])
            for n, (a, b) in enumerate(pairs)
        ]

    def start(self, backwards=False):
        for base in reversed(self.bases) if backwards else self.bases:
            for c in self.copies(base, self.arriving, 0):
                c.start()

    def wait(self, base):
        for c in self.copies(base, self.arriving, 0):
            c.wait()

    def leave(self, base):
        for c in self.copies(base, self.leaving, len(self.arriving)):
            c.start()

    def finish(self):
        for base in self.bases:
            for c in self.copies(base, self.leaving, len(self.arriving)):
                c.wait()


def stream_sems(total, count):
    return pltpu.SemaphoreType.DMA((count, total // TILE))


def recurrent_project(parts, cut, dims):
    total, width, half, size = dims
    wide = 2 * width + half
    packed = wide + LANES

    def kernel(place_ref, tok_far, *refs):
        left_pieces, right_pieces = refs[:parts], refs[parts : 2 * parts]
        inner, gate, forget, gains, normed, inner_low, gate_low, w_far, w, tok, sems, tile_sems = refs[2 * parts :]
        me = place_ref[0]
        small = [v.at[:, pl.ds(wide - cut, LANES)] for v in right_pieces]
        large = [v.at[:, pl.ds(0, wide - cut)] for v in right_pieces]
        ahead = piece_copies(me, small, w, pl.ds(wide, LANES), sems, 0)
        behind = piece_copies(me, left_pieces, w, pl.ds(0, cut), sems, parts)
        behind += piece_copies(me, large, w, pl.ds(cut, wide - cut), sems, 2 * parts)
        io = Streams(total, tile_sems, [(tok_far, tok)])
        keep = pltpu.make_async_copy(w, w_far, sems.at[3 * parts])
        for c in ahead:
            c.start()
        io.start()
        for c in behind:
            c.start()
        for c in ahead:
            c.wait()
        gains[...] = jnp.transpose(w[:, wide:packed].astype(F32))[0:8, :]

        def project(base):
            block = pl.ds(base, TILE)
            io.wait(base)
            gain = gains[0:1, :]

            def norm(at, rows):
                there = span(base + at, rows)
                x = tok[there, :]
                scale = lax.rsqrt(jnp.mean(x * x, axis=-1, keepdims=True) + 1e-06)
                normed[there, :] = (x * scale * gain).astype(BF)

            chunks("norm", norm)

            @pl.when(base == 0)
            def _():
                for c in behind:
                    c.wait()
                keep.start()

            value = normed[block, :]
            for n in range(0, width, 256):
                lanes = slice(n, n + 256)
                made = mm(value, w[:, n : n + 256])
                inner[block, lanes] = made
                inner_low[block, lanes] = made.astype(BF)
                made = mm(value, w[:, width + n : width + n + 256])
                gate[block, lanes] = made
                gate_low[block, lanes] = made.astype(BF)
            forget[block, :] = mm(value, w[:, 2 * width : wide])

        tiles_of(total, project)
        keep.wait()

    return kernel_call(
        kernel,
        "recurrent_project",
        [SMEM] + [HBM] + [ANY] * (2 * parts),
        [
            struct((total, width), F32),
            struct((total, width), F32),
            struct((total, half), F32),
            struct((8, width), F32),
            struct((total, width), BF),
            struct((total, width), BF),
            struct((total, width), BF),
            struct((width, packed), BF),
        ],
        [
            pltpu.VMEM((width, packed), BF),
            pltpu.VMEM((total, width), F32),
            pltpu.SemaphoreType.DMA((3 * parts + 1,)),
            stream_sems(total, 1),
        ],
        10,
        cost(6, 24 * total * width),
        distant=1,
    )


def recurrent_mix(dims):
    total, width, half, size = dims

    def kernel(len_ref, inner, gate, forget, gains, low_ref, *refs):
        tables, (gated, state, prod, keep, carry, ends) = refs[:4], refs[4:]
        first = len_ref[0, 0]
        second = first + len_ref[0, 1]
        carry[...] = jnp.concatenate([jnp.zeros((16, half), F32), jnp.ones((8, half), F32)], axis=0)
        bound = low_ref[0:1, :]

        def chain_tile(base):
            def sources(at, rows):
                here = pl.ds(at, rows)
                there = span(base + at, rows)
                time = slot_times(base + at, rows, total)
                start = (time == 0) | (time == first) | (time == second)
                rest = (1.0 - bound) * (1.0 - sigmoid(forget[there, :]))
                keep[here, :] = jnp.where(start, 0.0, 1.0 - rest)
                re = inner[there, 0:half]
                im = inner[there, half:width]
                re = rest * re * sigmoid(re)
                im = rest * im * sigmoid(im)
                c, s = turned(tables, base + at, rows)
                state[there, 0:half] = c * re + s * im
                state[there, half:width] = c * im - s * re

            chunks("sources", sources)

            def scan(j, held):
                re, im, p = held
                there = span(base + j * 8, 8)
                k = keep[span(j * 8, 8), :]
                re = k * re + state[there, 0:half]
                im = k * im + state[there, half:width]
                p = k * p
                state[there, 0:half] = re
                state[there, half:width] = im
                prod[there, :] = p
                return re, im, p

            held = (carry[0:8, :], carry[8:16, :], carry[16:24, :])
            held = lax.fori_loop(0, TILE // 8, scan, held, unroll=8)
            carry[0:8, :], carry[8:16, :], carry[16:24, :] = held

        tiles_of(total, chain_tile)
        p = carry[16:24, :]
        for h in (0, 8):
            z = carry[h : h + 8, :]
            rows = [jnp.zeros((1, half), F32)]
            for c in range(1, CHAINS):
                rows.append(z[c - 1 : c, :] + p[c - 1 : c, :] * rows[-1])
            ends[h : h + 8, :] = jnp.concatenate(rows, axis=0)
        gain = gains[1:2, :]

        def mix_tile(base):
            def mix(at, rows):
                there = span(base + at, rows)
                low = lax.broadcasted_iota(jnp.int32, (rows, LANES), 1) < LANES // 2
                p = prod[there, :]
                re = state[there, 0:half] + p * repeat(ends[0:8, :], rows)
                im = state[there, half:width] + p * repeat(ends[8:16, :], rows)
                state[there, 0:half] = re
                state[there, half:width] = im
                c, s = turned(tables, base + at, rows)
                mixed = strips(c * re - s * im) + strips(c * im + s * re)
                grouped, _ = centre_and_scale(mixed, low, size)
                for n in range(len(grouped)):
                    lanes = slice(n * LANES, (n + 1) * LANES)
                    opened = grouped[n] * gain[:, lanes] * sigmoid(gate[there, lanes])
                    gated[there, lanes] = opened.astype(BF)

            chunks("mix", mix)

        tiles_of(total, mix_tile)

    return kernel_call(
        kernel,
        "recurrent_mix",
        [SMEM] + [VMEM] * 9,
        [struct((total, width), BF), struct((total, width), F32)],
        [
            pltpu.VMEM((total, half), F32),
            pltpu.VMEM((TILE, half), F32),
            pltpu.VMEM((24, half), F32),
            pltpu.VMEM((16, half), F32),
        ],
        5,
        cost(8, 20 * total * width),
    )


def ffn_up(parts, cut, dims, ff):
    total, width, half, size = dims
    packed = width + 2 * ff

    def kernel(me_ref, gated, gains, tok_far, *refs):
        left_pieces, right_pieces = refs[:parts], refs[parts : 2 * parts]
        middle, ffn_in, to_left, to_right, hidden, w, tok, sems, tile_sems = refs[2 * parts :]
        me = me_ref[0]
        first = [v.at[:, pl.ds(0, width)] for v in left_pieces]
        then = [v.at[:, pl.ds(width, cut - width)] for v in left_pieces]
        ahead = piece_copies(me, first, w, pl.ds(0, width), sems, 0)
        behind = piece_copies(me, then, w, pl.ds(width, cut - width), sems, parts)
        behind += piece_copies(me, right_pieces, w, pl.ds(cut, packed - cut), sems, 2 * parts)
        for c in ahead:
            c.start()
        io = Streams(total, tile_sems, [(tok_far, tok)])
        io.start()
        for c in behind:
            c.start()
        gain = gains[2:3, :]
        for c in ahead:
            c.wait()

        def enter(base):
            block = pl.ds(base, TILE)
            io.wait(base)
            middle[block, :] = tok[block, :] + mm(gated[block, :], w[:, 0:width])

            def norm(at, rows):
                there = span(base + at, rows)
                x = middle[there, :]
                scale = lax.rsqrt(jnp.mean(x * x, axis=-1, keepdims=True) + 1e-06)
                ffn_in[there, :] = (x * scale * gain).astype(BF)

            chunks("norm", norm)

        tiles_of(total, enter)
        for c in behind:
            c.wait()

        def expand(base):
            block = pl.ds(base, 2 * TILE)
            value = ffn_in[block, :]
            for c in range(0, ff, 256):
                lanes = slice(c, c + 256)
                l = mm(value, w[:, width + c : width + c + 256])
                r = mm(value, w[:, width + ff + c : width + ff + c + 256])
                g = sigmoid(l)
                u = l * g
                to_right[block, lanes] = u.astype(BF)
                to_left[block, lanes] = ((g + u - u * g) * r).astype(BF)
                hidden[block, lanes] = (u * r).astype(BF)

        tiles_of(total, expand, tile=2 * TILE)

    return kernel_call(
        kernel,
        "ffn_up",
        [SMEM, VMEM, VMEM] + [HBM] + [ANY] * (2 * parts),
        [
            struct((total, width), F32),
            struct((total, width), BF),
            struct((total, ff), BF),
            struct((total, ff), BF),
            struct((total, ff), BF),
            struct((width, packed), BF),
        ],
        [
            pltpu.VMEM((total, width), F32),
            pltpu.SemaphoreType.DMA((3 * parts,)),
            stream_sems(total, 1),
        ],
        6,
        cost(10, 24 * total * width),
    )


def ffn_turn(parts, cut, dims, ff):
    total, width, half, size = dims

    def kernel(me_ref, grad, to_left, to_right, hidden, middle, *refs):
        left_pieces, right_pieces = refs[:parts], refs[parts : 2 * parts]
        d_left, d_right, w, hidden_far, middle_far, sems = refs[2 * parts :]
        me = me_ref[0]
        copies = piece_copies(me, left_pieces, w, pl.ds(0, cut), sems, 0)
        copies += piece_copies(me, right_pieces, w, pl.ds(cut, width - cut), sems, parts)
        for c in copies:
            c.start()
        for c in copies:
            c.wait()
        leaving = [
            pltpu.make_async_copy(hidden, hidden_far, sems.at[2 * parts]),
            pltpu.make_async_copy(middle, middle_far, sems.at[2 * parts + 1]),
        ]
        for c in leaving:
            c.start()

        def turn(base):
            block = pl.ds(base, TILE)
            value = grad[block, :]
            for c in range(0, ff, 256):
                lanes = slice(c, c + 256)
                dh = mm_nt(value, w[c : c + 256, :])
                d_right[block, lanes] = (dh * to_right[block, lanes].astype(F32)).astype(BF)
                d_left[block, lanes] = (dh * to_left[block, lanes].astype(F32)).astype(BF)

        tiles_of(total, turn)
        for c in leaving:
            c.wait()

    return kernel_call(
        kernel,
        "ffn_turn",
        [SMEM] + [VMEM] * 5 + [ANY] * (2 * parts),
        [
            struct((total, ff), BF),
            struct((total, ff), BF),
            struct((ff, width), BF),
            struct((total, ff), BF),
            struct((total, width), F32),
        ],
        [pltpu.SemaphoreType.DMA((2 * parts + 2,))],
        3,
        cost(5, 20 * total * width),
        distant=2,
    )


def ffn_out(dims, ff):
    total, width, half, size = dims

    def kernel(len_ref, hidden_far, middle_far, w, act_far, hidden, middle, act, tile_sems):
        second = len_ref[0, 0] + len_ref[0, 1]
        io = Streams(total, tile_sems, [(hidden_far, hidden), (middle_far, middle)], [(act, act_far)])
        io.start()

        def tile(base):
            block = pl.ds(base, TILE)
            io.wait(base)
            valid = (slot_times(base, TILE, total) < second).astype(F32)
            act[block, :] = valid * (middle[block, :] + mm(hidden[block, :], w[...]))
            io.leave(base)

        tiles_of(total, tile)
        io.finish()

    return kernel_call(
        kernel,
        "ffn_out",
        [SMEM] + [HBM] * 2 + [VMEM],
        [struct((total, width), F32)],
        [
            pltpu.VMEM((total, ff), BF),
            pltpu.VMEM((total, width), F32),
            pltpu.VMEM((total, width), F32),
            stream_sems(total, 3),
        ],
        11,
        cost(6, 10 * total * width),
        distant=1,
    )


def products_of(me, refs, counts, products, slot, parts, aligned, store):
    for n, (l, r, begin, end) in enumerate(products):
        if aligned:
            size = refs[l].shape[1] // parts
            left = refs[l][:, pl.ds(pl.multiple_of((me ^ slot) * size, LANES), size)]
        else:
            left = refs[l][...]
        for c in range(begin, end, 512):
            stop = min(c + 512, end)
            store(n, c - begin, stop - begin, mm_tn(left, refs[counts + r][:, c:stop]))


def prepared(me, lefts, slot, parts):
    sizes = [v.shape[1] // parts for v in lefts]
    aligned = all(size % LANES == 0 for size in sizes)
    if not aligned:
        lefts = [
            lax.dynamic_slice_in_dim(v, (me[0] ^ slot) * size, size, axis=1) for v, size in zip(lefts, sizes)
        ]
    return lefts, sizes, aligned


def grads_cost(lefts, sizes, products):
    flops = sum(2 * lefts[l].shape[0] * sizes[l] * (end - begin) for l, r, begin, end in products)
    return cost(flops / 0.6e9, flops // 256)


def weight_grads(name, me, lefts, rights, products, slot, parts):
    lefts, sizes, aligned = prepared(me, lefts, slot, parts)
    given = len(lefts) + len(rights)

    def kernel(me_ref, *refs):
        def store(n, begin, end, value):
            refs[given + n][:, begin:end] = value.astype(BF)

        products_of(me_ref[0], refs, len(lefts), products, slot, parts, aligned, store)

    outs = [struct((sizes[l], end - begin), BF) for l, r, begin, end in products]
    return kernel_call(
        kernel, name, [SMEM] + [VMEM] * given, outs, [], 8, grads_cost(lefts, sizes, products)
    )(me, *lefts, *rights)


def split_grads(name, place, axis, lefts, rights, products, swapped, parts, outer, rows, sums=None):
    lefts, sizes, aligned = prepared(place, lefts, 0, parts)
    given = len(lefts) + len(rights)
    base = rows * outer * (2 if axis == 3 else 4)
    inner = base // (2 * outer)
    places, width = [], 0
    for l, r, begin, end in products:
        places.append(width)
        width += (end - begin) * (sizes[l] // base)
    count = len(products)
    extra = [] if sums is None else [sums]
    flat = [v for arrays in swapped for v in arrays]
    per = len(flat) // max(parts - 1, 1)

    def kernel(place_ref, *refs):
        others = refs[given : given + per * (parts - 1)]
        tail = refs[given + per * (parts - 1) :]
        send, kept = tail[len(extra) : len(extra) + 2]
        high_is_mine = place_ref[axis] == 1

        def store(n, begin, end, value):
            for k in range(parts - 1):
                block, at = (k * per + n, 0) if per == count else (k, places[n])
                value = value + others[block][:, at + begin : at + end].astype(F32)
            times = value.shape[0] // base
            value = value.reshape(outer, 2, inner // rows, times, rows, end - begin)
            for t in range(times):
                to = places[n] + t * (products[n][3] - products[n][2]) + begin
                low = value[:, 0, :, t].reshape(outer, inner, end - begin)
                high = value[:, 1, :, t].reshape(outer, inner, end - begin)
                send[:, :, to : to + end - begin] = jnp.where(high_is_mine, low, high).astype(BF)
                kept[:, :, to : to + end - begin] = jnp.where(high_is_mine, high, low)

        products_of(place_ref[0], refs, len(lefts), products, 0, parts, aligned, store)
        if extra:
            held = tail[-1]
            held[place_ref[0]] = tail[0][...]
            for k in range(1, parts):
                block = others[(k - 1) * per]
                held[place_ref[0] ^ k] = unpack(block[0:32, block.shape[1] - LANES :])
            value = held[0]
            for k in range(1, parts):
                value = value + held[k]
            columns = slice(width, width + LANES)
            send[:, :, columns] = jnp.zeros((outer, inner, LANES), BF)
            kept[:, :, columns] = jnp.zeros((outer, inner, LANES), F32)
            send[0, :, columns] = pack(value)
            kept[0, 0:8, columns] = value

    shape = (outer, inner, width + LANES * len(extra))
    return kernel_call(
        kernel,
        name,
        [SMEM] + [VMEM] * (given + len(flat) + len(extra)),
        [struct(shape, BF), struct(shape, F32)],
        [pltpu.VMEM((parts, 8, LANES), F32)] * len(extra),
        8,
        grads_cost(lefts, sizes, products),
    )(place, *lefts, *rights, *flat, *extra)


def middle_back(dims, ff):
    total, width, half, size = dims
    packed = width + 2 * ff

    def kernel(len_ref, d_left, d_right, middle, gains, low_ref, state, gate, forget, w, *refs):
        tables, cot_far, refs = refs[:4], refs[4], refs[5:]
        d_mid, d_middle, d_gate, local, prod, cot, hold, keep, carry, tile_sems = refs
        first = len_ref[0, 0]
        second = first + len_ref[0, 1]
        bound = low_ref[0:1, :]
        io = Streams(total, tile_sems, [(cot_far, cot)])
        io.start(backwards=True)
        ffn_gain = gains[2:3, :]
        gain = gains[1:2, :]

        def keeps(base, rows, value):
            time = slot_times(base, rows, total)
            start = (time == 0) | (time == first) | (time == second)
            return jnp.where(start, 0.0, bound + (1.0 - bound) * sigmoid(value))

        k = keeps(0, 8, forget[0:8, :])
        carry[0:16, :] = jnp.zeros((16, half), F32)
        carry[16:24, :] = jnp.ones((8, half), F32)
        carry[24:32, :] = jnp.concatenate([k[1:8, :], jnp.zeros((1, half), F32)], axis=0)

        def enter(base):
            block = pl.ds(base, TILE)
            hold[...] = mm_nt(d_left[block, :], w[:, width : width + ff]) + mm_nt(
                d_right[block, :], w[:, width + ff : packed]
            )
            io.wait(base)

            def norm_back(at, rows):
                here = pl.ds(at, rows)
                there = span(base + at, rows)
                valid = (slot_times(base + at, rows, total) < second).astype(F32)
                x = middle[there, :]
                scale = lax.rsqrt(jnp.mean(x * x, axis=-1, keepdims=True) + 1e-06)
                d = hold[here, :]
                unit = x * scale
                d = d * ffn_gain
                back = scale * (d - unit * jnp.mean(d * unit, axis=-1, keepdims=True))
                back = back + valid * cot[there, :]
                d_middle[there, :] = back
                d_mid[there, :] = back.astype(BF)

            chunks("norm_back", norm_back)

        def tile(base):
            enter(base)
            block = pl.ds(base, TILE)
            hold[...] = mm_nt(d_mid[block, :], w[:, 0:width])

            def through(at, rows):
                here = pl.ds(at, rows)
                there = span(base + at, rows)
                low = lax.broadcasted_iota(jnp.int32, (rows, LANES), 1) < LANES // 2
                re, im = state[there, 0:half], state[there, half:width]
                c, s = turned(tables, base + at, rows)
                mixed = strips(c * re - s * im) + strips(c * im + s * re)
                grouped, scales = centre_and_scale(mixed, low, size)
                back = []
                for n in range(len(grouped)):
                    lanes = slice(n * LANES, (n + 1) * LANES)
                    opened = sigmoid(gate[there, lanes].astype(F32))
                    d = hold[here, lanes]
                    part = d * grouped[n] * opened
                    d_gate[there, lanes] = (part * gain[:, lanes] * (1.0 - opened)).astype(BF)
                    back.append(d * opened * gain[:, lanes])
                mean = group_spread(group_means(back, low, size), low)
                along = group_spread(group_means([b * g for b, g in zip(back, grouped)], low, size), low)
                back = [t * (b - m - g * a) for t, b, m, g, a in zip(scales, back, mean, grouped, along)]
                for n in range(3):
                    lanes = slice(n * LANES, (n + 1) * LANES)
                    cn, sn = c[:, lanes], s[:, lanes]
                    local[there, lanes] = cn * back[n] + sn * back[n + 3]
                    local[there, half + n * LANES : half + (n + 1) * LANES] = cn * back[n + 3] - sn * back[n]

            chunks("through", through)

            def kept(at, rows):
                there = span(base + at, rows)
                keep[pl.ds(at, rows), :] = keeps(base + at, rows, forget[there, :])

            chunks("kept", kept)

            def scan(i, held):
                re, im, p, k = held
                at = (TILE // 8 - 1 - i) * 8
                there = span(base + at, 8)
                re = k * re + local[there, 0:half]
                im = k * im + local[there, half:width]
                p = k * p
                local[there, 0:half] = re
                local[there, half:width] = im
                prod[there, :] = p
                return re, im, p, keep[span(at, 8), :]

            held = (carry[0:8, :], carry[8:16, :], carry[16:24, :], carry[24:32, :])
            held = lax.fori_loop(0, TILE // 8, scan, held, unroll=8)
            carry[0:8, :], carry[8:16, :], carry[16:24, :], carry[24:32, :] = held

        tiles_of(total, tile, backwards=True)

    return kernel_call(
        kernel,
        "middle_back",
        [SMEM] + [VMEM] * 13 + [HBM],
        [
            struct((total, width), BF),
            struct((total, width), F32),
            struct((total, width), BF),
            struct((total, width), F32),
            struct((total, half), F32),
        ],
        [
            pltpu.VMEM((total, width), F32),
            pltpu.VMEM((TILE, width), F32),
            pltpu.VMEM((TILE, half), F32),
            pltpu.VMEM((32, half), F32),
            stream_sems(total, 1),
        ],
        8,
        cost(19, 60 * total * width),
    )


def source_back(dims, parts, me, lefts, d_mid, shares, fine):
    total, width, half, size = dims
    wide = 2 * width + half
    given, sizes, aligned = [], None, True
    for slot in range(1, parts):
        made, sizes, aligned = prepared(me, lefts, slot, parts)
        given.append(list(made))
    if aligned:
        given = [list(lefts)] * max(parts - 1, 0)
        flat = list(lefts)
    else:
        flat = [v for made in given for v in made]
    products = [p for share in shares for p in share]
    count = len(shares)
    owner, widths = [], []
    for n, share in enumerate(shares):
        widths.append(0)
        for l, r, begin, end in share:
            owner.append((n, widths[n]))
            widths[n] += end - begin
    widths[0] += LANES if fine else 0

    def kernel(len_ref, me_ref, local, prod, d_gate, low_ref, state, forget, inner, *refs):
        tables, refs = refs[:4], refs[4:]
        left_refs, d_mid_ref, refs = refs[: len(flat)], refs[len(flat)], refs[len(flat) + 1 :]
        d_proj, sums = refs[:2]
        slots, (ends, acc) = refs[2 : 2 + count * (parts - 1)], refs[2 + count * (parts - 1) :]
        first = len_ref[0, 0]
        second = first + len_ref[0, 1]
        bound = low_ref[0:1, :]
        acc[...] = jnp.zeros_like(acc)
        p = prod[0:8, :]
        for h in (0, 1):
            z = local[0:8, h * half : (h + 1) * half]
            made = [jnp.zeros((1, half), F32)]
            for c in range(CHAINS - 2, -1, -1):
                made.append(z[c + 1 : c + 2, :] + p[c + 1 : c + 2, :] * made[-1])
            ends[8 * h : 8 * h + 8, 0:half] = jnp.concatenate(made[::-1], axis=0)
        old = state[total - 8 : total, :]
        ends[16:24, :] = jnp.concatenate([old[7:8, :], old[0:7, :]], axis=0)

        def tile(base):
            def back(at, rows):
                row = base + at
                there = span(row, rows)
                p = prod[there, :]
                re = local[there, 0:half] + p * repeat(ends[0:8, 0:half], rows)
                im = local[there, half:width] + p * repeat(ends[8:16, 0:half], rows)
                up = span(jnp.maximum(row - 8, 0), 8)
                stay = pl.ds(pl.multiple_of(row, 8), rows - 8)
                old_re = jnp.concatenate(
                    [jnp.where(row == 0, ends[16:24, 0:half], state[up, 0:half]), state[stay, 0:half]], axis=0
                )
                old_im = jnp.concatenate(
                    [jnp.where(row == 0, ends[16:24, half:width], state[up, half:width]), state[stay, half:width]],
                    axis=0,
                )
                time = slot_times(row, rows, total)
                start = (time == 0) | (time == first) | (time == second)
                sf = sigmoid(forget[there, :])
                rest = (1.0 - bound) * (1.0 - sf)
                turn = (1.0 - rest) * (im * old_re - re * old_im)
                acc[8:16, :] += fold(jnp.where(start, 0.0, turn))
                d_lam = jnp.where(start, 0.0, re * old_re + im * old_im)
                c, s = turned(tables, row, rows)
                d_re = c * re - s * im
                d_im = c * im + s * re
                for lane, d in ((0, d_re), (half, d_im)):
                    v = inner[there, lane : lane + half].astype(F32)
                    sv = sigmoid(v)
                    d_lam = d_lam - d * (v * sv)
                    d_proj[there, lane : lane + half] = (rest * d * (sv * (1.0 + v * (1.0 - sv)))).astype(BF)
                acc[0:8, :] += fold(d_lam * (1.0 - sf))
                d_proj[there, 2 * width : wide] = (d_lam * rest * sf).astype(BF)
                d_proj[there, width : 2 * width] = d_gate[there, :]

            chunks("source_back", back)

        tiles_of(total, tile)
        out = [jnp.sum(acc[8 * n : 8 * n + 8, :], axis=0, keepdims=True) for n in range(2)]
        out = strips(out[0]) + strips(out[1])
        sums[...] = jnp.concatenate(out + [jnp.zeros((8 - len(out), LANES), F32)], axis=0)
        for slot in range(1, parts):
            used = left_refs if aligned else left_refs[(slot - 1) * len(lefts) : slot * len(lefts)]

            def store(n, begin, end, value):
                share, at = owner[n]
                slots[(slot - 1) * count + share][:, at + begin : at + end] = value.astype(BF)

            products_of(
                me_ref[0], [*used, d_proj, d_mid_ref], len(lefts), products, slot, parts, aligned, store
            )
            if fine:
                block = slots[(slot - 1) * count]
                rest = jnp.zeros((block.shape[0] - 24, LANES), F32)
                carried = jnp.concatenate([pack(sums[...]).astype(F32), rest], axis=0)
                block[:, block.shape[1] - LANES :] = carried.astype(BF)

    outs = [struct((total, wide), BF), struct((8, LANES), F32)]
    outs += [struct((width // parts, n), BF) for n in widths] * (parts - 1)
    call = kernel_call(
        kernel,
        "source_back",
        [SMEM, SMEM] + [VMEM] * (12 + len(flat)),
        outs,
        [pltpu.VMEM((24, width), F32), pltpu.VMEM((16, half), F32)],
        6,
        cost(10, 40 * total * width),
    )

    def run(lengths, me, *arrays):
        d_proj, sums, *slots = call(lengths, me, *arrays, *flat, d_mid)
        return d_proj, sums, [slots[k * count : (k + 1) * count] for k in range(parts - 1)]

    return run


def input_back(dims):
    total, width, half, size = dims
    wide = 2 * width + half

    def kernel(order_ref, d_proj, gains, d_middle, tok_far, w_far, out, w, tok, hold, sem, tile_sems):
        weight = pltpu.make_async_copy(w_far, w, sem.at[0])
        weight.start()
        io = Streams(total, tile_sems, [(tok_far, tok)])
        io.start()
        gain = gains[0:1, :]
        weight.wait()

        def tile(base):
            hold[...] = mm_nt(d_proj[pl.ds(base, TILE), :], w[:, 0:wide])
            io.wait(base)

            def norm_back(at, rows):
                here = pl.ds(at, rows)
                there = span(base + at, rows)
                x = tok[there, :]
                scale = lax.rsqrt(jnp.mean(x * x, axis=-1, keepdims=True) + 1e-06)
                d = hold[here, :]
                unit = x * scale
                d = d * gain
                out[there, :] = d_middle[there, :] + scale * (d - unit * jnp.mean(d * unit, axis=-1, keepdims=True))

            chunks("norm_back", norm_back)

        tiles_of(total, tile)

    return kernel_call(
        kernel,
        "input_back",
        [SMEM, VMEM, VMEM, VMEM] + [HBM] * 2,
        [struct((total, width), F32)],
        [
            pltpu.VMEM((width, wide + LANES), BF),
            pltpu.VMEM((total, width), F32),
            pltpu.VMEM((TILE, width), F32),
            pltpu.SemaphoreType.DMA((1,)),
            stream_sems(total, 1),
        ],
        10,
        cost(7, 20 * total * width),
    )


def order_call(place, held, cut):
    rows, columns = held[0].shape
    deep = len(held)

    def kernel(place_ref, *refs):
        for k in range(deep):
            at = place_ref[1] ^ k
            refs[deep][at] = refs[k][:, 0:cut]
            refs[deep + 1][at] = refs[k][:, cut:columns]

    outs = [struct((deep, rows, cut), BF), struct((deep, rows, columns - cut), BF)]
    return kernel_call(kernel, "order_z", [SMEM] + [VMEM] * deep, outs, [], 2, cost(1, 4 * deep * rows * columns))(
        place, *held
    )


def join_call(place, axes, own, got):
    count = len(own)

    def kernel(place_ref, *refs):
        for n in range(count):
            bit = place_ref[axes[n]]
            refs[2 * count + n][:, pl.ds(bit, 1)] = refs[n][...][:, None]
            refs[2 * count + n][:, pl.ds(1 - bit, 1)] = refs[count + n][...][:, None]

    outs = [struct((v.shape[0], 2) + v.shape[1:], BF) for v in own]
    moved = sum(8 * v.size for v in own)
    return kernel_call(kernel, "join", [SMEM] + [VMEM] * (2 * count), outs, [], 2, cost(2, moved))(place, *own, *got)


def halve_call(place, axes, kept, got, carried):
    flat_kept = [v for share in kept for v in share]
    flat_got = [v for share in got for v in share]
    count = len(flat_kept)

    def kernel(place_ref, *refs):
        outs = refs[2 * count :]
        at = 0
        for n, share in enumerate(kept):
            bit = place_ref[axes[n]]
            begin = 0
            for v in share:
                end = begin + v.shape[-1]
                for out, half in ((outs[2 * n], 1 - bit), (outs[2 * n + 1], bit)):
                    value = refs[at][:, pl.ds(half, 1)] + refs[count + at][:, pl.ds(half, 1)].astype(F32)
                    out[:, :, begin:end] = value[:, 0].astype(out.dtype)
                at += 1
                begin = end
        if carried:
            columns = slice(flat_kept[0].shape[-1] - LANES, None)
            value = refs[0][0, 0, 0:8, columns] + unpack(refs[count][0, 0, :, columns])
            outs[0][0, :, columns] = pack(value)
            outs[1][0, 0:8, columns] = value

    outs = []
    for share in kept:
        shape = share[0].shape[:1] + share[0].shape[2:-1] + (sum(v.shape[-1] for v in share),)
        outs += [struct(shape, BF), struct(shape, F32)]
    moved = sum(10 * v.size for v in flat_kept)
    made = kernel_call(kernel, "halve", [SMEM] + [VMEM] * (2 * count), outs, [], 4, cost(3, moved))(
        place, *flat_kept, *flat_got
    )
    return [made[2 * n : 2 * n + 2] for n in range(len(kept))]


def deal_call(place, kept, got, carried):
    deep, rows = kept[0].shape[:2]
    widths = [v.shape[2] for v in kept]
    columns = sum(widths)
    widths[0] -= LANES if carried else 0

    def kernel(place_ref, *refs):
        begin = 0
        for n, width in enumerate(widths):
            for k in range(deep):
                at = place_ref[1] ^ k
                value = refs[n][at, :, 0:width] + refs[2 + n][at, :, 0:width].astype(F32)
                refs[4 + k][:, begin : begin + width] = value.astype(refs[4 + k].dtype)
            begin += width
        if carried:
            last = slice(widths[0], widths[0] + LANES)
            value = refs[0][0, 0:8, last] + unpack(refs[2][0, :, last])
            refs[4][:, begin:] = jnp.concatenate([value, jnp.zeros((rows - 8, LANES), F32)], axis=0)
            for k in range(1, deep):
                refs[4 + k][:, begin:] = pack(value)

    outs = [struct((rows, columns), F32 if k == 0 else BF) for k in range(deep)]
    return kernel_call(kernel, "deal_z", [SMEM] + [VMEM] * 4, outs, [], 4, cost(2, 10 * deep * rows * columns))(
        place, *kept, *got
    )


def finish_call(place, own, got, cuts, gains, carried):
    deep = len(got) + 1
    rows, columns = own.shape
    bounds = [0, *cuts, columns - (LANES if carried else 0)]
    pairs = list(zip(bounds[:-1], bounds[1:]))
    flat = [v for gain, weights in gains for v in (gain, *weights.values())]

    def kernel(place_ref, *refs):
        given = list(refs[deep : deep + len(flat)])
        outs = refs[deep + len(flat) :]
        for n, (a, b) in enumerate(pairs):
            value = refs[0][:, a:b]
            for k in range(1, deep):
                value = value + refs[k][:, a:b].astype(F32)
            outs[n][...] = value
        at = len(pairs)
        for gain, weights in gains:
            gain_ref = given.pop(0)
            total = jnp.zeros((rows, 1), F32)
            for n in weights:
                total = total + jnp.sum(given.pop(0)[...].astype(F32) * outs[n][...], axis=1, keepdims=True)
            shape = (rows, LANES)
            diagonal = lax.broadcasted_iota(jnp.int32, shape, 0) == lax.broadcasted_iota(jnp.int32, shape, 1)
            row = jnp.sum(jnp.where(diagonal, total, 0.0), axis=0, keepdims=True)
            outs[at][...] = (row[:, 0:rows] / gain_ref[...].astype(F32))[0]
            at += 1
        if carried:
            held = outs[-1]
            held[place_ref[1]] = refs[0][0:8, columns - LANES :]
            for k in range(1, deep):
                held[place_ref[1] ^ k] = unpack(refs[k][:, columns - LANES :])
            value = held[0]
            for k in range(1, deep):
                value = value + held[k]
            for n in range(2):
                strip = [value[3 * n + i : 3 * n + i + 1, :] for i in range(3)]
                outs[at + n][...] = jnp.concatenate(strip, axis=1)[0]

    outs = [struct((rows, b - a), F32) for a, b in pairs] + [struct((rows,), F32)] * len(gains)
    outs += [struct((3 * LANES,), F32)] * (2 * carried)
    scratch = [pltpu.VMEM((deep, 8, LANES), F32)] * carried
    return kernel_call(
        kernel, "finish", [SMEM] + [VMEM] * (deep + len(flat)), outs, scratch, 2, cost(2, 12 * rows * columns)
    )(place, own, *got, *flat)


class Exchange:
    def __init__(self, mesh, fine):
        self.parts = mesh.shape["dp"]
        self.count = mesh.shape["fsdp"]
        self.deep = self.count // 4
        me = lax.axis_index("fsdp")
        self.dp = lax.axis_index("dp")
        self.z = me // 4
        self.y_bit = (me // 2) % 2 == 1
        self.x_bit = me % 2 == 1
        self.fine = fine
        self.place = jnp.stack([self.dp, self.z, (me // 2) % 2, me % 2]).astype(jnp.int32)

    def swap(self, value, mask):
        return lax.ppermute(value, "fsdp", [(i, i ^ mask) for i in range(self.count)])

    def swap_dp(self, value, mask):
        return lax.ppermute(value, "dp", [(i, i ^ mask) for i in range(self.parts)])

    def send_z(self, shard, k):
        return self.swap(shard, 4 * k)

    def order_z(self, held, cut):
        if self.fine:
            return order_call(self.place, held, cut)
        step = 1
        while step < self.deep:
            bit = (self.z // step) % 2 == 1
            held = [jnp.where(bit, held[k ^ step], held[k]) for k in range(self.deep)]
            step *= 2
        stack = jnp.stack(held)
        return [stack[:, :, :cut], stack[:, :, cut:]]

    def send_first(self, shares):
        return [self.swap(shares[0], 1), self.swap(shares[1], 2)]

    def join_first(self, shares, got):
        if self.fine:
            return join_call(self.place, (3, 2), shares, got)
        out = []
        for own, other, bit in zip(shares, got, (self.x_bit, self.y_bit)):
            out.append(jnp.stack([jnp.where(bit, other, own), jnp.where(bit, own, other)], axis=1))
        return out

    def send_second(self, shares):
        return [self.swap(shares[0], 2), self.swap(shares[1], 1)]

    def join_second(self, shares, got):
        if self.fine:
            flat = [v.reshape((-1,) + v.shape[2:]) for v in (shares[1], got[1])]
            made = join_call(self.place, (2, 3), [shares[0], flat[0]], [got[0], flat[1]])
            return [v.reshape(-1, v.shape[-1]) for v in made]
        out = []
        for own, other, bit, place in zip(shares, got, (self.y_bit, self.x_bit), (1, 2)):
            v = jnp.stack([jnp.where(bit, other, own), jnp.where(bit, own, other)], axis=place)
            out.append(v.reshape(-1, v.shape[-1]))
        return out

    def gather_dp(self, shares):
        return [[v] + [self.swap_dp(v, k) for k in range(1, self.parts)] for v in shares]

    def cut_rows(self, own, swapped, outer, bit, rows):
        columns = []
        for n, value in enumerate(own):
            value = value.astype(F32)
            for arrays in swapped:
                value = value + arrays[n].astype(F32)
            value = value.reshape(self.count, -1, rows, value.shape[1])
            columns += [value[:, i] for i in range(value.shape[1])]
        total = jnp.concatenate(columns, axis=-1)
        total = total.reshape(outer, 2, -1, total.shape[-1])
        low, high = total[:, 0], total[:, 1]
        return jnp.where(bit, low, high).astype(BF), jnp.where(bit, high, low)

    def halves(self, total, bit):
        low, high = total[:, 0], total[:, 1]
        return jnp.where(bit, low, high).astype(BF), jnp.where(bit, high, low)

    def halve(self, kept, got, carried=False):
        kept = [[v.reshape(self.deep, 2, -1, v.shape[-1]) for v in share] for share in kept]
        got = [[g.reshape(k.shape) for g, k in zip(*pair)] for pair in zip(got, kept)]
        if self.fine:
            return halve_call(self.place, (2, 3), kept, got, carried)
        totals = [
            jnp.concatenate([k + g.astype(F32) for k, g in zip(*pair)], axis=-1) for pair in zip(kept, got)
        ]
        return [self.halves(total, bit) for total, bit in zip(totals, (self.y_bit, self.x_bit))]

    def send_halves(self, cuts):
        return [c[1] for c in cuts], [self.swap(cuts[0][0], 2), self.swap(cuts[1][0], 1)]

    def deal_z(self, kept, got, carried=False):
        if self.fine:
            own, *others = deal_call(self.place, kept, got, carried)
            return own, others
        total = jnp.concatenate([k + g.astype(F32) for k, g in zip(kept, got)], axis=-1)
        own, *others = [lax.dynamic_index_in_dim(total, self.z ^ k, 0, keepdims=False) for k in range(self.deep)]
        return own, [v.astype(BF) for v in others]

    def send_parts(self, others):
        return [self.swap(v, 4 * k) for k, v in enumerate(others, 1)]

    def finish_z(self, own, got, cuts, gains, carried=False):
        if self.fine:
            return finish_call(self.place, own, got, cuts, gains, carried)
        for v in got:
            own = own + v.astype(F32)
        made = jnp.split(own, cuts, axis=1)
        for gain, weights in gains:
            total = sum(jnp.sum(w.astype(F32) * made[n], axis=1) for n, w in weights.items())
            made.append(total / gain[0].astype(F32))
        return made

    def total(self, value):
        for k in range(self.parts.bit_length() - 1):
            value = value + self.swap_dp(value, 1 << k)
        for k in range(self.count.bit_length() - 1):
            value = value + self.swap(value, 1 << k)
        return value


def after(value, *others):
    return lax.optimization_barrier((value, *others))[0]


def to_chains(value, lengths=None):
    rows, columns = value.shape
    length = rows // CHAINS
    parts = range(columns // LANES)
    masked = 0 if lengths is None else 1

    def kernel(*refs):
        source = refs[masked]
        low, (out, natural, kept, sems) = refs[masked + 1 : 2 * masked + 1], refs[2 * masked + 1 :]
        arriving = [
            pltpu.make_async_copy(source.at[:, pl.ds(n * LANES, LANES)], natural.at[n], sems.at[0, n]) for n in parts
        ]
        leaving = [
            pltpu.make_async_copy(kept.at[n], out.at[:, pl.ds(n * LANES, LANES)], sems.at[1, n]) for n in parts
        ]
        for c in arriving:
            c.start()
        if masked:
            valid = (slot_times(0, rows, rows) < refs[0][0, 0] + refs[0][0, 1]).astype(F32)
        for n in parts:
            arriving[n].wait()

            def move(j, carry):
                kept[n, span(j * CHAINS, CHAINS), :] = natural[n, pl.ds(j, CHAINS, stride=length), :]
                return carry

            lax.fori_loop(0, length, move, 0, unroll=16)
            leaving[n].start()
            if masked:
                low[0][:, n * LANES : (n + 1) * LANES] = (valid * kept[n]).astype(BF)
        for c in leaving:
            c.wait()

    place = pltpu.VMEM((columns // LANES, rows, LANES), F32)
    made = kernel_call(
        kernel,
        "to_chains",
        [SMEM] * masked + [HBM],
        [struct((rows, columns), BF)] * masked + [struct((rows, columns), F32)],
        [place, place, pltpu.SemaphoreType.DMA((2, columns // LANES))],
        8,
        cost(4, 8 * rows * columns),
        distant=1,
    )(*([lengths] * masked), *far(value))
    return made if masked else made[0]


def from_chains(value):
    rows, columns = value.shape
    return value.reshape(rows // CHAINS, CHAINS, columns).transpose(1, 0, 2).reshape(rows, columns)


def turns(phase, rows):
    length = rows // CHAINS
    inside = jnp.arange(length, dtype=F32)[:, None] * phase
    outside = (jnp.arange(CHAINS, dtype=F32) * length)[:, None] * phase
    return [jnp.cos(inside), jnp.sin(inside), jnp.cos(outside), jnp.sin(outside)]


def build(mesh):
    def per_device(
        tokens,
        lengths,
        w_input,
        w_forget,
        w_gate,
        w_output,
        w_up_gate,
        w_up,
        w_down,
        norm_gain,
        group_gain,
        ffn_gain,
        lower_bound,
        phase,
        cotangent,
    ):
        ex = Exchange(mesh, w_input.shape[0] % 24 == 0)
        parts = ex.parts
        total, width = tokens.shape
        half = lower_bound.shape[0]
        ff = w_up.shape[1]
        dims = (total, width, half, width // GROUPS)
        shard = w_input.shape[0]

        columns = jnp.stack([norm_gain, group_gain, ffn_gain], axis=1)
        columns = jnp.pad(columns, ((0, 0), (0, LANES - 3)))
        pack1 = jnp.concatenate([w_input, w_gate, w_forget, columns], axis=1)
        pack1, tokens, rest = after((pack1, tokens, [w_output, w_up_gate, w_up]))
        pack2 = jnp.concatenate(rest, axis=1)
        cut1, cut2, cut3 = pack1.shape[1] // 2, pack2.shape[1] // 2, width // 2

        others = range(1, ex.deep)
        one = [pack1] + [ex.send_z(pack1, k) for k in others]
        one, pack2, ex.place, tokens = after((one, pack2, ex.place, tokens))
        tok = to_chains(tokens)
        one = ex.order_z(one, cut1)
        got = ex.send_first(one)
        two = [pack2] + [ex.send_z(pack2, k) for k in others[:2]]
        one, got, two, tok, phase, lower_bound = after((one, got, two, tok, phase, lower_bound))
        tables = turns(phase, total)
        low = jnp.broadcast_to(lower_bound, (8, half))
        one = ex.join_first(one, got)
        got = ex.send_second(one)
        two += [ex.send_z(two[0], k) for k in others[2:]]
        one, got, two, tables, low = after((one, got, two, tables, low))
        one = ex.gather_dp(ex.join_second(one, got))
        two = ex.order_z(two, cut2)
        got = ex.send_first(two)
        (tok,) = far(tok)
        inner, gate, forget, gains, normed, inner_low, gate_low, w_one = recurrent_project(parts, cut1, dims)(
            ex.place, tok, *one[0], *one[1]
        )
        two, got, gains, w_down, cotangent = after((two, got, gains, w_down, cotangent))
        grad, cot = to_chains(cotangent, lengths)
        two = ex.join_first(two, got)
        got = ex.send_second(two)
        three = [w_down] + [ex.send_z(w_down, k) for k in others]
        gated, state = recurrent_mix(dims)(lengths, inner, gate, forget, gains, low, *tables)
        three, gated = after((three, gated))
        three = ex.order_z(three, cut3)
        late = ex.send_first(three)
        two, got, three, late, gated, cot, grad = after((two, got, three, late, gated, cot, grad))
        two = ex.gather_dp(ex.join_second(two, got))
        three = ex.join_first(three, late)
        late = ex.send_second(three)
        (cot,) = far(cot)
        middle, ffn_in, to_left, to_right, hidden, w_two = ffn_up(parts, cut2, dims, ff)(
            ex.place, gated, gains, tok, *two[0], *two[1]
        )
        turn = (ex.place, lengths)
        three, late, ffn_in = after((three, late, ffn_in))
        three, turn = after((ex.join_second(three, late), turn))
        three = ex.gather_dp(three)
        fold_rows = ff // width

        def last_grads(name, n, turn, lefts, rights, products, swapped, sums=None):
            outer, bit = ((2 * ex.deep, ex.x_bit), (ex.deep, ex.y_bit))[n]
            if ex.fine:
                return split_grads(
                    name, turn[0], 3 - n, lefts, rights, products, swapped, parts, outer, shard, sums
                )
            made = weight_grads(name, turn[0], lefts, rights, products, 0, parts)
            return ex.cut_rows(made, swapped, outer, bit, shard)

        def grads_of(name, turn, lefts, rights, products):
            swapped = []
            for k in range(1, parts):
                made = weight_grads(name, turn[0], lefts, rights, products, k, parts)
                made, turn = after((made, turn))
                swapped.append([ex.swap_dp(v, k) for v in made])
            return swapped, turn

        halves = [(0, 0, 0, cut3), (0, 0, cut3, width)]
        swapped_down, turn = grads_of("down_grads", turn, [hidden], [grad], halves)
        d_left, d_right, w_three, hidden_far, middle_far = ffn_turn(parts, cut3, dims, ff)(
            turn[0], grad, to_left, to_right, hidden, middle, *three[0], *three[1]
        )
        d_left, swapped_down, turn = after((d_left, swapped_down, turn))
        swapped = []
        for n, right in enumerate((d_left, d_right)):
            made, turn = grads_of("up_grads", turn, [ffn_in], [right], [(0, 0, 0, ff)])
            swapped.append([up + down[n : n + 1] for up, down in zip(made, swapped_down)])
        kept, got = [], []
        for n, right in enumerate((d_left, d_right)):
            products = [(0, 0, 0, ff), (1, 1) + halves[n][2:]]
            send, keep = last_grads("ffn_grads", n, turn, [ffn_in, hidden], [right, grad], products, swapped[n])
            send, keep, turn = after((send, keep, turn))
            kept.append([keep])
            got.append([ex.swap(send, n + 1)])
        d_mid, d_middle, d_gate, local, prod = middle_back(dims, ff)(
            turn[1], d_left, d_right, middle, gains, low, state, gate_low, forget, w_two, *tables, cot
        )
        wide = 2 * width + half
        shares = [[(0, 0, 0, width), (0, 0, 2 * width, wide)], [(0, 0, 0, width), (1, 1, 0, width)]]
        local, turn = after((local, turn))
        swapped_b, turn = grads_of("recurrent_grads", turn, [normed, gated], [d_gate, d_mid], shares[1])
        kept, got, turn = after((kept, got, turn))
        cuts, turn = after((ex.halve(kept, got), turn))
        kept, got = ex.send_halves(cuts)
        d_proj, sums, made = source_back(dims, parts, ex.place, [normed], d_mid, shares[:1], ex.fine)(
            turn[1], turn[0], local, prod, d_gate, low, state, forget, inner_low, *tables
        )
        sums, turn = after((sums, turn))
        send_b, kept_b = last_grads(
            "recurrent_grads", 1, turn, [normed, gated], [d_gate, d_mid], shares[1], swapped_b
        )
        made, kept, got, sums, send_b, kept_b, turn = after((made, kept, got, sums, send_b, kept_b, turn))
        swapped_a = []
        for k, (v,) in enumerate(made, 1):
            v = ex.swap_dp(v, k)
            swapped_a.append([v] if ex.fine else [v[:, :width], v[:, width:]])
        ffn, others = ex.deal_z(kept, got)
        ffn, others, send_b, turn = after((ffn, others, send_b, turn))
        ffn_got = ex.send_parts(others)
        got_b = ex.swap(send_b, 2)
        send_a, kept_a = last_grads(
            "recurrent_grads", 0, turn, [normed], [d_proj], shares[0], swapped_a, sums if ex.fine else None
        )
        send_a, kept_a, turn = after((send_a, kept_a, turn))
        got_a = ex.swap(send_a, 1)
        kept, got = [[kept_a], [kept_b]], [[got_a], [got_b]]
        (input_grad,) = input_back(dims)(turn[0], d_proj, gains, d_middle, tok, *far(w_one))
        input_grad, turn = after((input_grad, turn))
        (act,) = ffn_out(dims, ff)(turn[1], *far(hidden_far, middle_far), w_three)
        input_grad, ffn_got, kept, got, act = after((input_grad, ffn_got, kept, got, act))
        cuts, act = after((ex.halve(kept, got, ex.fine), act))
        kept, got = ex.send_halves(cuts)
        act = from_chains(act)
        middle_at = ff + fold_rows * cut3
        bounds = [ff, middle_at, middle_at + ff]
        grad_up_gate, down_a, grad_up, down_b, grad_ffn_gain = ex.finish_z(
            ffn, ffn_got, bounds, [(ffn_gain[None], {0: w_up_gate, 2: w_up})]
        )
        kept, got, input_grad, act = after((kept, got, input_grad, act))
        rest, others = ex.deal_z(kept, got, ex.fine)
        rest, others, input_grad = after((rest, others, input_grad))
        got = ex.send_parts(others)
        input_grad = from_chains(input_grad)
        if not ex.fine:
            sums = ex.total(sums)
        norm_weights = {0: w_input, 1: w_forget, 2: w_gate}
        made = ex.finish_z(
            rest,
            got,
            [width, width + half, wide],
            [(norm_gain[None], norm_weights), (group_gain[None], {3: w_output})],
            ex.fine,
        )
        grad_input, grad_forget, grad_gate, grad_output, grad_norm_gain, grad_group_gain = made[:6]
        if ex.fine:
            grad_lower, grad_phase = made[6:]
        else:
            ahead = half // LANES
            grad_lower, grad_phase = sums[0:ahead].reshape(half), sums[ahead : 2 * ahead].reshape(half)

        halves = []
        for i in range(fold_rows):
            left_half = down_a[:, i * cut3 : (i + 1) * cut3]
            right_half = down_b[:, i * (width - cut3) : (i + 1) * (width - cut3)]
            halves.append(jnp.concatenate([left_half, right_half], axis=1))
        grad_down = jnp.concatenate(halves, axis=0)
        return (
            act,
            input_grad,
            grad_input,
            grad_forget,
            grad_gate,
            grad_output,
            grad_up_gate,
            grad_up,
            grad_down,
            grad_norm_gain,
            grad_group_gain,
            grad_ffn_gain,
            grad_lower,
            grad_phase,
        )

    return per_device


def solution(mesh):
    rows = P(("dp", "fsdp"), None)
    vec = P(("dp", "fsdp"))
    in_specs = (rows,) * 9 + (vec,) * 3 + (P(), P(), rows)
    out_specs = (rows,) * 9 + (vec,) * 3 + (P(), P())
    return jax.shard_map(build(mesh), mesh=mesh, in_specs=in_specs, out_specs=out_specs, check_vma=False)
```

```python
import jax
import jax.numpy as jnp
from jax import lax
from jax.experimental import pallas as pl
from jax.experimental.pallas import tpu as pltpu
from jax.sharding import PartitionSpec as P

GROUPS = 4
LANES = 128
CHAINS = 8
TILE = 256
BF = jnp.bfloat16
F32 = jnp.float32
TN = (((0,), (0,)), ((), ()))
NT = (((1,), (1,)), ((), ()))


def mm(left, right):
    return jnp.dot(left, right, preferred_element_type=F32)


def mm_nt(left, right):
    return lax.dot_general(left, right, NT, preferred_element_type=F32)


def mm_tn(left, right):
    return lax.dot_general(left, right, TN, preferred_element_type=F32)


def sigmoid(v):
    return 0.5 * jnp.tanh(0.5 * v) + 0.5


STEPS = {
    "norm": (256, 1),
    "sources": (64, 4),
    "mix": (64, 2),
    "finish": (256, 1),
    "norm_back": (256, 1),
    "through": (64, 4),
    "kept": (256, 1),
    "source_back": (64, 1),
}


def chunks(name, body):
    rows, unroll = STEPS[name]

    def step(i, carry):
        body(pl.multiple_of(i * rows, rows), rows)
        return carry

    lax.fori_loop(0, TILE // rows, step, 0, unroll=unroll)


def tiles_of(total, body, backwards=False, tile=TILE):
    count = total // tile

    def step(i, carry):
        body(pl.multiple_of(((count - 1 - i) if backwards else i) * tile, tile))
        return carry

    lax.fori_loop(0, count, step, 0)


def span(at, rows):
    return pl.ds(pl.multiple_of(at, rows), rows)


def repeat(value, rows):
    return jnp.concatenate([value] * (rows // 8), axis=0)


def fold(value):
    return jnp.sum(value.reshape(value.shape[0] // 8, 8, value.shape[1]), axis=0)


def cost(micros, moved):
    return pl.CostEstimate(flops=int(micros * 1.15e8), bytes_accessed=moved // 10, transcendentals=0)


def slot_times(base, rows, total):
    row = base + lax.broadcasted_iota(jnp.int32, (rows, 1), 0)
    return (row % CHAINS) * (total // CHAINS) + row // CHAINS


def turned(tables, base, rows):
    ci, si, co, so = tables
    inside = span(base // CHAINS, rows // CHAINS)
    half = ci.shape[1]
    c, s = ci[inside, :][:, None, :], si[inside, :][:, None, :]
    oc, os = co[...][None], so[...][None]
    return (c * oc - s * os).reshape(rows, half), (s * oc + c * os).reshape(rows, half)


def strips(value):
    return [value[:, i * LANES : (i + 1) * LANES] for i in range(value.shape[1] // LANES)]


def group_means(parts, low, size):
    zero = jnp.zeros_like(parts[0])
    sums = []
    for h in (0, 3):
        sums.append(parts[h] + jnp.where(low, parts[h + 1], zero))
        sums.append(jnp.where(low, zero, parts[h + 1]) + parts[h + 2])
    return [jnp.sum(s, axis=-1, keepdims=True) * (1.0 / size) for s in sums]


def group_spread(values, low):
    out = []
    for h in (0, 2):
        out += [values[h], jnp.where(low, values[h], values[h + 1]), values[h + 1]]
    return out


def pack(value):
    high = value.astype(BF).astype(F32)
    middle = (value - high).astype(BF).astype(F32)
    return jnp.concatenate([high, middle, value - high - middle], axis=0).astype(BF)


def unpack(value):
    value = value.astype(F32)
    return value[0:8, :] + value[8:16, :] + value[16:24, :]


def centre_and_scale(parts, low, size):
    means = group_spread(group_means(parts, low, size), low)
    parts = [p - m for p, m in zip(parts, means)]
    variances = group_means([p * p for p in parts], low, size)
    scales = group_spread([lax.rsqrt(v + 1e-05) for v in variances], low)
    return [p * s for p, s in zip(parts, scales)], scales


def piece_copies(me, pieces, target, columns, sems, first):
    rows = pieces[0].shape[0]
    out = []
    for k, piece in enumerate(pieces):
        at = pl.multiple_of((me ^ k) * rows, 16)
        out.append(pltpu.make_async_copy(piece, target.at[pl.ds(at, rows), columns], sems.at[first + k]))
    return out


HBM = pl.BlockSpec(memory_space=pltpu.HBM)
ANY = pl.BlockSpec(memory_space=pl.ANY)
SMEM = pl.BlockSpec(memory_space=pltpu.SMEM)


def struct(shape, dtype):
    return jax.ShapeDtypeStruct(shape, dtype)


VMEM = pl.BlockSpec(memory_space=pltpu.VMEM)


def far(*arrays):
    return [pltpu.with_memory_space_constraint(v, pltpu.HBM) for v in arrays]


def kernel_call(body, name, ins, outs, scratch, room, estimate, distant=0):
    near = len(outs) - distant
    outs = outs[:near] + [pltpu.HBM(v.shape, v.dtype) for v in outs[near:]]
    return pl.pallas_call(
        body,
        in_specs=ins,
        out_specs=[VMEM] * near + [HBM] * distant,
        out_shape=outs,
        scratch_shapes=scratch,
        compiler_params=pltpu.CompilerParams(vmem_limit_bytes=room * 2**20),
        cost_estimate=estimate,
        name=name,
    )


class Streams:
    def __init__(self, total, sems, arrived=(), leaving=()):
        self.bases = range(0, total, TILE)
        self.sems = sems
        self.arriving = [(far_ref, near_ref) for far_ref, near_ref in arrived]
        self.leaving = [(near_ref, far_ref) for near_ref, far_ref in leaving]

    def copies(self, base, pairs, first):
        block = pl.ds(base, TILE)
        return [
            pltpu.make_async_copy(a.at[block, :], b.at[block, :], self.sems.at[first + n, base // TILE])
            for n, (a, b) in enumerate(pairs)
        ]

    def start(self, backwards=False):
        for base in reversed(self.bases) if backwards else self.bases:
            for c in self.copies(base, self.arriving, 0):
                c.start()

    def wait(self, base):
        for c in self.copies(base, self.arriving, 0):
            c.wait()

    def leave(self, base):
        for c in self.copies(base, self.leaving, len(self.arriving)):
            c.start()

    def finish(self):
        for base in self.bases:
            for c in self.copies(base, self.leaving, len(self.arriving)):
                c.wait()


def stream_sems(total, count):
    return pltpu.SemaphoreType.DMA((count, total // TILE))


def recurrent_project(parts, cut, dims):
    total, width, half, size = dims
    wide = 2 * width + half
    packed = wide + LANES

    def kernel(place_ref, tok_far, *refs):
        left_pieces, right_pieces = refs[:parts], refs[parts : 2 * parts]
        inner, gate, forget, gains, normed, inner_low, gate_low, w_far, w, tok, sems, tile_sems = refs[2 * parts :]
        me = place_ref[0]
        small = [v.at[:, pl.ds(wide - cut, LANES)] for v in right_pieces]
        large = [v.at[:, pl.ds(0, wide - cut)] for v in right_pieces]
        ahead = piece_copies(me, small, w, pl.ds(wide, LANES), sems, 0)
        behind = piece_copies(me, left_pieces, w, pl.ds(0, cut), sems, parts)
        behind += piece_copies(me, large, w, pl.ds(cut, wide - cut), sems, 2 * parts)
        io = Streams(total, tile_sems, [(tok_far, tok)])
        keep = pltpu.make_async_copy(w, w_far, sems.at[3 * parts])
        for c in ahead:
            c.start()
        io.start()
        for c in behind:
            c.start()
        for c in ahead:
            c.wait()
        gains[...] = jnp.transpose(w[:, wide:packed].astype(F32))[0:8, :]

        def project(base):
            block = pl.ds(base, TILE)
            io.wait(base)
            gain = gains[0:1, :]

            def norm(at, rows):
                there = span(base + at, rows)
                x = tok[there, :]
                scale = lax.rsqrt(jnp.mean(x * x, axis=-1, keepdims=True) + 1e-06)
                normed[there, :] = (x * scale * gain).astype(BF)

            chunks("norm", norm)

            @pl.when(base == 0)
            def _():
                for c in behind:
                    c.wait()
                keep.start()

            value = normed[block, :]
            for n in range(0, width, 256):
                lanes = slice(n, n + 256)
                made = mm(value, w[:, n : n + 256])
                inner[block, lanes] = made
                inner_low[block, lanes] = made.astype(BF)
                made = mm(value, w[:, width + n : width + n + 256])
                gate[block, lanes] = made
                gate_low[block, lanes] = made.astype(BF)
            forget[block, :] = mm(value, w[:, 2 * width : wide])

        tiles_of(total, project)
        keep.wait()

    return kernel_call(
        kernel,
        "recurrent_project",
        [SMEM] + [HBM] + [ANY] * (2 * parts),
        [
            struct((total, width), F32),
            struct((total, width), F32),
            struct((total, half), F32),
            struct((8, width), F32),
            struct((total, width), BF),
            struct((total, width), BF),
            struct((total, width), BF),
            struct((width, packed), BF),
        ],
        [
            pltpu.VMEM((width, packed), BF),
            pltpu.VMEM((total, width), F32),
            pltpu.SemaphoreType.DMA((3 * parts + 1,)),
            stream_sems(total, 1),
        ],
        10,
        cost(6, 24 * total * width),
        distant=1,
    )


def recurrent_mix(dims):
    total, width, half, size = dims

    def kernel(len_ref, inner, gate, forget, gains, low_ref, *refs):
        tables, (gated, state, prod, keep, carry, ends) = refs[:4], refs[4:]
        first = len_ref[0, 0]
        second = first + len_ref[0, 1]
        carry[...] = jnp.concatenate([jnp.zeros((16, half), F32), jnp.ones((8, half), F32)], axis=0)
        bound = low_ref[0:1, :]

        def chain_tile(base):
            def sources(at, rows):
                here = pl.ds(at, rows)
                there = span(base + at, rows)
                time = slot_times(base + at, rows, total)
                start = (time == 0) | (time == first) | (time == second)
                rest = (1.0 - bound) * (1.0 - sigmoid(forget[there, :]))
                keep[here, :] = jnp.where(start, 0.0, 1.0 - rest)
                re = inner[there, 0:half]
                im = inner[there, half:width]
                re = rest * re * sigmoid(re)
                im = rest * im * sigmoid(im)
                c, s = turned(tables, base + at, rows)
                state[there, 0:half] = c * re + s * im
                state[there, half:width] = c * im - s * re

            chunks("sources", sources)

            def scan(j, held):
                re, im, p = held
                there = span(base + j * 8, 8)
                k = keep[span(j * 8, 8), :]
                re = k * re + state[there, 0:half]
                im = k * im + state[there, half:width]
                p = k * p
                state[there, 0:half] = re
                state[there, half:width] = im
                prod[there, :] = p
                return re, im, p

            held = (carry[0:8, :], carry[8:16, :], carry[16:24, :])
            held = lax.fori_loop(0, TILE // 8, scan, held, unroll=8)
            carry[0:8, :], carry[8:16, :], carry[16:24, :] = held

        tiles_of(total, chain_tile)
        p = carry[16:24, :]
        for h in (0, 8):
            z = carry[h : h + 8, :]
            rows = [jnp.zeros((1, half), F32)]
            for c in range(1, CHAINS):
                rows.append(z[c - 1 : c, :] + p[c - 1 : c, :] * rows[-1])
            ends[h : h + 8, :] = jnp.concatenate(rows, axis=0)
        gain = gains[1:2, :]

        def mix_tile(base):
            def mix(at, rows):
                there = span(base + at, rows)
                low = lax.broadcasted_iota(jnp.int32, (rows, LANES), 1) < LANES // 2
                p = prod[there, :]
                re = state[there, 0:half] + p * repeat(ends[0:8, :], rows)
                im = state[there, half:width] + p * repeat(ends[8:16, :], rows)
                state[there, 0:half] = re
                state[there, half:width] = im
                c, s = turned(tables, base + at, rows)
                mixed = strips(c * re - s * im) + strips(c * im + s * re)
                grouped, _ = centre_and_scale(mixed, low, size)
                for n in range(len(grouped)):
                    lanes = slice(n * LANES, (n + 1) * LANES)
                    opened = grouped[n] * gain[:, lanes] * sigmoid(gate[there, lanes])
                    gated[there, lanes] = opened.astype(BF)

            chunks("mix", mix)

        tiles_of(total, mix_tile)

    return kernel_call(
        kernel,
        "recurrent_mix",
        [SMEM] + [VMEM] * 9,
        [struct((total, width), BF), struct((total, width), F32)],
        [
            pltpu.VMEM((total, half), F32),
            pltpu.VMEM((TILE, half), F32),
            pltpu.VMEM((24, half), F32),
            pltpu.VMEM((16, half), F32),
        ],
        5,
        cost(8, 20 * total * width),
    )


def ffn_up(parts, cut, dims, ff):
    total, width, half, size = dims
    packed = width + 2 * ff

    def kernel(me_ref, gated, gains, tok_far, *refs):
        left_pieces, right_pieces = refs[:parts], refs[parts : 2 * parts]
        middle, ffn_in, to_left, to_right, hidden, w, tok, sems, tile_sems = refs[2 * parts :]
        me = me_ref[0]
        first = [v.at[:, pl.ds(0, width)] for v in left_pieces]
        then = [v.at[:, pl.ds(width, cut - width)] for v in left_pieces]
        ahead = piece_copies(me, first, w, pl.ds(0, width), sems, 0)
        behind = piece_copies(me, then, w, pl.ds(width, cut - width), sems, parts)
        behind += piece_copies(me, right_pieces, w, pl.ds(cut, packed - cut), sems, 2 * parts)
        for c in ahead:
            c.start()
        io = Streams(total, tile_sems, [(tok_far, tok)])
        io.start()
        for c in behind:
            c.start()
        gain = gains[2:3, :]
        for c in ahead:
            c.wait()

        def enter(base):
            block = pl.ds(base, TILE)
            io.wait(base)
            middle[block, :] = tok[block, :] + mm(gated[block, :], w[:, 0:width])

            def norm(at, rows):
                there = span(base + at, rows)
                x = middle[there, :]
                scale = lax.rsqrt(jnp.mean(x * x, axis=-1, keepdims=True) + 1e-06)
                ffn_in[there, :] = (x * scale * gain).astype(BF)

            chunks("norm", norm)

        tiles_of(total, enter)
        for c in behind:
            c.wait()

        def expand(base):
            block = pl.ds(base, 2 * TILE)
            value = ffn_in[block, :]
            for c in range(0, ff, 256):
                lanes = slice(c, c + 256)
                l = mm(value, w[:, width + c : width + c + 256])
                r = mm(value, w[:, width + ff + c : width + ff + c + 256])
                g = sigmoid(l)
                u = l * g
                to_right[block, lanes] = u.astype(BF)
                to_left[block, lanes] = ((g + u - u * g) * r).astype(BF)
                hidden[block, lanes] = (u * r).astype(BF)

        tiles_of(total, expand, tile=2 * TILE)

    return kernel_call(
        kernel,
        "ffn_up",
        [SMEM, VMEM, VMEM] + [HBM] + [ANY] * (2 * parts),
        [
            struct((total, width), F32),
            struct((total, width), BF),
            struct((total, ff), BF),
            struct((total, ff), BF),
            struct((total, ff), BF),
            struct((width, packed), BF),
        ],
        [
            pltpu.VMEM((total, width), F32),
            pltpu.SemaphoreType.DMA((3 * parts,)),
            stream_sems(total, 1),
        ],
        6,
        cost(10, 24 * total * width),
    )


def ffn_turn(parts, cut, dims, ff):
    total, width, half, size = dims

    def kernel(me_ref, grad, to_left, to_right, hidden, middle, *refs):
        left_pieces, right_pieces = refs[:parts], refs[parts : 2 * parts]
        d_left, d_right, w, hidden_far, middle_far, sems = refs[2 * parts :]
        me = me_ref[0]
        copies = piece_copies(me, left_pieces, w, pl.ds(0, cut), sems, 0)
        copies += piece_copies(me, right_pieces, w, pl.ds(cut, width - cut), sems, parts)
        for c in copies:
            c.start()
        for c in copies:
            c.wait()
        leaving = [
            pltpu.make_async_copy(hidden, hidden_far, sems.at[2 * parts]),
            pltpu.make_async_copy(middle, middle_far, sems.at[2 * parts + 1]),
        ]
        for c in leaving:
            c.start()

        def turn(base):
            block = pl.ds(base, 2 * TILE)
            value = grad[block, :]
            for c in range(0, ff, 256):
                lanes = slice(c, c + 256)
                dh = mm_nt(value, w[c : c + 256, :])
                d_right[block, lanes] = (dh * to_right[block, lanes].astype(F32)).astype(BF)
                d_left[block, lanes] = (dh * to_left[block, lanes].astype(F32)).astype(BF)

        tiles_of(total, turn, tile=2 * TILE)
        for c in leaving:
            c.wait()

    return kernel_call(
        kernel,
        "ffn_turn",
        [SMEM] + [VMEM] * 5 + [ANY] * (2 * parts),
        [
            struct((total, ff), BF),
            struct((total, ff), BF),
            struct((ff, width), BF),
            struct((total, ff), BF),
            struct((total, width), F32),
        ],
        [pltpu.SemaphoreType.DMA((2 * parts + 2,))],
        3,
        cost(5, 20 * total * width),
        distant=2,
    )


def ffn_out(dims, ff):
    total, width, half, size = dims

    def kernel(len_ref, hidden_far, middle_far, w, act_far, hidden, middle, act, tile_sems):
        second = len_ref[0, 0] + len_ref[0, 1]
        io = Streams(total, tile_sems, [(hidden_far, hidden), (middle_far, middle)], [(act, act_far)])
        io.start()

        def tile(base):
            block = pl.ds(base, TILE)
            io.wait(base)
            valid = (slot_times(base, TILE, total) < second).astype(F32)
            act[block, :] = valid * (middle[block, :] + mm(hidden[block, :], w[...]))
            io.leave(base)

        tiles_of(total, tile)
        io.finish()

    return kernel_call(
        kernel,
        "ffn_out",
        [SMEM] + [HBM] * 2 + [VMEM],
        [struct((total, width), F32)],
        [
            pltpu.VMEM((total, ff), BF),
            pltpu.VMEM((total, width), F32),
            pltpu.VMEM((total, width), F32),
            stream_sems(total, 3),
        ],
        11,
        cost(6, 10 * total * width),
        distant=1,
    )


def products_of(me, refs, counts, products, slot, parts, aligned, store):
    for n, (l, r, begin, end) in enumerate(products):
        if aligned:
            size = refs[l].shape[1] // parts
            left = refs[l][:, pl.ds(pl.multiple_of((me ^ slot) * size, LANES), size)]
        else:
            left = refs[l][...]
        for c in range(begin, end, 512):
            stop = min(c + 512, end)
            store(n, c - begin, stop - begin, mm_tn(left, refs[counts + r][:, c:stop]))


def prepared(me, lefts, slot, parts):
    sizes = [v.shape[1] // parts for v in lefts]
    aligned = all(size % LANES == 0 for size in sizes)
    if not aligned:
        lefts = [
            lax.dynamic_slice_in_dim(v, (me[0] ^ slot) * size, size, axis=1) for v, size in zip(lefts, sizes)
        ]
    return lefts, sizes, aligned


def grads_cost(lefts, sizes, products):
    flops = sum(2 * lefts[l].shape[0] * sizes[l] * (end - begin) for l, r, begin, end in products)
    return cost(flops / 0.6e9, flops // 256)


def weight_grads(name, me, lefts, rights, products, slot, parts):
    lefts, sizes, aligned = prepared(me, lefts, slot, parts)
    given = len(lefts) + len(rights)

    def kernel(me_ref, *refs):
        def store(n, begin, end, value):
            refs[given + n][:, begin:end] = value.astype(BF)

        products_of(me_ref[0], refs, len(lefts), products, slot, parts, aligned, store)

    outs = [struct((sizes[l], end - begin), BF) for l, r, begin, end in products]
    return kernel_call(
        kernel, name, [SMEM] + [VMEM] * given, outs, [], 8, grads_cost(lefts, sizes, products)
    )(me, *lefts, *rights)


def split_grads(name, place, axis, lefts, rights, products, swapped, parts, outer, rows, sums=None):
    lefts, sizes, aligned = prepared(place, lefts, 0, parts)
    given = len(lefts) + len(rights)
    base = rows * outer * (2 if axis == 3 else 4)
    inner = base // (2 * outer)
    places, width = [], 0
    for l, r, begin, end in products:
        places.append(width)
        width += (end - begin) * (sizes[l] // base)
    count = len(products)
    extra = [] if sums is None else [sums]
    flat = [v for arrays in swapped for v in arrays]
    per = len(flat) // max(parts - 1, 1)

    def kernel(place_ref, *refs):
        others = refs[given : given + per * (parts - 1)]
        tail = refs[given + per * (parts - 1) :]
        send, kept = tail[len(extra) : len(extra) + 2]
        high_is_mine = place_ref[axis] == 1

        def store(n, begin, end, value):
            for k in range(parts - 1):
                block, at = (k * per + n, 0) if per == count else (k, places[n])
                value = value + others[block][:, at + begin : at + end].astype(F32)
            times = value.shape[0] // base
            value = value.reshape(outer, 2, inner // rows, times, rows, end - begin)
            for t in range(times):
                to = places[n] + t * (products[n][3] - products[n][2]) + begin
                low = value[:, 0, :, t].reshape(outer, inner, end - begin)
                high = value[:, 1, :, t].reshape(outer, inner, end - begin)
                send[:, :, to : to + end - begin] = jnp.where(high_is_mine, low, high).astype(BF)
                kept[:, :, to : to + end - begin] = jnp.where(high_is_mine, high, low)

        products_of(place_ref[0], refs, len(lefts), products, 0, parts, aligned, store)
        if extra:
            held = tail[-1]
            held[place_ref[0]] = tail[0][...]
            for k in range(1, parts):
                block = others[(k - 1) * per]
                held[place_ref[0] ^ k] = unpack(block[0:32, block.shape[1] - LANES :])
            value = held[0]
            for k in range(1, parts):
                value = value + held[k]
            columns = slice(width, width + LANES)
            send[:, :, columns] = jnp.zeros((outer, inner, LANES), BF)
            kept[:, :, columns] = jnp.zeros((outer, inner, LANES), F32)
            send[0, :, columns] = pack(value)
            kept[0, 0:8, columns] = value

    shape = (outer, inner, width + LANES * len(extra))
    return kernel_call(
        kernel,
        name,
        [SMEM] + [VMEM] * (given + len(flat) + len(extra)),
        [struct(shape, BF), struct(shape, F32)],
        [pltpu.VMEM((parts, 8, LANES), F32)] * len(extra),
        8,
        grads_cost(lefts, sizes, products),
    )(place, *lefts, *rights, *flat, *extra)


def middle_back(dims, ff):
    total, width, half, size = dims
    packed = width + 2 * ff

    def kernel(len_ref, d_left, d_right, middle, gains, low_ref, state, gate, forget, w, *refs):
        tables, cot_far, refs = refs[:4], refs[4], refs[5:]
        d_mid, d_middle, d_gate, local, prod, cot, hold, keep, carry, tile_sems = refs
        first = len_ref[0, 0]
        second = first + len_ref[0, 1]
        bound = low_ref[0:1, :]
        io = Streams(total, tile_sems, [(cot_far, cot)])
        io.start(backwards=True)
        ffn_gain = gains[2:3, :]
        gain = gains[1:2, :]

        def keeps(base, rows, value):
            time = slot_times(base, rows, total)
            start = (time == 0) | (time == first) | (time == second)
            return jnp.where(start, 0.0, bound + (1.0 - bound) * sigmoid(value))

        k = keeps(0, 8, forget[0:8, :])
        carry[0:16, :] = jnp.zeros((16, half), F32)
        carry[16:24, :] = jnp.ones((8, half), F32)
        carry[24:32, :] = jnp.concatenate([k[1:8, :], jnp.zeros((1, half), F32)], axis=0)

        def enter(base):
            block = pl.ds(base, TILE)
            hold[...] = mm_nt(d_left[block, :], w[:, width : width + ff]) + mm_nt(
                d_right[block, :], w[:, width + ff : packed]
            )
            io.wait(base)

            def norm_back(at, rows):
                here = pl.ds(at, rows)
                there = span(base + at, rows)
                valid = (slot_times(base + at, rows, total) < second).astype(F32)
                x = middle[there, :]
                scale = lax.rsqrt(jnp.mean(x * x, axis=-1, keepdims=True) + 1e-06)
                d = hold[here, :]
                unit = x * scale
                d = d * ffn_gain
                back = scale * (d - unit * jnp.mean(d * unit, axis=-1, keepdims=True))
                back = back + valid * cot[there, :]
                d_middle[there, :] = back
                d_mid[there, :] = back.astype(BF)

            chunks("norm_back", norm_back)

        def tile(base):
            enter(base)
            block = pl.ds(base, TILE)
            hold[...] = mm_nt(d_mid[block, :], w[:, 0:width])

            def through(at, rows):
                here = pl.ds(at, rows)
                there = span(base + at, rows)
                low = lax.broadcasted_iota(jnp.int32, (rows, LANES), 1) < LANES // 2
                re, im = state[there, 0:half], state[there, half:width]
                c, s = turned(tables, base + at, rows)
                mixed = strips(c * re - s * im) + strips(c * im + s * re)
                grouped, scales = centre_and_scale(mixed, low, size)
                back = []
                for n in range(len(grouped)):
                    lanes = slice(n * LANES, (n + 1) * LANES)
                    opened = sigmoid(gate[there, lanes].astype(F32))
                    d = hold[here, lanes]
                    part = d * grouped[n] * opened
                    d_gate[there, lanes] = (part * gain[:, lanes] * (1.0 - opened)).astype(BF)
                    back.append(d * opened * gain[:, lanes])
                mean = group_spread(group_means(back, low, size), low)
                along = group_spread(group_means([b * g for b, g in zip(back, grouped)], low, size), low)
                back = [t * (b - m - g * a) for t, b, m, g, a in zip(scales, back, mean, grouped, along)]
                for n in range(3):
                    lanes = slice(n * LANES, (n + 1) * LANES)
                    cn, sn = c[:, lanes], s[:, lanes]
                    local[there, lanes] = cn * back[n] + sn * back[n + 3]
                    local[there, half + n * LANES : half + (n + 1) * LANES] = cn * back[n + 3] - sn * back[n]

            chunks("through", through)

            def kept(at, rows):
                there = span(base + at, rows)
                keep[pl.ds(at, rows), :] = keeps(base + at, rows, forget[there, :])

            chunks("kept", kept)

            def scan(i, held):
                re, im, p, k = held
                at = (TILE // 8 - 1 - i) * 8
                there = span(base + at, 8)
                re = k * re + local[there, 0:half]
                im = k * im + local[there, half:width]
                p = k * p
                local[there, 0:half] = re
                local[there, half:width] = im
                prod[there, :] = p
                return re, im, p, keep[span(at, 8), :]

            held = (carry[0:8, :], carry[8:16, :], carry[16:24, :], carry[24:32, :])
            held = lax.fori_loop(0, TILE // 8, scan, held, unroll=8)
            carry[0:8, :], carry[8:16, :], carry[16:24, :], carry[24:32, :] = held

        tiles_of(total, tile, backwards=True)

    return kernel_call(
        kernel,
        "middle_back",
        [SMEM] + [VMEM] * 13 + [HBM],
        [
            struct((total, width), BF),
            struct((total, width), F32),
            struct((total, width), BF),
            struct((total, width), F32),
            struct((total, half), F32),
        ],
        [
            pltpu.VMEM((total, width), F32),
            pltpu.VMEM((TILE, width), F32),
            pltpu.VMEM((TILE, half), F32),
            pltpu.VMEM((32, half), F32),
            stream_sems(total, 1),
        ],
        8,
        cost(19, 60 * total * width),
    )


def source_back(dims, parts, me, lefts, d_mid, shares, fine):
    total, width, half, size = dims
    wide = 2 * width + half
    given, sizes, aligned = [], None, True
    for slot in range(1, parts):
        made, sizes, aligned = prepared(me, lefts, slot, parts)
        given.append(list(made))
    if aligned:
        given = [list(lefts)] * max(parts - 1, 0)
        flat = list(lefts)
    else:
        flat = [v for made in given for v in made]
    products = [p for share in shares for p in share]
    count = len(shares)
    owner, widths = [], []
    for n, share in enumerate(shares):
        widths.append(0)
        for l, r, begin, end in share:
            owner.append((n, widths[n]))
            widths[n] += end - begin
    widths[0] += LANES if fine else 0

    def kernel(len_ref, me_ref, local, prod, d_gate, low_ref, state, forget, inner, *refs):
        tables, refs = refs[:4], refs[4:]
        left_refs, d_mid_ref, refs = refs[: len(flat)], refs[len(flat)], refs[len(flat) + 1 :]
        d_proj, sums = refs[:2]
        slots, (ends, acc) = refs[2 : 2 + count * (parts - 1)], refs[2 + count * (parts - 1) :]
        first = len_ref[0, 0]
        second = first + len_ref[0, 1]
        bound = low_ref[0:1, :]
        acc[...] = jnp.zeros_like(acc)
        p = prod[0:8, :]
        for h in (0, 1):
            z = local[0:8, h * half : (h + 1) * half]
            made = [jnp.zeros((1, half), F32)]
            for c in range(CHAINS - 2, -1, -1):
                made.append(z[c + 1 : c + 2, :] + p[c + 1 : c + 2, :] * made[-1])
            ends[8 * h : 8 * h + 8, 0:half] = jnp.concatenate(made[::-1], axis=0)
        old = state[total - 8 : total, :]
        ends[16:24, :] = jnp.concatenate([old[7:8, :], old[0:7, :]], axis=0)

        def tile(base):
            def back(at, rows):
                row = base + at
                there = span(row, rows)
                p = prod[there, :]
                re = local[there, 0:half] + p * repeat(ends[0:8, 0:half], rows)
                im = local[there, half:width] + p * repeat(ends[8:16, 0:half], rows)
                up = span(jnp.maximum(row - 8, 0), 8)
                stay = pl.ds(pl.multiple_of(row, 8), rows - 8)
                old_re = jnp.concatenate(
                    [jnp.where(row == 0, ends[16:24, 0:half], state[up, 0:half]), state[stay, 0:half]], axis=0
                )
                old_im = jnp.concatenate(
                    [jnp.where(row == 0, ends[16:24, half:width], state[up, half:width]), state[stay, half:width]],
                    axis=0,
                )
                time = slot_times(row, rows, total)
                start = (time == 0) | (time == first) | (time == second)
                sf = sigmoid(forget[there, :])
                rest = (1.0 - bound) * (1.0 - sf)
                turn = (1.0 - rest) * (im * old_re - re * old_im)
                acc[8:16, :] += fold(jnp.where(start, 0.0, turn))
                d_lam = jnp.where(start, 0.0, re * old_re + im * old_im)
                c, s = turned(tables, row, rows)
                d_re = c * re - s * im
                d_im = c * im + s * re
                for lane, d in ((0, d_re), (half, d_im)):
                    v = inner[there, lane : lane + half].astype(F32)
                    sv = sigmoid(v)
                    d_lam = d_lam - d * (v * sv)
                    d_proj[there, lane : lane + half] = (rest * d * (sv * (1.0 + v * (1.0 - sv)))).astype(BF)
                acc[0:8, :] += fold(d_lam * (1.0 - sf))
                d_proj[there, 2 * width : wide] = (d_lam * rest * sf).astype(BF)
                d_proj[there, width : 2 * width] = d_gate[there, :]

            chunks("source_back", back)

        tiles_of(total, tile)
        out = [jnp.sum(acc[8 * n : 8 * n + 8, :], axis=0, keepdims=True) for n in range(2)]
        out = strips(out[0]) + strips(out[1])
        sums[...] = jnp.concatenate(out + [jnp.zeros((8 - len(out), LANES), F32)], axis=0)
        for slot in range(1, parts):
            used = left_refs if aligned else left_refs[(slot - 1) * len(lefts) : slot * len(lefts)]

            def store(n, begin, end, value):
                share, at = owner[n]
                slots[(slot - 1) * count + share][:, at + begin : at + end] = value.astype(BF)

            products_of(
                me_ref[0], [*used, d_proj, d_mid_ref], len(lefts), products, slot, parts, aligned, store
            )
            if fine:
                block = slots[(slot - 1) * count]
                rest = jnp.zeros((block.shape[0] - 24, LANES), F32)
                carried = jnp.concatenate([pack(sums[...]).astype(F32), rest], axis=0)
                block[:, block.shape[1] - LANES :] = carried.astype(BF)

    outs = [struct((total, wide), BF), struct((8, LANES), F32)]
    outs += [struct((width // parts, n), BF) for n in widths] * (parts - 1)
    call = kernel_call(
        kernel,
        "source_back",
        [SMEM, SMEM] + [VMEM] * (12 + len(flat)),
        outs,
        [pltpu.VMEM((24, width), F32), pltpu.VMEM((16, half), F32)],
        6,
        cost(10, 40 * total * width),
    )

    def run(lengths, me, *arrays):
        d_proj, sums, *slots = call(lengths, me, *arrays, *flat, d_mid)
        return d_proj, sums, [slots[k * count : (k + 1) * count] for k in range(parts - 1)]

    return run


def input_back(dims):
    total, width, half, size = dims
    wide = 2 * width + half

    def kernel(order_ref, d_proj, gains, d_middle, tok_far, w_far, out, w, tok, hold, sem, tile_sems):
        weight = pltpu.make_async_copy(w_far, w, sem.at[0])
        weight.start()
        io = Streams(total, tile_sems, [(tok_far, tok)])
        io.start()
        gain = gains[0:1, :]
        weight.wait()

        def tile(base):
            hold[...] = mm_nt(d_proj[pl.ds(base, TILE), :], w[:, 0:wide])
            io.wait(base)

            def norm_back(at, rows):
                here = pl.ds(at, rows)
                there = span(base + at, rows)
                x = tok[there, :]
                scale = lax.rsqrt(jnp.mean(x * x, axis=-1, keepdims=True) + 1e-06)
                d = hold[here, :]
                unit = x * scale
                d = d * gain
                out[there, :] = d_middle[there, :] + scale * (d - unit * jnp.mean(d * unit, axis=-1, keepdims=True))

            chunks("norm_back", norm_back)

        tiles_of(total, tile)

    return kernel_call(
        kernel,
        "input_back",
        [SMEM, VMEM, VMEM, VMEM] + [HBM] * 2,
        [struct((total, width), F32)],
        [
            pltpu.VMEM((width, wide + LANES), BF),
            pltpu.VMEM((total, width), F32),
            pltpu.VMEM((TILE, width), F32),
            pltpu.SemaphoreType.DMA((1,)),
            stream_sems(total, 1),
        ],
        10,
        cost(7, 20 * total * width),
    )


def order_call(place, held, cut):
    rows, columns = held[0].shape
    deep = len(held)

    def kernel(place_ref, *refs):
        for k in range(deep):
            at = place_ref[1] ^ k
            refs[deep][at] = refs[k][:, 0:cut]
            refs[deep + 1][at] = refs[k][:, cut:columns]

    outs = [struct((deep, rows, cut), BF), struct((deep, rows, columns - cut), BF)]
    return kernel_call(kernel, "order_z", [SMEM] + [VMEM] * deep, outs, [], 2, cost(1, 4 * deep * rows * columns))(
        place, *held
    )


def join_call(place, axes, own, got):
    count = len(own)

    def kernel(place_ref, *refs):
        for n in range(count):
            bit = place_ref[axes[n]]
            refs[2 * count + n][:, pl.ds(bit, 1)] = refs[n][...][:, None]
            refs[2 * count + n][:, pl.ds(1 - bit, 1)] = refs[count + n][...][:, None]

    outs = [struct((v.shape[0], 2) + v.shape[1:], BF) for v in own]
    moved = sum(8 * v.size for v in own)
    return kernel_call(kernel, "join", [SMEM] + [VMEM] * (2 * count), outs, [], 2, cost(2, moved))(place, *own, *got)


def halve_call(place, axes, kept, got, carried):
    flat_kept = [v for share in kept for v in share]
    flat_got = [v for share in got for v in share]
    count = len(flat_kept)

    def kernel(place_ref, *refs):
        outs = refs[2 * count :]
        at = 0
        for n, share in enumerate(kept):
            bit = place_ref[axes[n]]
            begin = 0
            for v in share:
                end = begin + v.shape[-1]
                for out, half in ((outs[2 * n], 1 - bit), (outs[2 * n + 1], bit)):
                    value = refs[at][:, pl.ds(half, 1)] + refs[count + at][:, pl.ds(half, 1)].astype(F32)
                    out[:, :, begin:end] = value[:, 0].astype(out.dtype)
                at += 1
                begin = end
        if carried:
            columns = slice(flat_kept[0].shape[-1] - LANES, None)
            value = refs[0][0, 0, 0:8, columns] + unpack(refs[count][0, 0, :, columns])
            outs[0][0, :, columns] = pack(value)
            outs[1][0, 0:8, columns] = value

    outs = []
    for share in kept:
        shape = share[0].shape[:1] + share[0].shape[2:-1] + (sum(v.shape[-1] for v in share),)
        outs += [struct(shape, BF), struct(shape, F32)]
    moved = sum(10 * v.size for v in flat_kept)
    made = kernel_call(kernel, "halve", [SMEM] + [VMEM] * (2 * count), outs, [], 4, cost(3, moved))(
        place, *flat_kept, *flat_got
    )
    return [made[2 * n : 2 * n + 2] for n in range(len(kept))]


def deal_call(place, kept, got, carried):
    deep, rows = kept[0].shape[:2]
    widths = [v.shape[2] for v in kept]
    columns = sum(widths)
    widths[0] -= LANES if carried else 0

    def kernel(place_ref, *refs):
        begin = 0
        for n, width in enumerate(widths):
            for k in range(deep):
                at = place_ref[1] ^ k
                value = refs[n][at, :, 0:width] + refs[2 + n][at, :, 0:width].astype(F32)
                refs[4 + k][:, begin : begin + width] = value.astype(refs[4 + k].dtype)
            begin += width
        if carried:
            last = slice(widths[0], widths[0] + LANES)
            value = refs[0][0, 0:8, last] + unpack(refs[2][0, :, last])
            refs[4][:, begin:] = jnp.concatenate([value, jnp.zeros((rows - 8, LANES), F32)], axis=0)
            for k in range(1, deep):
                refs[4 + k][:, begin:] = pack(value)

    outs = [struct((rows, columns), F32 if k == 0 else BF) for k in range(deep)]
    return kernel_call(kernel, "deal_z", [SMEM] + [VMEM] * 4, outs, [], 4, cost(2, 10 * deep * rows * columns))(
        place, *kept, *got
    )


def finish_call(place, own, got, cuts, gains, carried):
    deep = len(got) + 1
    rows, columns = own.shape
    bounds = [0, *cuts, columns - (LANES if carried else 0)]
    pairs = list(zip(bounds[:-1], bounds[1:]))
    flat = [v for gain, weights in gains for v in (gain, *weights.values())]

    def kernel(place_ref, *refs):
        given = list(refs[deep : deep + len(flat)])
        outs = refs[deep + len(flat) :]
        for n, (a, b) in enumerate(pairs):
            value = refs[0][:, a:b]
            for k in range(1, deep):
                value = value + refs[k][:, a:b].astype(F32)
            outs[n][...] = value
        at = len(pairs)
        for gain, weights in gains:
            gain_ref = given.pop(0)
            total = jnp.zeros((rows, 1), F32)
            for n in weights:
                total = total + jnp.sum(given.pop(0)[...].astype(F32) * outs[n][...], axis=1, keepdims=True)
            shape = (rows, LANES)
            diagonal = lax.broadcasted_iota(jnp.int32, shape, 0) == lax.broadcasted_iota(jnp.int32, shape, 1)
            row = jnp.sum(jnp.where(diagonal, total, 0.0), axis=0, keepdims=True)
            outs[at][...] = (row[:, 0:rows] / gain_ref[...].astype(F32))[0]
            at += 1
        if carried:
            held = outs[-1]
            held[place_ref[1]] = refs[0][0:8, columns - LANES :]
            for k in range(1, deep):
                held[place_ref[1] ^ k] = unpack(refs[k][:, columns - LANES :])
            value = held[0]
            for k in range(1, deep):
                value = value + held[k]
            for n in range(2):
                strip = [value[3 * n + i : 3 * n + i + 1, :] for i in range(3)]
                outs[at + n][...] = jnp.concatenate(strip, axis=1)[0]

    outs = [struct((rows, b - a), F32) for a, b in pairs] + [struct((rows,), F32)] * len(gains)
    outs += [struct((3 * LANES,), F32)] * (2 * carried)
    scratch = [pltpu.VMEM((deep, 8, LANES), F32)] * carried
    return kernel_call(
        kernel, "finish", [SMEM] + [VMEM] * (deep + len(flat)), outs, scratch, 2, cost(2, 12 * rows * columns)
    )(place, own, *got, *flat)


class Exchange:
    def __init__(self, mesh, fine):
        self.parts = mesh.shape["dp"]
        self.count = mesh.shape["fsdp"]
        self.deep = self.count // 4
        me = lax.axis_index("fsdp")
        self.dp = lax.axis_index("dp")
        self.z = me // 4
        self.y_bit = (me // 2) % 2 == 1
        self.x_bit = me % 2 == 1
        self.fine = fine
        self.place = jnp.stack([self.dp, self.z, (me // 2) % 2, me % 2]).astype(jnp.int32)

    def swap(self, value, mask):
        return lax.ppermute(value, "fsdp", [(i, i ^ mask) for i in range(self.count)])

    def swap_dp(self, value, mask):
        return lax.ppermute(value, "dp", [(i, i ^ mask) for i in range(self.parts)])

    def send_z(self, shard, k):
        return self.swap(shard, 4 * k)

    def order_z(self, held, cut):
        if self.fine:
            return order_call(self.place, held, cut)
        step = 1
        while step < self.deep:
            bit = (self.z // step) % 2 == 1
            held = [jnp.where(bit, held[k ^ step], held[k]) for k in range(self.deep)]
            step *= 2
        stack = jnp.stack(held)
        return [stack[:, :, :cut], stack[:, :, cut:]]

    def send_first(self, shares):
        return [self.swap(shares[0], 1), self.swap(shares[1], 2)]

    def join_first(self, shares, got):
        if self.fine:
            return join_call(self.place, (3, 2), shares, got)
        out = []
        for own, other, bit in zip(shares, got, (self.x_bit, self.y_bit)):
            out.append(jnp.stack([jnp.where(bit, other, own), jnp.where(bit, own, other)], axis=1))
        return out

    def send_second(self, shares):
        return [self.swap(shares[0], 2), self.swap(shares[1], 1)]

    def join_second(self, shares, got):
        if self.fine:
            flat = [v.reshape((-1,) + v.shape[2:]) for v in (shares[1], got[1])]
            made = join_call(self.place, (2, 3), [shares[0], flat[0]], [got[0], flat[1]])
            return [v.reshape(-1, v.shape[-1]) for v in made]
        out = []
        for own, other, bit, place in zip(shares, got, (self.y_bit, self.x_bit), (1, 2)):
            v = jnp.stack([jnp.where(bit, other, own), jnp.where(bit, own, other)], axis=place)
            out.append(v.reshape(-1, v.shape[-1]))
        return out

    def gather_dp(self, shares):
        return [[v] + [self.swap_dp(v, k) for k in range(1, self.parts)] for v in shares]

    def cut_rows(self, own, swapped, outer, bit, rows):
        columns = []
        for n, value in enumerate(own):
            value = value.astype(F32)
            for arrays in swapped:
                value = value + arrays[n].astype(F32)
            value = value.reshape(self.count, -1, rows, value.shape[1])
            columns += [value[:, i] for i in range(value.shape[1])]
        total = jnp.concatenate(columns, axis=-1)
        total = total.reshape(outer, 2, -1, total.shape[-1])
        low, high = total[:, 0], total[:, 1]
        return jnp.where(bit, low, high).astype(BF), jnp.where(bit, high, low)

    def halves(self, total, bit):
        low, high = total[:, 0], total[:, 1]
        return jnp.where(bit, low, high).astype(BF), jnp.where(bit, high, low)

    def halve(self, kept, got, carried=False):
        kept = [[v.reshape(self.deep, 2, -1, v.shape[-1]) for v in share] for share in kept]
        got = [[g.reshape(k.shape) for g, k in zip(*pair)] for pair in zip(got, kept)]
        if self.fine:
            return halve_call(self.place, (2, 3), kept, got, carried)
        totals = [
            jnp.concatenate([k + g.astype(F32) for k, g in zip(*pair)], axis=-1) for pair in zip(kept, got)
        ]
        return [self.halves(total, bit) for total, bit in zip(totals, (self.y_bit, self.x_bit))]

    def send_halves(self, cuts):
        return [c[1] for c in cuts], [self.swap(cuts[0][0], 2), self.swap(cuts[1][0], 1)]

    def deal_z(self, kept, got, carried=False):
        if self.fine:
            own, *others = deal_call(self.place, kept, got, carried)
            return own, others
        total = jnp.concatenate([k + g.astype(F32) for k, g in zip(kept, got)], axis=-1)
        own, *others = [lax.dynamic_index_in_dim(total, self.z ^ k, 0, keepdims=False) for k in range(self.deep)]
        return own, [v.astype(BF) for v in others]

    def send_parts(self, others):
        return [self.swap(v, 4 * k) for k, v in enumerate(others, 1)]

    def finish_z(self, own, got, cuts, gains, carried=False):
        if self.fine:
            return finish_call(self.place, own, got, cuts, gains, carried)
        for v in got:
            own = own + v.astype(F32)
        made = jnp.split(own, cuts, axis=1)
        for gain, weights in gains:
            total = sum(jnp.sum(w.astype(F32) * made[n], axis=1) for n, w in weights.items())
            made.append(total / gain[0].astype(F32))
        return made

    def total(self, value):
        for k in range(self.parts.bit_length() - 1):
            value = value + self.swap_dp(value, 1 << k)
        for k in range(self.count.bit_length() - 1):
            value = value + self.swap(value, 1 << k)
        return value


def after(value, *others):
    return lax.optimization_barrier((value, *others))[0]


def to_chains(value, lengths=None):
    rows, columns = value.shape
    length = rows // CHAINS
    parts = range(columns // LANES)
    masked = 0 if lengths is None else 1

    def kernel(*refs):
        source = refs[masked]
        low, (out, natural, kept, sems) = refs[masked + 1 : 2 * masked + 1], refs[2 * masked + 1 :]
        arriving = [
            pltpu.make_async_copy(source.at[:, pl.ds(n * LANES, LANES)], natural.at[n], sems.at[0, n]) for n in parts
        ]
        leaving = [
            pltpu.make_async_copy(kept.at[n], out.at[:, pl.ds(n * LANES, LANES)], sems.at[1, n]) for n in parts
        ]
        for c in arriving:
            c.start()
        if masked:
            valid = (slot_times(0, rows, rows) < refs[0][0, 0] + refs[0][0, 1]).astype(F32)
        for n in parts:
            arriving[n].wait()

            def move(j, carry):
                kept[n, span(j * CHAINS, CHAINS), :] = natural[n, pl.ds(j, CHAINS, stride=length), :]
                return carry

            lax.fori_loop(0, length, move, 0, unroll=16)
            leaving[n].start()
            if masked:
                low[0][:, n * LANES : (n + 1) * LANES] = (valid * kept[n]).astype(BF)
        for c in leaving:
            c.wait()

    place = pltpu.VMEM((columns // LANES, rows, LANES), F32)
    made = kernel_call(
        kernel,
        "to_chains",
        [SMEM] * masked + [HBM],
        [struct((rows, columns), BF)] * masked + [struct((rows, columns), F32)],
        [place, place, pltpu.SemaphoreType.DMA((2, columns // LANES))],
        8,
        cost(4, 8 * rows * columns),
        distant=1,
    )(*([lengths] * masked), *far(value))
    return made if masked else made[0]


def from_chains(value):
    rows, columns = value.shape
    return value.reshape(rows // CHAINS, CHAINS, columns).transpose(1, 0, 2).reshape(rows, columns)


def turns(phase, rows):
    length = rows // CHAINS
    inside = jnp.arange(length, dtype=F32)[:, None] * phase
    outside = (jnp.arange(CHAINS, dtype=F32) * length)[:, None] * phase
    return [jnp.cos(inside), jnp.sin(inside), jnp.cos(outside), jnp.sin(outside)]


def build(mesh):
    def per_device(
        tokens,
        lengths,
        w_input,
        w_forget,
        w_gate,
        w_output,
        w_up_gate,
        w_up,
        w_down,
        norm_gain,
        group_gain,
        ffn_gain,
        lower_bound,
        phase,
        cotangent,
    ):
        ex = Exchange(mesh, w_input.shape[0] % 24 == 0)
        parts = ex.parts
        total, width = tokens.shape
        half = lower_bound.shape[0]
        ff = w_up.shape[1]
        dims = (total, width, half, width // GROUPS)
        shard = w_input.shape[0]

        columns = jnp.stack([norm_gain, group_gain, ffn_gain], axis=1)
        columns = jnp.pad(columns, ((0, 0), (0, LANES - 3)))
        pack1 = jnp.concatenate([w_input, w_gate, w_forget, columns], axis=1)
        pack1, tokens, rest = after((pack1, tokens, [w_output, w_up_gate, w_up]))
        pack2 = jnp.concatenate(rest, axis=1)
        cut1, cut2, cut3 = pack1.shape[1] // 2, pack2.shape[1] // 2, width // 2

        others = range(1, ex.deep)
        one = [pack1] + [ex.send_z(pack1, k) for k in others]
        one, pack2, ex.place, tokens = after((one, pack2, ex.place, tokens))
        tok = to_chains(tokens)
        one = ex.order_z(one, cut1)
        got = ex.send_first(one)
        two = [pack2] + [ex.send_z(pack2, k) for k in others[:2]]
        one, got, two, tok, phase, lower_bound = after((one, got, two, tok, phase, lower_bound))
        tables = turns(phase, total)
        low = jnp.broadcast_to(lower_bound, (8, half))
        one = ex.join_first(one, got)
        got = ex.send_second(one)
        two += [ex.send_z(two[0], k) for k in others[2:]]
        one, got, two, tables, low = after((one, got, two, tables, low))
        one = ex.gather_dp(ex.join_second(one, got))
        two = ex.order_z(two, cut2)
        got = ex.send_first(two)
        (tok,) = far(tok)
        inner, gate, forget, gains, normed, inner_low, gate_low, w_one = recurrent_project(parts, cut1, dims)(
            ex.place, tok, *one[0], *one[1]
        )
        two, got, gains, w_down, cotangent = after((two, got, gains, w_down, cotangent))
        grad, cot = to_chains(cotangent, lengths)
        two = ex.join_first(two, got)
        got = ex.send_second(two)
        three = [w_down] + [ex.send_z(w_down, k) for k in others]
        gated, state = recurrent_mix(dims)(lengths, inner, gate, forget, gains, low, *tables)
        three, gated = after((three, gated))
        three = ex.order_z(three, cut3)
        late = ex.send_first(three)
        two, got, three, late, gated, cot, grad = after((two, got, three, late, gated, cot, grad))
        two = ex.gather_dp(ex.join_second(two, got))
        three = ex.join_first(three, late)
        late = ex.send_second(three)
        (cot,) = far(cot)
        middle, ffn_in, to_left, to_right, hidden, w_two = ffn_up(parts, cut2, dims, ff)(
            ex.place, gated, gains, tok, *two[0], *two[1]
        )
        turn = (ex.place, lengths)
        three, late, ffn_in = after((three, late, ffn_in))
        three, turn = after((ex.join_second(three, late), turn))
        three = ex.gather_dp(three)
        fold_rows = ff // width

        def last_grads(name, n, turn, lefts, rights, products, swapped, sums=None):
            outer, bit = ((2 * ex.deep, ex.x_bit), (ex.deep, ex.y_bit))[n]
            if ex.fine:
                return split_grads(
                    name, turn[0], 3 - n, lefts, rights, products, swapped, parts, outer, shard, sums
                )
            made = weight_grads(name, turn[0], lefts, rights, products, 0, parts)
            return ex.cut_rows(made, swapped, outer, bit, shard)

        def grads_of(name, turn, lefts, rights, products):
            swapped = []
            for k in range(1, parts):
                made = weight_grads(name, turn[0], lefts, rights, products, k, parts)
                made, turn = after((made, turn))
                swapped.append([ex.swap_dp(v, k) for v in made])
            return swapped, turn

        halves = [(0, 0, 0, cut3), (0, 0, cut3, width)]
        swapped_down, turn = grads_of("down_grads", turn, [hidden], [grad], halves)
        d_left, d_right, w_three, hidden_far, middle_far = ffn_turn(parts, cut3, dims, ff)(
            turn[0], grad, to_left, to_right, hidden, middle, *three[0], *three[1]
        )
        d_left, swapped_down, turn = after((d_left, swapped_down, turn))
        swapped = []
        for n, right in enumerate((d_left, d_right)):
            made, turn = grads_of("up_grads", turn, [ffn_in], [right], [(0, 0, 0, ff)])
            swapped.append([up + down[n : n + 1] for up, down in zip(made, swapped_down)])
        kept, got = [], []
        for n, right in enumerate((d_left, d_right)):
            products = [(0, 0, 0, ff), (1, 1) + halves[n][2:]]
            send, keep = last_grads("ffn_grads", n, turn, [ffn_in, hidden], [right, grad], products, swapped[n])
            send, keep, turn = after((send, keep, turn))
            kept.append([keep])
            got.append([ex.swap(send, n + 1)])
        d_mid, d_middle, d_gate, local, prod = middle_back(dims, ff)(
            turn[1], d_left, d_right, middle, gains, low, state, gate_low, forget, w_two, *tables, cot
        )
        wide = 2 * width + half
        shares = [[(0, 0, 0, width), (0, 0, 2 * width, wide)], [(0, 0, 0, width), (1, 1, 0, width)]]
        local, turn = after((local, turn))
        swapped_b, turn = grads_of("recurrent_grads", turn, [normed, gated], [d_gate, d_mid], shares[1])
        kept, got, turn = after((kept, got, turn))
        cuts, turn = after((ex.halve(kept, got), turn))
        kept, got = ex.send_halves(cuts)
        d_proj, sums, made = source_back(dims, parts, ex.place, [normed], d_mid, shares[:1], ex.fine)(
            turn[1], turn[0], local, prod, d_gate, low, state, forget, inner_low, *tables
        )
        sums, turn = after((sums, turn))
        send_b, kept_b = last_grads(
            "recurrent_grads", 1, turn, [normed, gated], [d_gate, d_mid], shares[1], swapped_b
        )
        made, kept, got, sums, send_b, kept_b, turn = after((made, kept, got, sums, send_b, kept_b, turn))
        swapped_a = []
        for k, (v,) in enumerate(made, 1):
            v = ex.swap_dp(v, k)
            swapped_a.append([v] if ex.fine else [v[:, :width], v[:, width:]])
        ffn, others = ex.deal_z(kept, got)
        ffn, others, send_b, turn = after((ffn, others, send_b, turn))
        ffn_got = ex.send_parts(others)
        got_b = ex.swap(send_b, 2)
        send_a, kept_a = last_grads(
            "recurrent_grads", 0, turn, [normed], [d_proj], shares[0], swapped_a, sums if ex.fine else None
        )
        send_a, kept_a, turn = after((send_a, kept_a, turn))
        got_a = ex.swap(send_a, 1)
        kept, got = [[kept_a], [kept_b]], [[got_a], [got_b]]
        (input_grad,) = input_back(dims)(turn[0], d_proj, gains, d_middle, tok, *far(w_one))
        input_grad, turn = after((input_grad, turn))
        (act,) = ffn_out(dims, ff)(turn[1], *far(hidden_far, middle_far), w_three)
        input_grad, ffn_got, kept, got, act = after((input_grad, ffn_got, kept, got, act))
        cuts, act = after((ex.halve(kept, got, ex.fine), act))
        kept, got = ex.send_halves(cuts)
        act = from_chains(act)
        middle_at = ff + fold_rows * cut3
        bounds = [ff, middle_at, middle_at + ff]
        grad_up_gate, down_a, grad_up, down_b, grad_ffn_gain = ex.finish_z(
            ffn, ffn_got, bounds, [(ffn_gain[None], {0: w_up_gate, 2: w_up})]
        )
        kept, got, input_grad, act = after((kept, got, input_grad, act))
        rest, others = ex.deal_z(kept, got, ex.fine)
        rest, others, input_grad = after((rest, others, input_grad))
        got = ex.send_parts(others)
        input_grad = from_chains(input_grad)
        if not ex.fine:
            sums = ex.total(sums)
        norm_weights = {0: w_input, 1: w_forget, 2: w_gate}
        made = ex.finish_z(
            rest,
            got,
            [width, width + half, wide],
            [(norm_gain[None], norm_weights), (group_gain[None], {3: w_output})],
            ex.fine,
        )
        grad_input, grad_forget, grad_gate, grad_output, grad_norm_gain, grad_group_gain = made[:6]
        if ex.fine:
            grad_lower, grad_phase = made[6:]
        else:
            ahead = half // LANES
            grad_lower, grad_phase = sums[0:ahead].reshape(half), sums[ahead : 2 * ahead].reshape(half)

        halves = []
        for i in range(fold_rows):
            left_half = down_a[:, i * cut3 : (i + 1) * cut3]
            right_half = down_b[:, i * (width - cut3) : (i + 1) * (width - cut3)]
            halves.append(jnp.concatenate([left_half, right_half], axis=1))
        grad_down = jnp.concatenate(halves, axis=0)
        return (
            act,
            input_grad,
            grad_input,
            grad_forget,
            grad_gate,
            grad_output,
            grad_up_gate,
            grad_up,
            grad_down,
            grad_norm_gain,
            grad_group_gain,
            grad_ffn_gain,
            grad_lower,
            grad_phase,
        )

    return per_device


def solution(mesh):
    rows = P(("dp", "fsdp"), None)
    vec = P(("dp", "fsdp"))
    in_specs = (rows,) * 9 + (vec,) * 3 + (P(), P(), rows)
    out_specs = (rows,) * 9 + (vec,) * 3 + (P(), P())
    return jax.shard_map(build(mesh), mesh=mesh, in_specs=in_specs, out_specs=out_specs, check_vma=False)
```
